256 devices in a mesh: inst: 32 (over z, x), tp: 8 (over y, core).
Axes of the slice: x: 4, y: 4, z: 8, core: 2. Of those that a mesh axis runs over, the one named last changes fastest.
Arguments:
- queries: bfloat16 [256, 2, 64, 128], P('inst', None, 'tp'), may hold values from -100 to 100
- new_keys: bfloat16 [256, 2, 8, 128], P('inst', None, 'tp'), may hold values from -8 to 8
- new_values: bfloat16 [256, 2, 8, 128], P('inst', None, 'tp'), may hold values from -6 to 6
- key_pool: bfloat16 [2048, 8, 128, 128], P('inst', 'tp'), may hold values from -8 to 8
- value_pool: bfloat16 [2048, 8, 128, 128], P('inst', 'tp'), may hold values from -6 to 6
- block_table: int32 [256, 8], P('inst'), may hold values from 0 to 63
- lengths: int32 [256], P('inst'), may hold values from 1 to 1024, 131072 in all
- lend_entry: int32 [1024], P('inst'), may hold values from 0 to 63, as said below
- lend_target: int32 [1024, 1], P('inst'), may hold values from 0 to 31; in each aligned block of 32 rows (0 to 31, 32 to 63, ...) at most 2 rows name the same one
- out_weight: bfloat16 [8192, 4096], P('tp'), may hold values from -0.0625 to 0.0625
Outputs:
- projected: bfloat16 [256, 2, 4096], P('inst', None, 'tp')
The draws below stay inside these ranges and needn't reach their ends.
Inputs may be any that keep to these rules, and one draw needn't show every extreme that they name: `lend_entry`: each of an instance's 32 entries is distinct. `lend_target`: among the 32 rows of one instance no creditor is named more than 2 times, and some instance names one creditor exactly 2 times; a creditor may be the instance itself. `block_table`: slots may be shared by several entries. The lengths sum to 131072 and the largest is exactly 1024.
All inputs are finite; a program needn't handle non-finite values. No bound on the sum of `lengths` on one device may be relied on, other than what follows from the above.
Results may differ from the reference program's by a relative error of at most 0.019.
Values may be sent and summed in bfloat16 or wider, within the bound.
No kernel may reach another device: no remote copies, remote signals or barrier semaphores. Data moves between devices by JAX's collectives and lax.ppermute only.
A program may use at most 64 MiB of HBM per device.

```python
import math
import jax
import jax.numpy as jnp
import numpy as np
from jax import lax

QH = 64
KVH = 8
HD = 128
DW = 4096
BLK = 128
MAXB = 8
STEPS = 2
REQ_DEV = 8
POOL = 64
LEND_DEV = 32
CAP = 2
REQUESTS = 256
LENDS = 1024
N_INST = 32


def shared_keys(key):
    base_key = jax.random.fold_in(key, 501)
    normal_draw = jax.random.normal(base_key, (REQUESTS, STEPS, KVH, HD), jnp.float32)
    return 1.4 * jnp.clip(normal_draw, -4.0, 4.0)


def draw_new_keys(key, part):
    fresh = shared_keys(key)
    return fresh.astype(jnp.bfloat16)


def draw_queries(key, part):
    key = jax.random.fold_in(key, 9)
    result = 1.4 * jax.random.normal(key, (REQUESTS, STEPS, QH, HD), jnp.float32)
    return result.astype(jnp.bfloat16)


def draw_lend_entry(key, part):
    key = jax.random.fold_in(key, 3)
    instance_keys = jax.random.split(key, LENDS // LEND_DEV)
    picks = jax.vmap(lambda single: jax.random.permutation(single, REQ_DEV * MAXB)[:LEND_DEV])(instance_keys)
    return picks.reshape(LENDS).astype(jnp.int32)


def set_ends(entries, stream_key, low, top_value):
    index_at = [jax.random.randint(jax.random.fold_in(stream_key, axis), (), 0, length) for axis, length in enumerate(entries.shape)]
    longest = entries.shape.index(max(entries.shape))
    next_to = index_at[:longest] + [(index_at[longest] + 1) % entries.shape[longest]] + index_at[longest + 1:]
    return entries.at[tuple(index_at)].set(low).at[tuple(next_to)].set(top_value)


def level_of(key, shape, cuts, smallest, largest):
    def one(position, blocks):
        steps = jax.random.uniform(jax.random.fold_in(jax.random.fold_in(key, 6), position), (blocks,), jnp.float32, smallest / len(cuts), largest / len(cuts))
        return jnp.repeat(jnp.exp(steps), shape[position] // blocks).reshape((-1,) + (1,) * (len(shape) - position - 1))

    loudness = one(*cuts[0])
    for cut in cuts[1:]:
        loudness = loudness * one(*cut)
    return loudness


def profile(amount, total, most, slope):
    weights = [(1 << 20) // math.isqrt(grade ** slope) + 1 for grade in range(2, amount + 1)]
    rest, counts = total - most - (amount - 1), [1] * (amount - 1)
    while rest > 0:
        candidates = [i for i in range(amount - 1) if counts[i] < most]
        whole, left = sum([weights[i] for i in candidates]), rest
        for i in candidates:
            more = min(most - counts[i], max(1, left * weights[i] // whole), rest)
            counts[i] = counts[i] + more
            rest = rest - more
    return np.array([most] + counts)


def ragged_sizes(own_key, number_of, total, most, slope):
    if number_of == 2:
        one = jax.random.randint(own_key, (), max(1, total - most), min(most, total - 1) + 1)
        return jnp.stack([one, total - one])
    tallies = jnp.asarray(profile(number_of, total, most, slope), jnp.int32)
    twos = (number_of - 1) // 2
    giver, receiver = tallies[1:1 + 2 * twos:2], tallies[2:2 + 2 * twos:2]
    margin = jnp.minimum(giver - 1, most - receiver)
    moved = jax.random.randint(jax.random.fold_in(own_key, 1), (twos,), 0, 1 << 20) % (margin + 1)
    tallies = tallies.at[1:1 + 2 * twos:2].set(giver - moved).at[2:2 + 2 * twos:2].set(receiver + moved)
    return tallies[jax.random.permutation(jax.random.fold_in(own_key, 2), number_of)]


def routed_block(key, own, number, rows, count, top, bound, skew):
    sequence = jax.random.permutation(key, count)
    crowded, ordinary = shares(count, rows * top, bound, skew, True), shares(count, rows * top, bound, skew, False)
    places = jnp.arange(count)

    def named(sizes, offset_by):
        used = int((sizes > 0).sum())
        fixed = max(1, used // 4)
        shifted = fixed + (places - fixed + offset_by * (used - fixed)) % max(1, count - fixed)
        return jnp.zeros((count,), jnp.int32).at[sequence[jnp.where(places < fixed, places, shifted)]].set(jnp.asarray(sizes, jnp.int32))

    sizes = jnp.where(number % 4 == 0, named(crowded, number // 4), named(ordinary, number - number // 4 - 1))
    mixed = jax.random.permutation(jax.random.fold_in(own, 3), count)
    giver, sink = mixed[0:count // 2 * 2:2], mixed[1:count // 2 * 2:2]
    slack = jnp.minimum(sizes[giver] - 1, bound - sizes[sink]) // 2
    slack = jnp.where((giver == sequence[0]) | (sink == sequence[0]) | (sizes[sink] == 0), 0, jnp.maximum(slack, 0))
    shifted = jax.random.randint(jax.random.fold_in(own, 4), (count // 2,), 0, 1 << 20) % (slack + 1)
    sizes = sizes.at[giver].add(-shifted).at[sink].add(shifted)
    items = jnp.searchsorted(jnp.cumsum(sizes), jnp.arange(rows * top), side="right").astype(jnp.int32)
    grid = items.reshape(top, rows).T
    grid = grid[jax.random.permutation(jax.random.fold_in(own, 1), rows)]
    offset_by = jax.random.randint(jax.random.fold_in(own, 2), (rows, 1), 0, top)
    return jnp.take_along_axis(grid, (jnp.arange(top)[None, :] + offset_by) % top, axis=1)


def shares(count, total, most, lean, full):
    loads = [(1 << 20) // math.isqrt(standing ** lean) + 1 for standing in range(1, count + 1)]
    largest = most if full else min(most, max(-(-total // count), total * loads[0] // sum(loads)))
    least = 1 if total - largest >= count - 1 else 0
    given, surplus = [largest] + [least] * (count - 1), total - largest - least * (count - 1)
    while surplus > 0:
        free = [i for i in range(1, count) if given[i] < largest] or [i for i in range(1, count) if given[i] < most]
        pool, remaining = sum([loads[i] for i in free]), surplus
        for i in free:
            more = min(most - given[i], max(1, remaining * loads[i] // pool), surplus)
            given[i] = given[i] + more
            surplus = surplus - more
    return np.array(given)


def normal_values(stream_key, shape, spread, limit, shards=(), kind=jnp.bfloat16):
    values = jax.random.normal(stream_key, shape, jnp.float32) * spread
    if len(shards) > 0:
        values = level_of(stream_key, shape, shards, -0.22, 0.18) * values
    return jnp.clip(values, min=-limit, max=limit).astype(kind)


def setup_inputs(seed: int = 0) -> dict:
    seeds = jax.random.split(jax.random.key(seed), 11)
    queries = draw_queries(jax.random.fold_in(seeds[10], 71), 0)
    new_keys = draw_new_keys(jax.random.fold_in(seeds[10], 71), 0)
    new_values = normal_values(seeds[2], (REQUESTS, STEPS, KVH, HD), 1.0, 6.0, ((0, 32), (2, 8)))
    key_pool = normal_values(seeds[3], (N_INST * POOL, KVH, BLK, HD), 1.4, 8.0, ((0, 32), (1, 8)))
    value_pool = normal_values(seeds[4], (N_INST * POOL, KVH, BLK, HD), 1.0, 6.0, ((0, 32), (1, 8)))
    block_table = set_ends(jax.random.randint(seeds[5], (REQUESTS, MAXB), 0, POOL), jax.random.fold_in(seeds[5], 1), 0, POOL - 1).astype(jnp.int32)
    lengths = ragged_sizes(seeds[6], REQUESTS, REQUESTS * MAXB * BLK // 2, MAXB * BLK, 2).astype(jnp.int32)
    lend_entry = draw_lend_entry(jax.random.fold_in(seeds[10], 71), 0)
    lend_target_keys = jax.random.split(jax.random.fold_in(seeds[8], 1), LENDS // LEND_DEV)
    lend_target_turns = jax.random.permutation(jax.random.fold_in(seeds[8], 3), LENDS // LEND_DEV)
    lend_target = jax.vmap(lambda own, number: routed_block(jax.random.fold_in(seeds[8], 2), own, number, LEND_DEV, N_INST, 1, CAP, 2))(lend_target_keys, lend_target_turns).reshape((LENDS, 1))
    out_weight = normal_values(seeds[9], (QH * HD, DW), (QH * HD) ** -0.5, 0.0625, ((0, 8),))
    return {"queries": queries, "new_keys": new_keys, "new_values": new_values, "key_pool": key_pool, "value_pool": value_pool, "block_table": block_table, "lengths": lengths, "lend_entry": lend_entry, "lend_target": lend_target, "out_weight": out_weight}


MASKED_SCORE = -1e30


def reference(queries, new_keys, new_values, key_pool, value_pool, block_table, lengths, lend_entry, lend_target, out_weight):
    entry_owner = (jnp.arange(REQUESTS * MAXB, dtype=jnp.int32) // (REQ_DEV * MAXB)).astype(jnp.int32)
    lent_global = ((jnp.arange(LENDS, dtype=jnp.int32) // LEND_DEV) * (REQ_DEV * MAXB) + lend_entry).astype(jnp.int32)
    entry_owner = entry_owner.at[lent_global].set(lend_target[:, 0]).reshape(REQUESTS, MAXB)
    pool_index = (entry_owner * POOL + block_table).astype(jnp.int32)
    group_size = QH // KVH
    positions = jnp.arange(MAXB * BLK, dtype=jnp.int32)
    step_index = jnp.arange(STEPS, dtype=jnp.int32)
    fresh_live = step_index[None, :] <= step_index[:, None]
    scale_factor = HD ** -0.5

    def attend_request(packed):
        query_block, fresh_keys, fresh_values, pool_rows, context = packed
        key_rows = jnp.transpose(key_pool[pool_rows], (1, 0, 2, 3)).reshape(KVH, MAXB * BLK, HD)
        value_rows = jnp.transpose(value_pool[pool_rows], (1, 0, 2, 3)).reshape(KVH, MAXB * BLK, HD)
        key_rows = jnp.concatenate([key_rows, jnp.transpose(fresh_keys, (1, 0, 2))], axis=1).astype(jnp.float32)
        value_rows = jnp.concatenate([value_rows, jnp.transpose(fresh_values, (1, 0, 2))], axis=1).astype(jnp.float32)
        query_rows = query_block.reshape(STEPS, KVH, group_size, HD).astype(jnp.float32)
        scores = jnp.einsum("skgd,ktd->skgt", query_rows, key_rows, precision=lax.Precision.HIGHEST) * scale_factor
        cached_live = jnp.broadcast_to((positions < context)[None, :], (STEPS, MAXB * BLK))
        live_mask = jnp.concatenate([cached_live, fresh_live], axis=1)[:, None, None, :]
        masked = jnp.where(live_mask, scores, MASKED_SCORE)
        peak_score = jnp.max(masked, axis=-1, keepdims=True)
        weights = jnp.where(live_mask, jnp.exp(masked - peak_score), 0.0)
        weighted = jnp.einsum("skgt,ktd->skgd", weights, value_rows, precision=lax.Precision.HIGHEST)
        attention = weighted / jnp.sum(weights, axis=-1)[..., None]
        return attention.reshape(STEPS, QH * HD).astype(jnp.bfloat16)

    attention = lax.map(attend_request, (queries, new_keys, new_values, pool_index, lengths))
    projected = jnp.dot(attention.reshape(REQUESTS * STEPS, QH * HD), out_weight, preferred_element_type=jnp.float32)
    return projected.reshape(REQUESTS, STEPS, DW).astype(jnp.bfloat16)
```

```python
import functools

import jax
import jax.numpy as jnp
from jax import lax
from jax.experimental import pallas as pl
from jax.experimental.pallas import tpu as pltpu
from jax.sharding import PartitionSpec as P

DEAD = -1e30
CAP = 2
GROUP = 8
ROWS = 16
SLAB = 48
BF = jnp.bfloat16
F32 = jnp.float32
VM = pl.BlockSpec(memory_space=pltpu.VMEM)
SM = pl.BlockSpec(memory_space=pltpu.SMEM)


def lane_iota():
    return lax.broadcasted_iota(jnp.int32, (ROWS, 128), 1)


def pack_kernel(entry, target, table, lengths, q, send, count, slots, lives):
    peers = send.shape[0]
    blocks = table.shape[1]

    def clear(i, _):
        count[i] = 0
        for c in range(CAP):
            slots[i * CAP + c] = 0
            lives[i * CAP + c] = 0
        return 0

    lax.fori_loop(0, peers, clear, 0)

    def place(j, _):
        e = entry[j]
        t = target[j, 0]
        r = e // blocks
        b = e % blocks
        rank = count[t]
        count[t] = rank + 1
        live = jnp.clip(lengths[r] - b * 128, 0, 128)
        slots[t * CAP + rank] = table[r, b]
        lives[t * CAP + rank] = live
        send[t, pl.ds(pl.multiple_of(rank * ROWS, ROWS), ROWS), :] = q[r]
        return 0

    lax.fori_loop(0, entry.shape[0], place, 0)
    lane = lane_iota()

    def side(i, _):
        v = jnp.where(lane == 0, slots[i * CAP], 0)
        v = jnp.where(lane == 1, lives[i * CAP], v)
        v = jnp.where(lane == 2, slots[i * CAP + 1], v)
        v = jnp.where(lane == 3, lives[i * CAP + 1], v)
        send[i, CAP * ROWS :, :] = v.astype(F32).astype(BF)
        return 0

    lax.fori_loop(0, peers, side, 0)


def block_partial(q, k, v, live, scale):
    s = lax.dot_general(q, k, (((1,), (1,)), ((), ())), preferred_element_type=F32) * scale
    s = jnp.where(lane_iota() < live, s, DEAD)
    m = jnp.max(s, axis=1, keepdims=True)
    p = jnp.exp(s - m)
    l = jnp.sum(p, axis=1, keepdims=True)
    o = jnp.dot(p.astype(BF), v, preferred_element_type=F32) / l
    return o, m + jnp.log(l)


def serve_kernel(recv, kp, vp, back, side_f, side_i, side_s, ids, lse, sem):
    peers = recv.shape[0]
    scale = 128**-0.5
    side_f[...] = recv[:, CAP * ROWS :, :].astype(F32).reshape(peers * ROWS, 128)
    side_i[...] = side_f[pl.ds(0, peers, stride=ROWS), :].astype(jnp.int32)
    copy = pltpu.make_async_copy(side_i, side_s, sem)
    copy.start()
    back[...] = jnp.zeros(back.shape, BF)
    lse[...] = jnp.full(lse.shape, DEAD, F32)
    copy.wait()

    def listing(i, n):
        for c in range(CAP):
            ids[n] = i * CAP + c
            n = n + jnp.where(side_s[i, 2 * c + 1] > 0, 1, 0)
        return n

    n = lax.fori_loop(0, peers, listing, 0)
    last = jnp.maximum(n - 1, 0)

    def work(g, _):
        todo = []
        for i in range(GROUP):
            item = ids[jnp.minimum(g * GROUP + i, last)]
            peer = item // CAP
            c = item % CAP
            slot = side_s[peer, 2 * c]
            live = side_s[peer, 2 * c + 1]
            q = recv[peer, pl.ds(pl.multiple_of(c * ROWS, ROWS), ROWS), :]
            todo.append((item, peer, c, block_partial(q, kp[slot], vp[slot], live, scale)))
        for item, peer, c, (o, z) in todo:
            back[peer, pl.ds(pl.multiple_of(c * ROWS, ROWS), ROWS), :] = o.astype(BF)
            lse[item] = jnp.broadcast_to(z, (ROWS, 128))
        return 0

    lax.fori_loop(0, (n + GROUP - 1) // GROUP, work, 0)
    lane = lane_iota()

    def side(i, _):
        out = jnp.zeros((ROWS, 128), F32)
        for c in range(CAP):
            rest = lse[i * CAP + c]
            for piece in range(3):
                part = rest.astype(BF).astype(F32)
                rest = rest - part
                out = jnp.where(lane == 3 * c + piece, part, out)
        back[i, CAP * ROWS :, :] = out.astype(BF)
        return 0

    lax.fori_loop(0, peers, side, 0, unroll=4)


def home_kernel(entry, table, lengths, q, nk, nv, kp, vp, o_out, z_out, lent, ids):
    requests, blocks = table.shape
    scale = 128**-0.5
    entries = requests * blocks
    z_out[...] = jnp.full(z_out.shape, DEAD, F32)
    o_out[...] = jnp.zeros(o_out.shape, BF)

    def clear(i, _):
        lent[i] = 0
        return 0

    lax.fori_loop(0, entries, clear, 0, unroll=8)

    def mark(j, _):
        lent[entry[j]] = 1
        return 0

    lax.fori_loop(0, entry.shape[0], mark, 0, unroll=8)

    def listing(e, n):
        ids[n] = e
        alive = lengths[e // blocks] > (e % blocks) * 128
        return n + jnp.where(jnp.logical_and(alive, lent[e] == 0), 1, 0)

    n = lax.fori_loop(0, entries, listing, 0, unroll=4)
    last = jnp.maximum(n - 1, 0)

    def work(g, _):
        todo = []
        for i in range(GROUP):
            e = ids[jnp.minimum(g * GROUP + i, last)]
            r = e // blocks
            b = e % blocks
            slot = table[r, b]
            todo.append((e, block_partial(q[r], kp[slot], vp[slot], lengths[r] - b * 128, scale)))
        for e, (o, z) in todo:
            o_out[e] = o.astype(BF)
            z_out[e] = jnp.broadcast_to(z, (ROWS, 128))
        return 0

    lax.fori_loop(0, (n + GROUP - 1) // GROUP, work, 0)
    second = lax.broadcasted_iota(jnp.int32, (ROWS, 1), 0) >= ROWS // 2
    for r in range(requests):
        qr = q[r].astype(F32)
        k = nk[r].astype(F32)
        v = nv[r].astype(F32)
        s0 = jnp.sum(qr * k[0:1], axis=1, keepdims=True) * scale
        s1 = jnp.sum(qr * k[1:2], axis=1, keepdims=True) * scale
        s1 = jnp.where(second, s1, DEAD)
        m = jnp.maximum(s0, s1)
        p0 = jnp.exp(s0 - m)
        p1 = jnp.where(second, jnp.exp(s1 - m), 0.0)
        l = p0 + p1
        o = (p0 * v[0:1] + p1 * v[1:2]) / l
        o_out[entries + r] = o.astype(BF)
        z_out[entries + r] = jnp.broadcast_to(m + jnp.log(l), (ROWS, 128))


def merge_kernel(entry, target, back, o_home, z_home, w, out, o_all, z_all, att, count):
    requests = o_home.shape[0] // 9
    entries = requests * 8
    peers = back.shape[0]
    o_all[...] = o_home[...].astype(F32)
    z_all[...] = z_home[...]

    def clear(i, _):
        count[i] = 0
        return 0

    lax.fori_loop(0, peers, clear, 0, unroll=8)

    def fetch(j, _):
        e = entry[j]
        t = target[j, 0]
        rank = count[t]
        count[t] = rank + 1
        o_all[e] = back[t, pl.ds(pl.multiple_of(rank * ROWS, ROWS), ROWS), :].astype(F32)
        side = back[t, CAP * ROWS :, :].astype(F32)
        z = jnp.where(
            rank == 0,
            side[:, 0:1] + side[:, 1:2] + side[:, 2:3],
            side[:, 3:4] + side[:, 4:5] + side[:, 5:6],
        )
        z_all[e] = jnp.broadcast_to(z, (ROWS, 128))
        return 0

    lax.fori_loop(0, entry.shape[0], fetch, 0, unroll=4)
    for r in range(requests):
        z = [z_all[r * 8 + b] for b in range(8)] + [z_all[entries + r]]
        o = [o_all[r * 8 + b] for b in range(8)] + [o_all[entries + r]]
        m = functools.reduce(jnp.maximum, z)
        f = [jnp.exp(x - m) for x in z]
        top = functools.reduce(jnp.add, [a * b for a, b in zip(f, o)])
        att[r * ROWS : (r + 1) * ROWS, :] = top / functools.reduce(jnp.add, f)
    heads = ROWS // 2
    a = jnp.concatenate(
        [att[pl.ds(g, 2 * requests, stride=heads), :].astype(BF) for g in range(heads)], axis=1
    )
    width = out.shape[2]

    def project(p, _):
        cols = pl.ds(pl.multiple_of(p * width, width), width)
        out[p] = jnp.dot(a, w[:, cols], preferred_element_type=F32).astype(BF)
        return 0

    lax.fori_loop(0, out.shape[0], project, 0)


def sum_kernel(parts, out):
    total = parts[0].astype(F32)
    for i in range(1, parts.shape[0]):
        total = total + parts[i].astype(F32)
    out[...] = total.astype(BF)


def params(limit):
    return pltpu.CompilerParams(vmem_limit_bytes=limit * 1024 * 1024)


def on_device(
    queries,
    new_keys,
    new_values,
    key_pool,
    value_pool,
    block_table,
    lengths,
    lend_entry,
    lend_target,
    out_weight,
):
    requests, steps, heads, size = queries.shape
    peers = lax.axis_size("inst")
    parts = lax.axis_size("tp")
    pool = key_pool.shape[0]
    entries = requests * block_table.shape[1]
    q = queries.reshape(requests, steps * heads, size)
    nk = new_keys.reshape(requests, steps, size)
    nv = new_values.reshape(requests, steps, size)
    kp = key_pool.reshape(pool, 128, size)
    vp = value_pool.reshape(pool, 128, size)
    smem = lambda n: pltpu.SMEM((n,), jnp.int32)

    send = pl.pallas_call(
        pack_kernel,
        out_shape=jax.ShapeDtypeStruct((peers, SLAB, size), BF),
        in_specs=[SM, SM, SM, SM, VM],
        out_specs=VM,
        scratch_shapes=[smem(peers), smem(peers * CAP), smem(peers * CAP)],
        compiler_params=params(8),
    )(lend_entry, lend_target, block_table, lengths, q)

    recv = lax.all_to_all(send, "inst", split_axis=0, concat_axis=0, tiled=True)

    o_home, z_home = pl.pallas_call(
        home_kernel,
        out_shape=(
            jax.ShapeDtypeStruct((entries + requests, ROWS, size), BF),
            jax.ShapeDtypeStruct((entries + requests, ROWS, size), F32),
        ),
        in_specs=[SM, SM, SM, VM, VM, VM, VM, VM],
        out_specs=(VM, VM),
        scratch_shapes=[smem(entries), smem(entries + 1)],
        compiler_params=params(16),
    )(lend_entry, block_table, lengths, q, nk, nv, kp, vp)

    back = pl.pallas_call(
        serve_kernel,
        out_shape=jax.ShapeDtypeStruct((peers, SLAB, size), BF),
        in_specs=[VM, VM, VM],
        out_specs=VM,
        scratch_shapes=[
            pltpu.VMEM((peers * ROWS, 128), F32),
            pltpu.VMEM((peers, 128), jnp.int32),
            pltpu.SMEM((peers, 128), jnp.int32),
            smem(peers * CAP + 1),
            pltpu.VMEM((peers * CAP, ROWS, 128), F32),
            pltpu.SemaphoreType.DMA,
        ],
        compiler_params=params(16),
    )(recv, kp, vp)

    mine = lax.all_to_all(back, "inst", split_axis=0, concat_axis=0, tiled=True)

    partial = pl.pallas_call(
        merge_kernel,
        out_shape=jax.ShapeDtypeStruct((parts, requests * steps, out_weight.shape[1] // parts), BF),
        in_specs=[SM, SM, VM, VM, VM, VM],
        out_specs=VM,
        scratch_shapes=[
            pltpu.VMEM((entries + requests, ROWS, size), F32),
            pltpu.VMEM((entries + requests, ROWS, size), F32),
            pltpu.VMEM((requests * ROWS, size), F32),
            smem(peers),
        ],
        compiler_params=params(24),
    )(lend_entry, lend_target, mine, o_home, z_home, out_weight)

    shares = lax.all_to_all(partial, "tp", split_axis=0, concat_axis=0, tiled=True)

    total = pl.pallas_call(
        sum_kernel,
        out_shape=jax.ShapeDtypeStruct(shares.shape[1:], BF),
        in_specs=[VM],
        out_specs=VM,
    )(shares)
    return total.reshape(requests, steps, total.shape[1])


def solution(mesh):
    placed = (
        P("inst", None, "tp", None),
        P("inst", None, "tp", None),
        P("inst", None, "tp", None),
        P("inst", "tp", None, None),
        P("inst", "tp", None, None),
        P("inst", None),
        P("inst"),
        P("inst"),
        P("inst", None),
        P("tp", None),
    )
    return jax.shard_map(
        on_device, mesh=mesh, in_specs=placed, out_specs=P("inst", None, "tp"), check_vma=False
    )
```

```python
import functools

import jax
import jax.numpy as jnp
from jax import lax
from jax.experimental import pallas as pl
from jax.experimental.pallas import tpu as pltpu
from jax.sharding import PartitionSpec as P

DEAD = -1e30
CAP = 2
GROUP = 8
ROWS = 16
HALF = 8
SLAB = 40
BF = jnp.bfloat16
F32 = jnp.float32
VM = pl.BlockSpec(memory_space=pltpu.VMEM)
HB = pl.BlockSpec(memory_space=pl.ANY)


def lane_iota(rows=ROWS):
    return lax.broadcasted_iota(jnp.int32, (rows, 128), 1)


def fetch_all(pairs, sems):
    copies = [pltpu.make_async_copy(a, b, sems.at[i]) for i, (a, b) in enumerate(pairs)]
    for c in copies:
        c.start()
    return copies


def pack_kernel(
    entry_h, target_h, table_h, lengths_h, q_h, kp_h, vp_h,
    send, kp, vp,
    entry, target, table, lengths, q, tiles, count, slots, lives, sems,
):
    peers = send.shape[0]
    blocks = table.shape[1]
    small = fetch_all(
        [(entry_h, entry), (target_h, target), (table_h, table), (lengths_h, lengths), (q_h, q), (kp_h, kp), (vp_h, vp)],
        sems,
    )

    def clear(i, _):
        count[i] = 0
        for c in range(CAP):
            slots[i * CAP + c] = 0
            lives[i * CAP + c] = 0
        return 0

    lax.fori_loop(0, peers, clear, 0, unroll=4)
    for c in small[:5]:
        c.wait()

    def place(j, _):
        e = entry[j]
        t = target[j]
        r = e // blocks
        b = e % blocks
        rank = count[t]
        count[t] = rank + 1
        i = t * CAP + rank
        slots[i] = table[r, b]
        lives[i] = jnp.clip(lengths[r] - b * 128, 0, 128)
        tiles[i] = q[r]
        return 0

    lax.fori_loop(0, entry.shape[0], place, 0, unroll=4)
    lane = lane_iota(HALF)

    def lay(i, _):
        v = jnp.where(lane == 0, slots[i * CAP], 0)
        v = jnp.where(lane == 1, lives[i * CAP], v)
        v = jnp.where(lane == 2, slots[i * CAP + 1], v)
        v = jnp.where(lane == 3, lives[i * CAP + 1], v)
        send[i] = jnp.concatenate(
            [tiles[i * CAP], tiles[i * CAP + 1], v.astype(F32).astype(BF)], axis=0
        )
        return 0

    lax.fori_loop(0, peers, lay, 0, unroll=4)
    for c in small[5:]:
        c.wait()


def attend(n, query, slot_of, live_of, store, kp, vp, scores):
    scale = 128**-0.5
    groups = (n + GROUP - 1) // GROUP
    lane = lane_iota()

    def score(g):
        out = []
        for i in range(GROUP):
            item = jnp.minimum(g * GROUP + i, n - 1)
            out.append(
                lax.dot_general(
                    query(item),
                    kp[slot_of(item)],
                    (((1,), (1,)), ((), ())),
                    preferred_element_type=F32,
                )
            )
        return out

    @pl.when(n > 0)
    def _():
        for i, s in enumerate(score(0)):
            scores[0, i] = s

    def work(g, _):
        now = lax.rem(g, 2)
        held = [scores[now, i] for i in range(GROUP)]
        later = score(jnp.minimum(g + 1, groups - 1))
        done = []
        for i in range(GROUP):
            item = jnp.minimum(g * GROUP + i, n - 1)
            s = jnp.where(lane < live_of(item), held[i] * scale, DEAD)
            m = jnp.max(s, axis=1, keepdims=True)
            p = jnp.exp(s - m)
            l = jnp.sum(p, axis=1, keepdims=True)
            o = jnp.dot(p.astype(BF), vp[slot_of(item)], preferred_element_type=F32) / l
            done.append((item, o, jnp.broadcast_to(m + jnp.log(l), (ROWS, 128))))
        for item, o, z in done:
            store(item, o, z)
        for i, s in enumerate(later):
            scores[1 - now, i] = s
        return 0

    lax.fori_loop(0, groups, work, 0)


def serve_kernel(recv, kp, vp, back, side_f, side_i, side_s, ids, att, lse, scores, sem):
    peers = recv.shape[0]
    side = recv[...][:, CAP * ROWS :, :].astype(F32)
    side_f[...] = side.reshape(peers * HALF, 128)
    side_i[...] = side_f[pl.ds(0, peers, stride=HALF), :].astype(jnp.int32)
    copy = pltpu.make_async_copy(side_i, side_s, sem)
    copy.start()
    att[...] = jnp.zeros(att.shape, F32)
    lse[...] = jnp.full(lse.shape, DEAD, F32)
    copy.wait()

    def listing(i, n):
        for c in range(CAP):
            ids[n] = i * CAP + c
            n = n + jnp.where(side_s[i, 2 * c + 1] > 0, 1, 0)
        return n

    n = lax.fori_loop(0, peers, listing, 0, unroll=4)

    def query(item):
        i = ids[item]
        return recv[i // CAP, pl.ds(pl.multiple_of((i % CAP) * ROWS, ROWS), ROWS), :]

    def slot_of(item):
        i = ids[item]
        return side_s[i // CAP, 2 * (i % CAP)]

    def live_of(item):
        i = ids[item]
        return side_s[i // CAP, 2 * (i % CAP) + 1]

    def store(item, o, z):
        att[ids[item]] = o
        lse[ids[item]] = z

    attend(n, query, slot_of, live_of, store, kp, vp, scores)
    lane = lane_iota(HALF)

    def lay(i, _):
        side = jnp.zeros((HALF, 128), F32)
        for c in range(CAP):
            for h in range(2):
                rest = lse[i * CAP + c, h * HALF : (h + 1) * HALF, :]
                for piece in range(3):
                    part = rest.astype(BF).astype(F32)
                    rest = rest - part
                    side = jnp.where(lane == (h * CAP + c) * 4 + piece, part, side)
        rows = jnp.concatenate([att[i * CAP], att[i * CAP + 1], side], axis=0)
        back[i] = rows.astype(BF)
        return 0

    lax.fori_loop(0, peers, lay, 0, unroll=4)


def home_kernel(
    entry_h, table_h, lengths_h, w_h, q, nk, nv, kp, vp,
    o_out, z_out, w,
    entry, table, lengths, lent, ids, scores, sems,
):
    requests, blocks = table.shape
    entries = requests * blocks
    copies = fetch_all(
        [(entry_h, entry), (table_h, table), (lengths_h, lengths), (w_h, w)], sems
    )
    z_out[...] = jnp.full(z_out.shape, DEAD, F32)
    o_out[...] = jnp.zeros(o_out.shape, F32)

    def clear(i, _):
        lent[i] = 0
        return 0

    lax.fori_loop(0, entries, clear, 0, unroll=8)
    for c in copies[:3]:
        c.wait()

    def mark(j, _):
        lent[entry[j]] = 1
        return 0

    lax.fori_loop(0, entry.shape[0], mark, 0, unroll=8)

    def listing(e, n):
        ids[n] = e
        alive = lengths[e // blocks] > (e % blocks) * 128
        return n + jnp.where(jnp.logical_and(alive, lent[e] == 0), 1, 0)

    n = lax.fori_loop(0, entries, listing, 0, unroll=4)

    def query(item):
        return q[ids[item] // blocks]

    def slot_of(item):
        e = ids[item]
        return table[e // blocks, e % blocks]

    def live_of(item):
        e = ids[item]
        return lengths[e // blocks] - (e % blocks) * 128

    def store(item, o, z):
        o_out[ids[item]] = o
        z_out[ids[item]] = z

    attend(n, query, slot_of, live_of, store, kp, vp, scores)
    scale = 128**-0.5
    second = lax.broadcasted_iota(jnp.int32, (ROWS, 1), 0) >= HALF
    for r in range(requests):
        qr = q[r].astype(F32)
        k = nk[r].astype(F32)
        v = nv[r].astype(F32)
        s0 = jnp.sum(qr * k[0:1], axis=1, keepdims=True) * scale
        s1 = jnp.sum(qr * k[1:2], axis=1, keepdims=True) * scale
        s1 = jnp.where(second, s1, DEAD)
        m = jnp.maximum(s0, s1)
        p0 = jnp.exp(s0 - m)
        p1 = jnp.where(second, jnp.exp(s1 - m), 0.0)
        l = p0 + p1
        o_out[entries + r] = (p0 * v[0:1] + p1 * v[1:2]) / l
        z_out[entries + r] = jnp.broadcast_to(m + jnp.log(l), (ROWS, 128))
    copies[3].wait()


def merge_kernel(
    entry_h, target_h, back, o_home, z_home, w,
    out,
    entry, target, o_all, z_all, z_back, att, count, sems,
):
    requests = o_home.shape[0] // 9
    entries = requests * 8
    peers = back.shape[0]
    copies = fetch_all([(entry_h, entry), (target_h, target)], sems)
    o_all[...] = o_home[...]
    z_all[...] = z_home[...]
    side = back[...][:, CAP * ROWS :, :].reshape(peers * HALF, 128)
    kinds = 2 * CAP
    lane = lax.broadcasted_iota(jnp.int32, (128, kinds * 128), 0)
    block = lax.broadcasted_iota(jnp.int32, (128, kinds * 128), 1) // 128
    pick = jnp.logical_and(lane >= block * 4, lane < block * 4 + 3)
    z_back[...] = jnp.dot(side, pick.astype(F32).astype(BF), preferred_element_type=F32)

    def clear(i, _):
        count[i] = 0
        return 0

    lax.fori_loop(0, peers, clear, 0, unroll=8)
    for c in copies:
        c.wait()

    def fetch(j, _):
        e = entry[j]
        t = target[j]
        rank = count[t]
        count[t] = rank + 1
        o_all[e] = back[t, pl.ds(pl.multiple_of(rank * ROWS, ROWS), ROWS), :].astype(F32)
        rows = pl.ds(pl.multiple_of(t * HALF, HALF), HALF)
        for h in range(2):
            cols = pl.ds(pl.multiple_of((h * CAP + rank) * 128, 128), 128)
            z_all[e, h * HALF : (h + 1) * HALF, :] = z_back[rows, cols]
        return 0

    lax.fori_loop(0, entry.shape[0], fetch, 0, unroll=4)
    for r in range(requests):
        z = [z_all[r * 8 + b] for b in range(8)] + [z_all[entries + r]]
        o = [o_all[r * 8 + b] for b in range(8)] + [o_all[entries + r]]
        m = functools.reduce(jnp.maximum, z)
        f = [jnp.exp(x - m) for x in z]
        top = functools.reduce(jnp.add, [a * b for a, b in zip(f, o)])
        att[r * ROWS : (r + 1) * ROWS, :] = top / functools.reduce(jnp.add, f)
    heads = ROWS // 2
    a = jnp.concatenate(
        [att[pl.ds(g, 2 * requests, stride=heads), :].astype(BF) for g in range(heads)], axis=1
    )
    width = out.shape[2]

    def project(p, _):
        cols = pl.ds(pl.multiple_of(p * width, width), width)
        out[p] = jnp.dot(a, w[:, cols], preferred_element_type=F32).astype(BF)
        return 0

    lax.fori_loop(0, out.shape[0], project, 0)


def sum_kernel(parts, out):
    total = parts[0].astype(F32)
    for i in range(1, parts.shape[0]):
        total = total + parts[i].astype(F32)
    out[...] = total.astype(BF).reshape(out.shape)


def params(limit):
    return pltpu.CompilerParams(vmem_limit_bytes=limit * 1024 * 1024)


def on_device(
    queries,
    new_keys,
    new_values,
    key_pool,
    value_pool,
    block_table,
    lengths,
    lend_entry,
    lend_target,
    out_weight,
):
    requests, steps, heads, size = queries.shape
    peers = lax.axis_size("inst")
    parts = lax.axis_size("tp")
    pool = key_pool.shape[0]
    entries = block_table.size
    lends = lend_entry.shape[0]
    q = queries.reshape(requests, steps * heads, size)
    nk = new_keys.reshape(requests, steps, size)
    nv = new_values.reshape(requests, steps, size)
    kp = key_pool.reshape(pool, 128, size)
    vp = value_pool.reshape(pool, 128, size)
    target = lend_target.reshape(lends)
    held = lambda x: pltpu.with_memory_space_constraint(x, pltpu.HBM)
    smem = lambda *n: pltpu.SMEM(n, jnp.int32)
    sems = lambda n: pltpu.SemaphoreType.DMA((n,))
    like = lambda x: jax.ShapeDtypeStruct(x.shape, x.dtype)
    scores = pltpu.VMEM((2, GROUP, ROWS, 128), F32)

    send, kp, vp = pl.pallas_call(
        pack_kernel,
        out_shape=(jax.ShapeDtypeStruct((peers, SLAB, size), BF), like(kp), like(vp)),
        in_specs=[HB] * 7,
        out_specs=(VM, VM, VM),
        scratch_shapes=[
            smem(lends),
            smem(lends),
            smem(*block_table.shape),
            smem(requests),
            pltpu.VMEM(q.shape, BF),
            pltpu.VMEM((peers * CAP, ROWS, size), BF),
            smem(peers),
            smem(peers * CAP),
            smem(peers * CAP),
            sems(7),
        ],
        compiler_params=params(16),
    )(*map(held, (lend_entry, target, block_table, lengths, q, kp, vp)))

    recv = lax.all_to_all(send, "inst", split_axis=0, concat_axis=0, tiled=True)

    tile_state = jax.ShapeDtypeStruct((entries + requests, ROWS, size), F32)
    o_home, z_home, weight = pl.pallas_call(
        home_kernel,
        out_shape=(tile_state, tile_state, like(out_weight)),
        in_specs=[HB] * 4 + [VM] * 5,
        out_specs=(VM, VM, VM),
        scratch_shapes=[
            smem(lends),
            smem(*block_table.shape),
            smem(requests),
            smem(entries),
            smem(entries + 1),
            scores,
            sems(4),
        ],
        compiler_params=params(24),
        cost_estimate=pl.CostEstimate(flops=10**9, bytes_accessed=16 * 2**20, transcendentals=0),
    )(*map(held, (lend_entry, block_table, lengths, out_weight)), q, nk, nv, kp, vp)

    back = pl.pallas_call(
        serve_kernel,
        out_shape=jax.ShapeDtypeStruct((peers, SLAB, size), BF),
        in_specs=[VM, VM, VM],
        out_specs=VM,
        scratch_shapes=[
            pltpu.VMEM((peers * HALF, 128), F32),
            pltpu.VMEM((peers, 128), jnp.int32),
            smem(peers, 128),
            smem(peers * CAP + 1),
            pltpu.VMEM((peers * CAP, ROWS, 128), F32),
            pltpu.VMEM((peers * CAP, ROWS, 128), F32),
            scores,
            pltpu.SemaphoreType.DMA,
        ],
        compiler_params=params(16),
    )(recv, kp, vp)

    mine = lax.all_to_all(back, "inst", split_axis=0, concat_axis=0, tiled=True)

    partial = pl.pallas_call(
        merge_kernel,
        out_shape=jax.ShapeDtypeStruct((parts, requests * steps, out_weight.shape[1] // parts), BF),
        in_specs=[HB] * 2 + [VM] * 4,
        out_specs=VM,
        scratch_shapes=[
            smem(lends),
            smem(lends),
            pltpu.VMEM(tile_state.shape, F32),
            pltpu.VMEM(tile_state.shape, F32),
            pltpu.VMEM((peers * HALF, 2 * CAP * 128), F32),
            pltpu.VMEM((requests * ROWS, size), F32),
            smem(peers),
            sems(2),
        ],
        compiler_params=params(24),
    )(held(lend_entry), held(target), mine, o_home, z_home, weight)

    shares = lax.all_to_all(partial, "tp", split_axis=0, concat_axis=0, tiled=True)

    return pl.pallas_call(
        sum_kernel,
        out_shape=jax.ShapeDtypeStruct((requests, steps, shares.shape[2]), BF),
        in_specs=[VM],
        out_specs=VM,
    )(shares)


def solution(mesh):
    placed = (
        P("inst", None, "tp", None),
        P("inst", None, "tp", None),
        P("inst", None, "tp", None),
        P("inst", "tp", None, None),
        P("inst", "tp", None, None),
        P("inst", None),
        P("inst"),
        P("inst"),
        P("inst", None),
        P("tp", None),
    )
    return jax.shard_map(
        on_device, mesh=mesh, in_specs=placed, out_specs=P("inst", None, "tp"), check_vma=False
    )
```

```python
import functools

import jax
import jax.numpy as jnp
from jax import lax
from jax.experimental import pallas as pl
from jax.experimental.pallas import tpu as pltpu
from jax.sharding import PartitionSpec as P

DEAD = -1e30
CAP = 2
GROUP = 8
ROWS = 16
HALF = 8
SLAB = 40
BF = jnp.bfloat16
F32 = jnp.float32
VM = pl.BlockSpec(memory_space=pltpu.VMEM)
HB = pl.BlockSpec(memory_space=pl.ANY)


def lane_iota(rows=ROWS):
    return lax.broadcasted_iota(jnp.int32, (rows, 128), 1)


def fetch_all(pairs, sems):
    copies = [pltpu.make_async_copy(a, b, sems.at[i]) for i, (a, b) in enumerate(pairs)]
    for c in copies:
        c.start()
    return copies


def pack_kernel(
    entry_h, target_h, table_h, lengths_h, q_h, kp_h, vp_h,
    send, kp, vp,
    entry, target, table, lengths, q, tiles, count, slots, lives, sems,
):
    peers = send.shape[0]
    blocks = table.shape[1]
    small = fetch_all(
        [(entry_h, entry), (target_h, target), (table_h, table), (lengths_h, lengths), (q_h, q), (kp_h, kp), (vp_h, vp)],
        sems,
    )

    def clear(i, _):
        count[i] = 0
        for c in range(CAP):
            slots[i * CAP + c] = 0
            lives[i * CAP + c] = 0
        return 0

    lax.fori_loop(0, peers, clear, 0, unroll=4)
    for c in small[:5]:
        c.wait()

    def place(j, _):
        e = entry[j]
        t = target[j]
        r = e // blocks
        b = e % blocks
        rank = count[t]
        count[t] = rank + 1
        i = t * CAP + rank
        slots[i] = table[r, b]
        lives[i] = jnp.clip(lengths[r] - b * 128, 0, 128)
        tiles[i] = q[r]
        return 0

    lax.fori_loop(0, entry.shape[0], place, 0, unroll=4)
    lane = lane_iota(HALF)

    def lay(i, _):
        v = jnp.where(lane == 0, slots[i * CAP], 0)
        v = jnp.where(lane == 1, lives[i * CAP], v)
        v = jnp.where(lane == 2, slots[i * CAP + 1], v)
        v = jnp.where(lane == 3, lives[i * CAP + 1], v)
        send[i] = jnp.concatenate(
            [tiles[i * CAP], tiles[i * CAP + 1], v.astype(F32).astype(BF)], axis=0
        )
        return 0

    lax.fori_loop(0, peers, lay, 0, unroll=4)
    for c in small[5:]:
        c.wait()


def attend(n, query, slot_of, live_of, store, kp, vp, scores):
    scale = 128**-0.5
    groups = (n + GROUP - 1) // GROUP
    lane = lane_iota()

    def score(g):
        out = []
        for i in range(GROUP):
            item = jnp.minimum(g * GROUP + i, n - 1)
            out.append(
                lax.dot_general(
                    query(item),
                    kp[slot_of(item)],
                    (((1,), (1,)), ((), ())),
                    preferred_element_type=F32,
                )
            )
        return out

    @pl.when(n > 0)
    def _():
        for i, s in enumerate(score(0)):
            scores[0, i] = s

    def work(g, _):
        now = lax.rem(g, 2)
        held = [scores[now, i] for i in range(GROUP)]
        later = score(jnp.minimum(g + 1, groups - 1))
        done = []
        for i in range(GROUP):
            item = jnp.minimum(g * GROUP + i, n - 1)
            s = jnp.where(lane < live_of(item), held[i] * scale, DEAD)
            m = jnp.max(s, axis=1, keepdims=True)
            p = jnp.exp(s - m)
            l = jnp.sum(p, axis=1, keepdims=True)
            o = jnp.dot(p.astype(BF), vp[slot_of(item)], preferred_element_type=F32) / l
            done.append((item, o, jnp.broadcast_to(m + jnp.log(l), (ROWS, 128))))
        for item, o, z in done:
            store(item, o, z)
        for i, s in enumerate(later):
            scores[1 - now, i] = s
        return 0

    lax.fori_loop(0, groups, work, 0)


def serve_kernel(recv, kp, vp, back, side_f, side_i, side_s, ids, att, lse, scores, sem):
    peers = recv.shape[0]
    side = recv[...][:, CAP * ROWS :, :].astype(F32)
    side_f[...] = side.reshape(peers * HALF, 128)
    side_i[...] = side_f[pl.ds(0, peers, stride=HALF), :].astype(jnp.int32)
    copy = pltpu.make_async_copy(side_i, side_s, sem)
    copy.start()
    att[...] = jnp.zeros(att.shape, F32)
    lse[...] = jnp.full(lse.shape, DEAD, F32)
    copy.wait()

    def listing(i, n):
        for c in range(CAP):
            ids[n] = i * CAP + c
            n = n + jnp.where(side_s[i, 2 * c + 1] > 0, 1, 0)
        return n

    n = lax.fori_loop(0, peers, listing, 0, unroll=4)

    def query(item):
        i = ids[item]
        return recv[i // CAP, pl.ds(pl.multiple_of((i % CAP) * ROWS, ROWS), ROWS), :]

    def slot_of(item):
        i = ids[item]
        return side_s[i // CAP, 2 * (i % CAP)]

    def live_of(item):
        i = ids[item]
        return side_s[i // CAP, 2 * (i % CAP) + 1]

    def store(item, o, z):
        att[ids[item]] = o
        lse[ids[item]] = z

    attend(n, query, slot_of, live_of, store, kp, vp, scores)
    lane = lane_iota(HALF)

    def lay(i, _):
        side = jnp.zeros((HALF, 128), F32)
        for c in range(CAP):
            for h in range(2):
                rest = lse[i * CAP + c, h * HALF : (h + 1) * HALF, :]
                for piece in range(3):
                    part = rest.astype(BF).astype(F32)
                    rest = rest - part
                    side = jnp.where(lane == (h * CAP + c) * 4 + piece, part, side)
        rows = jnp.concatenate([att[i * CAP], att[i * CAP + 1], side], axis=0)
        back[i] = rows.astype(BF)
        return 0

    lax.fori_loop(0, peers, lay, 0, unroll=4)


def weigh(states):
    top = functools.reduce(jnp.maximum, [z for _, z in states])
    shares = [jnp.exp(z - top) for _, z in states]
    total = functools.reduce(jnp.add, shares)
    o = functools.reduce(jnp.add, [f * o for f, (o, _) in zip(shares, states)])
    return o / total, top, total


def home_kernel(
    entry_h, table_h, lengths_h, kp_h, vp_h, q, nk, nv,
    o_out, z_out,
    entry, table, lengths, kp, vp, o_part, z_part, lent, ids, scores, sems,
):
    requests, blocks = table.shape
    entries = requests * blocks
    copies = fetch_all(
        [(entry_h, entry), (table_h, table), (lengths_h, lengths), (kp_h, kp), (vp_h, vp)], sems
    )
    z_part[...] = jnp.full(z_part.shape, DEAD, F32)
    o_part[...] = jnp.zeros(o_part.shape, F32)

    def clear(i, _):
        lent[i] = 0
        return 0

    lax.fori_loop(0, entries, clear, 0, unroll=8)
    for c in copies[:3]:
        c.wait()

    def mark(j, _):
        lent[entry[j]] = 1
        return 0

    lax.fori_loop(0, entry.shape[0], mark, 0, unroll=8)

    def listing(e, n):
        ids[n] = e
        alive = lengths[e // blocks] > (e % blocks) * 128
        return n + jnp.where(jnp.logical_and(alive, lent[e] == 0), 1, 0)

    n = lax.fori_loop(0, entries, listing, 0, unroll=4)

    def query(item):
        return q[ids[item] // blocks]

    def slot_of(item):
        e = ids[item]
        return table[e // blocks, e % blocks]

    def live_of(item):
        e = ids[item]
        return lengths[e // blocks] - (e % blocks) * 128

    def store(item, o, z):
        o_part[ids[item]] = o
        z_part[ids[item]] = z

    for c in copies[3:]:
        c.wait()
    attend(n, query, slot_of, live_of, store, kp, vp, scores)
    scale = 128**-0.5
    second = lax.broadcasted_iota(jnp.int32, (ROWS, 1), 0) >= HALF
    for r in range(requests):
        qr = q[r].astype(F32)
        k = nk[r].astype(F32)
        v = nv[r].astype(F32)
        s0 = jnp.sum(qr * k[0:1], axis=1, keepdims=True) * scale
        s1 = jnp.sum(qr * k[1:2], axis=1, keepdims=True) * scale
        s1 = jnp.where(second, s1, DEAD)
        m = jnp.maximum(s0, s1)
        p0 = jnp.exp(s0 - m)
        p1 = jnp.where(second, jnp.exp(s1 - m), 0.0)
        l = p0 + p1
        fresh = ((p0 * v[0:1] + p1 * v[1:2]) / l, jnp.broadcast_to(m + jnp.log(l), (ROWS, 128)))
        o, top, total = weigh([fresh] + [(o_part[r * 8 + b], z_part[r * 8 + b]) for b in range(8)])
        o_out[r] = o
        z_out[r] = top + jnp.log(total)


def merge_kernel(
    entry_h, target_h, w_h, back, o_home, z_home,
    out,
    entry, target, w, o_all, z_all, z_back, att, count, sems,
):
    requests = o_home.shape[0]
    peers = back.shape[0]
    width = out.shape[2]
    chunks = [(w_h.at[:, pl.ds(i * width, width)], w.at[i]) for i in range(out.shape[0])]
    copies = fetch_all([(entry_h, entry), (target_h, target)] + chunks, sems)
    o_all[...] = jnp.zeros(o_all.shape, F32)
    z_all[...] = jnp.full(z_all.shape, DEAD, F32)
    side = back[...][:, CAP * ROWS :, :].reshape(peers * HALF, 128)
    kinds = 2 * CAP
    lane = lax.broadcasted_iota(jnp.int32, (128, kinds * 128), 0)
    block = lax.broadcasted_iota(jnp.int32, (128, kinds * 128), 1) // 128
    pick = jnp.logical_and(lane >= block * 4, lane < block * 4 + 3)
    z_back[...] = jnp.dot(side, pick.astype(F32).astype(BF), preferred_element_type=F32)

    def clear(i, _):
        count[i] = 0
        return 0

    lax.fori_loop(0, peers, clear, 0, unroll=8)
    for c in copies[:2]:
        c.wait()

    def fetch(j, _):
        e = entry[j]
        t = target[j]
        rank = count[t]
        count[t] = rank + 1
        o_all[e] = back[t, pl.ds(pl.multiple_of(rank * ROWS, ROWS), ROWS), :].astype(F32)
        rows = pl.ds(pl.multiple_of(t * HALF, HALF), HALF)
        for h in range(2):
            cols = pl.ds(pl.multiple_of((h * CAP + rank) * 128, 128), 128)
            z_all[e, h * HALF : (h + 1) * HALF, :] = z_back[rows, cols]
        return 0

    lax.fori_loop(0, entry.shape[0], fetch, 0, unroll=4)
    for r in range(requests):
        parts = [(o_home[r], z_home[r])] + [(o_all[r * 8 + b], z_all[r * 8 + b]) for b in range(8)]
        att[r * ROWS : (r + 1) * ROWS, :] = weigh(parts)[0]
    heads = ROWS // 2
    a = jnp.concatenate(
        [att[pl.ds(g, 2 * requests, stride=heads), :].astype(BF) for g in range(heads)], axis=1
    )
    for i, c in enumerate(copies[2:]):
        c.wait()
        out[i] = jnp.dot(a, w[i], preferred_element_type=F32).astype(BF)


def sum_kernel(parts, out):
    total = parts[0].astype(F32)
    for i in range(1, parts.shape[0]):
        total = total + parts[i].astype(F32)
    out[...] = total.astype(BF).reshape(out.shape)


def params(limit):
    return pltpu.CompilerParams(vmem_limit_bytes=limit * 1024 * 1024)


def on_device(
    queries,
    new_keys,
    new_values,
    key_pool,
    value_pool,
    block_table,
    lengths,
    lend_entry,
    lend_target,
    out_weight,
):
    requests, steps, heads, size = queries.shape
    peers = lax.axis_size("inst")
    parts = lax.axis_size("tp")
    pool = key_pool.shape[0]
    entries = block_table.size
    lends = lend_entry.shape[0]
    q = queries.reshape(requests, steps * heads, size)
    nk = new_keys.reshape(requests, steps, size)
    nv = new_values.reshape(requests, steps, size)
    k_hbm = key_pool.reshape(pool, 128, size)
    v_hbm = value_pool.reshape(pool, 128, size)
    target = lend_target.reshape(lends)
    held = lambda x: pltpu.with_memory_space_constraint(x, pltpu.HBM)
    smem = lambda *n: pltpu.SMEM(n, jnp.int32)
    sems = lambda n: pltpu.SemaphoreType.DMA((n,))
    like = lambda x: jax.ShapeDtypeStruct(x.shape, x.dtype)
    scores = pltpu.VMEM((2, GROUP, ROWS, 128), F32)

    send, kp, vp = pl.pallas_call(
        pack_kernel,
        out_shape=(jax.ShapeDtypeStruct((peers, SLAB, size), BF), like(k_hbm), like(v_hbm)),
        in_specs=[HB] * 7,
        out_specs=(VM, VM, VM),
        scratch_shapes=[
            smem(lends),
            smem(lends),
            smem(*block_table.shape),
            smem(requests),
            pltpu.VMEM(q.shape, BF),
            pltpu.VMEM((peers * CAP, ROWS, size), BF),
            smem(peers),
            smem(peers * CAP),
            smem(peers * CAP),
            sems(7),
        ],
        compiler_params=params(16),
    )(*map(held, (lend_entry, target, block_table, lengths, q, k_hbm, v_hbm)))

    recv = lax.all_to_all(send, "inst", split_axis=0, concat_axis=0, tiled=True)

    tile_state = jax.ShapeDtypeStruct((requests, ROWS, size), F32)
    o_home, z_home = pl.pallas_call(
        home_kernel,
        out_shape=(tile_state, tile_state),
        in_specs=[HB] * 5 + [VM] * 3,
        out_specs=(VM, VM),
        scratch_shapes=[
            smem(lends),
            smem(*block_table.shape),
            smem(requests),
            pltpu.VMEM(k_hbm.shape, BF),
            pltpu.VMEM(v_hbm.shape, BF),
            pltpu.VMEM((entries, ROWS, size), F32),
            pltpu.VMEM((entries, ROWS, size), F32),
            smem(entries),
            smem(entries + 1),
            scores,
            sems(5),
        ],
        compiler_params=params(24),
        cost_estimate=pl.CostEstimate(flops=10**9, bytes_accessed=16 * 2**20, transcendentals=0),
    )(*map(held, (lend_entry, block_table, lengths, k_hbm, v_hbm)), q, nk, nv)

    back = pl.pallas_call(
        serve_kernel,
        out_shape=jax.ShapeDtypeStruct((peers, SLAB, size), BF),
        in_specs=[VM, VM, VM],
        out_specs=VM,
        scratch_shapes=[
            pltpu.VMEM((peers * HALF, 128), F32),
            pltpu.VMEM((peers, 128), jnp.int32),
            smem(peers, 128),
            smem(peers * CAP + 1),
            pltpu.VMEM((peers * CAP, ROWS, 128), F32),
            pltpu.VMEM((peers * CAP, ROWS, 128), F32),
            scores,
            pltpu.SemaphoreType.DMA,
        ],
        compiler_params=params(16),
    )(recv, kp, vp)

    mine = lax.all_to_all(back, "inst", split_axis=0, concat_axis=0, tiled=True)

    partial = pl.pallas_call(
        merge_kernel,
        out_shape=jax.ShapeDtypeStruct((parts, requests * steps, out_weight.shape[1] // parts), BF),
        in_specs=[HB] * 3 + [VM] * 3,
        out_specs=VM,
        scratch_shapes=[
            smem(lends),
            smem(lends),
            pltpu.VMEM((parts, out_weight.shape[0], out_weight.shape[1] // parts), BF),
            pltpu.VMEM((entries, ROWS, size), F32),
            pltpu.VMEM((entries, ROWS, size), F32),
            pltpu.VMEM((peers * HALF, 2 * CAP * 128), F32),
            pltpu.VMEM((requests * ROWS, size), F32),
            smem(peers),
            sems(2 + parts),
        ],
        compiler_params=params(24),
    )(*map(held, (lend_entry, target, out_weight)), mine, o_home, z_home)

    shares = lax.all_to_all(partial, "tp", split_axis=0, concat_axis=0, tiled=True)

    return pl.pallas_call(
        sum_kernel,
        out_shape=jax.ShapeDtypeStruct((requests, steps, shares.shape[2]), BF),
        in_specs=[VM],
        out_specs=VM,
        compiler_params=params(8),
    )(shares)


def solution(mesh):
    placed = (
        P("inst", None, "tp", None),
        P("inst", None, "tp", None),
        P("inst", None, "tp", None),
        P("inst", "tp", None, None),
        P("inst", "tp", None, None),
        P("inst", None),
        P("inst"),
        P("inst"),
        P("inst", None),
        P("tp", None),
    )
    return jax.shard_map(
        on_device, mesh=mesh, in_specs=placed, out_specs=P("inst", None, "tp"), check_vma=False
    )
```

```python
import functools

import jax
import jax.numpy as jnp
from jax import lax
from jax.experimental import pallas as pl
from jax.experimental.pallas import tpu as pltpu
from jax.sharding import PartitionSpec as P

DEAD = -1e30
CAP = 2
GROUP = 8
ROWS = 16
HALF = 8
SLAB = 40
BF = jnp.bfloat16
F32 = jnp.float32
VM = pl.BlockSpec(memory_space=pltpu.VMEM)
HB = pl.BlockSpec(memory_space=pl.ANY)


def lane_iota(rows=ROWS):
    return lax.broadcasted_iota(jnp.int32, (rows, 128), 1)


def fetch_all(pairs, sems):
    copies = [pltpu.make_async_copy(a, b, sems.at[i]) for i, (a, b) in enumerate(pairs)]
    for c in copies:
        c.start()
    return copies


def pack_kernel(
    entry_h, target_h, table_h, lengths_h, q_h, kp_h,
    send, kp,
    entry, target, table, lengths, q, tiles, count, slots, lives, sems,
):
    peers = send.shape[0]
    blocks = table.shape[1]
    small = fetch_all(
        [(entry_h, entry), (target_h, target), (table_h, table), (lengths_h, lengths), (q_h, q), (kp_h, kp)],
        sems,
    )

    def clear(i, _):
        count[i] = 0
        for c in range(CAP):
            slots[i * CAP + c] = 0
            lives[i * CAP + c] = 0
        return 0

    lax.fori_loop(0, peers, clear, 0, unroll=4)
    for c in small[:5]:
        c.wait()

    def place(j, _):
        e = entry[j]
        t = target[j]
        r = e // blocks
        b = e % blocks
        rank = count[t]
        count[t] = rank + 1
        i = t * CAP + rank
        slots[i] = table[r, b]
        lives[i] = jnp.clip(lengths[r] - b * 128, 0, 128)
        tiles[i] = q[r]
        return 0

    lax.fori_loop(0, entry.shape[0], place, 0, unroll=4)
    lane = lane_iota(HALF)

    def lay(i, _):
        v = jnp.where(lane == 0, slots[i * CAP], 0)
        v = jnp.where(lane == 1, lives[i * CAP], v)
        v = jnp.where(lane == 2, slots[i * CAP + 1], v)
        v = jnp.where(lane == 3, lives[i * CAP + 1], v)
        send[i] = jnp.concatenate(
            [tiles[i * CAP], tiles[i * CAP + 1], v.astype(F32).astype(BF)], axis=0
        )
        return 0

    lax.fori_loop(0, peers, lay, 0, unroll=4)
    for c in small[5:]:
        c.wait()


def attend(n, query, slot_of, live_of, store, kp, vp, scores, ready):
    scale = 128**-0.5
    groups = (n + GROUP - 1) // GROUP
    lane = lane_iota()

    def score(g):
        out = []
        for i in range(GROUP):
            item = jnp.minimum(g * GROUP + i, n - 1)
            out.append(
                lax.dot_general(
                    query(item),
                    kp[slot_of(item)],
                    (((1,), (1,)), ((), ())),
                    preferred_element_type=F32,
                )
            )
        return out

    @pl.when(n > 0)
    def _():
        for i, s in enumerate(score(0)):
            scores[0, i] = s

    ready()

    def work(g, _):
        now = lax.rem(g, 2)
        held = [scores[now, i] for i in range(GROUP)]
        later = score(jnp.minimum(g + 1, groups - 1))
        done = []
        for i in range(GROUP):
            item = jnp.minimum(g * GROUP + i, n - 1)
            s = jnp.where(lane < live_of(item), held[i] * scale, DEAD)
            m = jnp.max(s, axis=1, keepdims=True)
            p = jnp.exp(s - m)
            l = jnp.sum(p, axis=1, keepdims=True)
            o = jnp.dot(p.astype(BF), vp[slot_of(item)], preferred_element_type=F32) / l
            done.append((item, o, jnp.broadcast_to(m + jnp.log(l), (ROWS, 128))))
        for item, o, z in done:
            store(item, o, z)
        for i, s in enumerate(later):
            scores[1 - now, i] = s
        return 0

    lax.fori_loop(0, groups, work, 0)


def serve_kernel(
    vp_h, w_h, recv, kp, after,
    back, w,
    vp, side_f, side_i, side_s, ids, att, lse, scores, sems,
):
    peers = recv.shape[0]
    values = pltpu.make_async_copy(vp_h, vp, sems.at[1])
    values.start()
    width = w.shape[2]
    chunks = [(w_h.at[:, pl.ds(i * width, width)], w.at[i]) for i in range(w.shape[0])]
    weights = fetch_all(chunks, sems.at[pl.ds(2, len(chunks))])
    side = recv[...][:, CAP * ROWS :, :].astype(F32)
    side_f[...] = side.reshape(peers * HALF, 128)
    side_i[...] = side_f[pl.ds(0, peers, stride=HALF), :].astype(jnp.int32)
    copy = pltpu.make_async_copy(side_i, side_s, sems.at[0])
    copy.start()
    att[...] = jnp.zeros(att.shape, F32)
    lse[...] = jnp.full(lse.shape, DEAD, F32)
    copy.wait()

    def listing(i, n):
        for c in range(CAP):
            ids[n] = i * CAP + c
            n = n + jnp.where(side_s[i, 2 * c + 1] > 0, 1, 0)
        return n

    n = lax.fori_loop(0, peers, listing, 0, unroll=4)

    def query(item):
        i = ids[item]
        return recv[lax.shift_right_logical(i, 1), pl.ds(pl.multiple_of((i & 1) * ROWS, ROWS), ROWS), :]

    def slot_of(item):
        i = ids[item]
        return side_s[lax.shift_right_logical(i, 1), 2 * (i & 1)]

    def live_of(item):
        i = ids[item]
        return side_s[lax.shift_right_logical(i, 1), 2 * (i & 1) + 1]

    def store(item, o, z):
        att[ids[item]] = o
        lse[ids[item]] = z

    attend(n, query, slot_of, live_of, store, kp, vp, scores, values.wait)
    lane = lane_iota(HALF)

    def lay(i, _):
        side = jnp.zeros((HALF, 128), F32)
        for c in range(CAP):
            for h in range(2):
                rest = lse[i * CAP + c, h * HALF : (h + 1) * HALF, :]
                for piece in range(3):
                    part = rest.astype(BF).astype(F32)
                    rest = rest - part
                    side = jnp.where(lane == (h * CAP + c) * 4 + piece, part, side)
        rows = jnp.concatenate([att[i * CAP], att[i * CAP + 1], side], axis=0)
        back[i] = rows.astype(BF)
        return 0

    lax.fori_loop(0, peers, lay, 0, unroll=4)
    for c in weights:
        c.wait()


def weigh(states):
    top = functools.reduce(jnp.maximum, [z for _, z in states])
    shares = [jnp.exp(z - top) for _, z in states]
    total = functools.reduce(jnp.add, shares)
    o = functools.reduce(jnp.add, [f * o for f, (o, _) in zip(shares, states)])
    return o / total, top, total


def home_kernel(
    entry_h, table_h, lengths_h, kp_h, vp_h, q, nk, nv,
    o_out, z_out,
    entry, table, lengths, kp, vp, o_part, z_part, lent, ids, scores, sems,
):
    requests, blocks = table.shape
    entries = requests * blocks
    copies = fetch_all(
        [(entry_h, entry), (table_h, table), (lengths_h, lengths), (kp_h, kp), (vp_h, vp)], sems
    )
    z_part[...] = jnp.full(z_part.shape, DEAD, F32)
    o_part[...] = jnp.zeros(o_part.shape, F32)

    def clear(i, _):
        lent[i] = 0
        return 0

    lax.fori_loop(0, entries, clear, 0, unroll=8)
    for c in copies[:3]:
        c.wait()

    def mark(j, _):
        lent[entry[j]] = 1
        return 0

    lax.fori_loop(0, entry.shape[0], mark, 0, unroll=8)

    def listing(e, n):
        ids[n] = e
        alive = lengths[e // blocks] > (e % blocks) * 128
        return n + jnp.where(jnp.logical_and(alive, lent[e] == 0), 1, 0)

    n = lax.fori_loop(0, entries, listing, 0, unroll=4)

    def query(item):
        return q[ids[item] // blocks]

    def slot_of(item):
        e = ids[item]
        return table[e // blocks, e % blocks]

    def live_of(item):
        e = ids[item]
        return lengths[e // blocks] - (e % blocks) * 128

    def store(item, o, z):
        o_part[ids[item]] = o
        z_part[ids[item]] = z

    copies[3].wait()
    attend(n, query, slot_of, live_of, store, kp, vp, scores, copies[4].wait)
    scale = 128**-0.5
    second = lax.broadcasted_iota(jnp.int32, (ROWS, 1), 0) >= HALF
    for r in range(requests):
        qr = q[r].astype(F32)
        k = nk[r].astype(F32)
        v = nv[r].astype(F32)
        s0 = jnp.sum(qr * k[0:1], axis=1, keepdims=True) * scale
        s1 = jnp.sum(qr * k[1:2], axis=1, keepdims=True) * scale
        s1 = jnp.where(second, s1, DEAD)
        m = jnp.maximum(s0, s1)
        p0 = jnp.exp(s0 - m)
        p1 = jnp.where(second, jnp.exp(s1 - m), 0.0)
        l = p0 + p1
        fresh = ((p0 * v[0:1] + p1 * v[1:2]) / l, jnp.broadcast_to(m + jnp.log(l), (ROWS, 128)))
        o, top, total = weigh([fresh] + [(o_part[r * 8 + b], z_part[r * 8 + b]) for b in range(8)])
        o_out[r] = o
        z_out[r] = top + jnp.log(total)


def merge_kernel(
    entry_h, target_h, w_h, w_early, back, o_home, z_home,
    out,
    entry, target, w, o_all, z_all, z_back, att, count, sems,
):
    requests = o_home.shape[0]
    peers = back.shape[0]
    width = out.shape[2]
    early = w_early.shape[0]
    chunks = [(w_h.at[:, pl.ds((early + i) * width, width)], w.at[i]) for i in range(w.shape[0])]
    copies = fetch_all([(entry_h, entry), (target_h, target)] + chunks, sems)
    o_all[...] = jnp.zeros(o_all.shape, F32)
    z_all[...] = jnp.full(z_all.shape, DEAD, F32)
    side = back[...][:, CAP * ROWS :, :].reshape(peers * HALF, 128)
    kinds = 2 * CAP
    lane = lax.broadcasted_iota(jnp.int32, (128, kinds * 128), 0)
    block = lax.broadcasted_iota(jnp.int32, (128, kinds * 128), 1) // 128
    pick = jnp.logical_and(lane >= block * 4, lane < block * 4 + 3)
    z_back[...] = jnp.dot(side, pick.astype(F32).astype(BF), preferred_element_type=F32)

    def clear(i, _):
        count[i] = 0
        return 0

    lax.fori_loop(0, peers, clear, 0, unroll=8)
    for c in copies[:2]:
        c.wait()

    def fetch(j, _):
        e = entry[j]
        t = target[j]
        rank = count[t]
        count[t] = rank + 1
        o_all[e] = back[t, pl.ds(pl.multiple_of(rank * ROWS, ROWS), ROWS), :].astype(F32)
        rows = pl.ds(pl.multiple_of(t * HALF, HALF), HALF)
        for h in range(2):
            cols = pl.ds(pl.multiple_of((h * CAP + rank) * 128, 128), 128)
            z_all[e, h * HALF : (h + 1) * HALF, :] = z_back[rows, cols]
        return 0

    lax.fori_loop(0, entry.shape[0], fetch, 0, unroll=4)
    for r in range(requests):
        parts = [(o_home[r], z_home[r])] + [(o_all[r * 8 + b], z_all[r * 8 + b]) for b in range(8)]
        att[r * ROWS : (r + 1) * ROWS, :] = weigh(parts)[0]
    heads = ROWS // 2
    a = jnp.concatenate(
        [att[pl.ds(g, 2 * requests, stride=heads), :].astype(BF) for g in range(heads)], axis=1
    )
    for i in range(out.shape[0]):
        if i >= early:
            copies[2 + i - early].wait()
        block = w_early[i] if i < early else w[i - early]
        out[i] = jnp.dot(a, block, preferred_element_type=F32).astype(BF)


def sum_kernel(parts, out):
    total = parts[0].astype(F32)
    for i in range(1, parts.shape[0]):
        total = total + parts[i].astype(F32)
    out[...] = total.astype(BF).reshape(out.shape)


def params(limit):
    return pltpu.CompilerParams(vmem_limit_bytes=limit * 1024 * 1024)


def on_device(
    queries,
    new_keys,
    new_values,
    key_pool,
    value_pool,
    block_table,
    lengths,
    lend_entry,
    lend_target,
    out_weight,
):
    requests, steps, heads, size = queries.shape
    peers = lax.axis_size("inst")
    parts = lax.axis_size("tp")
    pool = key_pool.shape[0]
    entries = block_table.size
    lends = lend_entry.shape[0]
    q = queries.reshape(requests, steps * heads, size)
    nk = new_keys.reshape(requests, steps, size)
    nv = new_values.reshape(requests, steps, size)
    k_hbm = key_pool.reshape(pool, 128, size)
    v_hbm = value_pool.reshape(pool, 128, size)
    target = lend_target.reshape(lends)
    held = lambda x: pltpu.with_memory_space_constraint(x, pltpu.HBM)
    smem = lambda *n: pltpu.SMEM(n, jnp.int32)
    sems = lambda n: pltpu.SemaphoreType.DMA((n,))
    like = lambda x: jax.ShapeDtypeStruct(x.shape, x.dtype)
    scores = pltpu.VMEM((2, GROUP, ROWS, 128), F32)

    send, kp = pl.pallas_call(
        pack_kernel,
        out_shape=(jax.ShapeDtypeStruct((peers, SLAB, size), BF), like(k_hbm)),
        in_specs=[HB] * 6,
        out_specs=(VM, VM),
        scratch_shapes=[
            smem(lends),
            smem(lends),
            smem(*block_table.shape),
            smem(requests),
            pltpu.VMEM(q.shape, BF),
            pltpu.VMEM((peers * CAP, ROWS, size), BF),
            smem(peers),
            smem(peers * CAP),
            smem(peers * CAP),
            sems(6),
        ],
        compiler_params=params(16),
    )(*map(held, (lend_entry, target, block_table, lengths, q, k_hbm)))

    recv = lax.all_to_all(send, "inst", split_axis=0, concat_axis=0, tiled=True)

    tile_state = jax.ShapeDtypeStruct((requests, ROWS, size), F32)
    o_home, z_home = pl.pallas_call(
        home_kernel,
        out_shape=(tile_state, tile_state),
        in_specs=[HB] * 5 + [VM] * 3,
        out_specs=(VM, VM),
        scratch_shapes=[
            smem(lends),
            smem(*block_table.shape),
            smem(requests),
            pltpu.VMEM(k_hbm.shape, BF),
            pltpu.VMEM(v_hbm.shape, BF),
            pltpu.VMEM((entries, ROWS, size), F32),
            pltpu.VMEM((entries, ROWS, size), F32),
            smem(entries),
            smem(entries + 1),
            scores,
            sems(5),
        ],
        compiler_params=params(24),
        cost_estimate=pl.CostEstimate(flops=10**9, bytes_accessed=16 * 2**20, transcendentals=0),
    )(*map(held, (lend_entry, block_table, lengths, k_hbm, v_hbm)), q, nk, nv)

    width = out_weight.shape[1] // parts
    early = parts // 2
    back, w_early = pl.pallas_call(
        serve_kernel,
        out_shape=(
            jax.ShapeDtypeStruct((peers, SLAB, size), BF),
            jax.ShapeDtypeStruct((early, out_weight.shape[0], width), BF),
        ),
        in_specs=[HB, HB, VM, VM, VM],
        out_specs=(VM, VM),
        scratch_shapes=[
            pltpu.VMEM(v_hbm.shape, BF),
            pltpu.VMEM((peers * HALF, 128), F32),
            pltpu.VMEM((peers, 128), jnp.int32),
            smem(peers, 128),
            smem(peers * CAP + 1),
            pltpu.VMEM((peers * CAP, ROWS, 128), F32),
            pltpu.VMEM((peers * CAP, ROWS, 128), F32),
            scores,
            sems(2 + early),
        ],
        compiler_params=params(24),
    )(held(v_hbm), held(out_weight), recv, kp, z_home)

    mine = lax.all_to_all(back, "inst", split_axis=0, concat_axis=0, tiled=True)

    partial = pl.pallas_call(
        merge_kernel,
        out_shape=jax.ShapeDtypeStruct((parts, requests * steps, out_weight.shape[1] // parts), BF),
        in_specs=[HB] * 3 + [VM] * 4,
        out_specs=VM,
        scratch_shapes=[
            smem(lends),
            smem(lends),
            pltpu.VMEM((parts - early, out_weight.shape[0], width), BF),
            pltpu.VMEM((entries, ROWS, size), F32),
            pltpu.VMEM((entries, ROWS, size), F32),
            pltpu.VMEM((peers * HALF, 2 * CAP * 128), F32),
            pltpu.VMEM((requests * ROWS, size), F32),
            smem(peers),
            sems(2 + parts - early),
        ],
        compiler_params=params(24),
    )(*map(held, (lend_entry, target, out_weight)), w_early, mine, o_home, z_home)

    shares = lax.all_to_all(partial, "tp", split_axis=0, concat_axis=0, tiled=True)

    return pl.pallas_call(
        sum_kernel,
        out_shape=jax.ShapeDtypeStruct((requests, steps, shares.shape[2]), BF),
        in_specs=[VM],
        out_specs=VM,
        compiler_params=params(8),
    )(shares)


def solution(mesh):
    placed = (
        P("inst", None, "tp", None),
        P("inst", None, "tp", None),
        P("inst", None, "tp", None),
        P("inst", "tp", None, None),
        P("inst", "tp", None, None),
        P("inst", None),
        P("inst"),
        P("inst"),
        P("inst", None),
        P("tp", None),
    )
    return jax.shard_map(
        on_device, mesh=mesh, in_specs=placed, out_specs=P("inst", None, "tp"), check_vma=False
    )
```

```python
import functools

import jax
import jax.numpy as jnp
from jax import lax
from jax.experimental import pallas as pl
from jax.experimental.pallas import tpu as pltpu
from jax.sharding import PartitionSpec as P

DEAD = -1e30
CAP = 2
GROUP = 8
ROWS = 16
HALF = 8
SLAB = 40
BF = jnp.bfloat16
F32 = jnp.float32
VM = pl.BlockSpec(memory_space=pltpu.VMEM)
HB = pl.BlockSpec(memory_space=pl.ANY)


def lane_iota(rows=ROWS):
    return lax.broadcasted_iota(jnp.int32, (rows, 128), 1)


def fetch_all(pairs, sems):
    copies = [pltpu.make_async_copy(a, b, sems.at[i]) for i, (a, b) in enumerate(pairs)]
    for c in copies:
        c.start()
    return copies


def pack_kernel(
    entry_h, target_h, table_h, lengths_h, q_h,
    send,
    entry, target, table, lengths, q, tiles, count, slots, lives, sems,
):
    peers = send.shape[0]
    blocks = table.shape[1]
    small = fetch_all(
        [(entry_h, entry), (target_h, target), (table_h, table), (lengths_h, lengths), (q_h, q)],
        sems,
    )

    def clear(i, _):
        count[i] = 0
        for c in range(CAP):
            slots[i * CAP + c] = 0
            lives[i * CAP + c] = 0
        return 0

    lax.fori_loop(0, peers, clear, 0, unroll=4)
    for c in small:
        c.wait()

    def place(j, _):
        e = entry[j]
        t = target[j]
        r = e // blocks
        b = e % blocks
        rank = count[t]
        count[t] = rank + 1
        i = t * CAP + rank
        slots[i] = table[r, b]
        lives[i] = jnp.clip(lengths[r] - b * 128, 0, 128)
        tiles[i] = q[r]
        return 0

    lax.fori_loop(0, entry.shape[0], place, 0, unroll=4)
    lane = lane_iota(HALF)

    def lay(i, _):
        v = jnp.where(lane == 0, slots[i * CAP], 0)
        v = jnp.where(lane == 1, lives[i * CAP], v)
        v = jnp.where(lane == 2, slots[i * CAP + 1], v)
        v = jnp.where(lane == 3, lives[i * CAP + 1], v)
        send[i] = jnp.concatenate(
            [tiles[i * CAP], tiles[i * CAP + 1], v.astype(F32).astype(BF)], axis=0
        )
        return 0

    lax.fori_loop(0, peers, lay, 0, unroll=4)


def attend(n, query, slot_of, live_of, store, kp, vp, scores, ready):
    scale = 128**-0.5
    groups = (n + GROUP - 1) // GROUP
    lane = lane_iota()

    def score(g):
        out = []
        for i in range(GROUP):
            item = jnp.minimum(g * GROUP + i, n - 1)
            out.append(
                lax.dot_general(
                    query(item),
                    kp[slot_of(item)],
                    (((1,), (1,)), ((), ())),
                    preferred_element_type=F32,
                )
            )
        return out

    @pl.when(n > 0)
    def _():
        for i, s in enumerate(score(0)):
            scores[0, i] = s

    ready()

    def work(g, _):
        now = lax.rem(g, 2)
        held = [scores[now, i] for i in range(GROUP)]
        later = score(jnp.minimum(g + 1, groups - 1))
        done = []
        for i in range(GROUP):
            item = jnp.minimum(g * GROUP + i, n - 1)
            s = jnp.where(lane < live_of(item), held[i] * scale, DEAD)
            m = jnp.max(s, axis=1, keepdims=True)
            p = jnp.exp(s - m)
            l = jnp.sum(p, axis=1, keepdims=True)
            o = jnp.dot(p.astype(BF), vp[slot_of(item)], preferred_element_type=F32) / l
            done.append((item, o, jnp.broadcast_to(m + jnp.log(l), (ROWS, 128))))
        for item, o, z in done:
            store(item, o, z)
        for i, s in enumerate(later):
            scores[1 - now, i] = s
        return 0

    lax.fori_loop(0, groups, work, 0)


def serve_kernel(
    vp_h, w_h, recv, kp,
    back, w,
    vp, side_f, side_i, side_s, ids, att, lse, scores, sems,
):
    peers = recv.shape[0]
    values = pltpu.make_async_copy(vp_h, vp, sems.at[1])
    values.start()
    width = w.shape[2]
    chunks = [(w_h.at[:, pl.ds(i * width, width)], w.at[i]) for i in range(w.shape[0])]
    weights = fetch_all(chunks, sems.at[pl.ds(2, len(chunks))])
    side = recv[...][:, CAP * ROWS :, :].astype(F32)
    side_f[...] = side.reshape(peers * HALF, 128)
    side_i[...] = side_f[pl.ds(0, peers, stride=HALF), :].astype(jnp.int32)
    copy = pltpu.make_async_copy(side_i, side_s, sems.at[0])
    copy.start()
    att[...] = jnp.zeros(att.shape, F32)
    lse[...] = jnp.full(lse.shape, DEAD, F32)
    copy.wait()

    def listing(i, n):
        for c in range(CAP):
            ids[n] = i * CAP + c
            n = n + jnp.where(side_s[i, 2 * c + 1] > 0, 1, 0)
        return n

    n = lax.fori_loop(0, peers, listing, 0, unroll=4)

    def query(item):
        i = ids[item]
        return recv[lax.shift_right_logical(i, 1), pl.ds(pl.multiple_of((i & 1) * ROWS, ROWS), ROWS), :]

    def slot_of(item):
        i = ids[item]
        return side_s[lax.shift_right_logical(i, 1), 2 * (i & 1)]

    def live_of(item):
        i = ids[item]
        return side_s[lax.shift_right_logical(i, 1), 2 * (i & 1) + 1]

    def store(item, o, z):
        att[ids[item]] = o
        lse[ids[item]] = z

    attend(n, query, slot_of, live_of, store, kp, vp, scores, values.wait)
    lane = lane_iota(HALF)

    def lay(i, _):
        side = jnp.zeros((HALF, 128), F32)
        for c in range(CAP):
            for h in range(2):
                rest = lse[i * CAP + c, h * HALF : (h + 1) * HALF, :]
                for piece in range(3):
                    part = rest.astype(BF).astype(F32)
                    rest = rest - part
                    side = jnp.where(lane == (h * CAP + c) * 4 + piece, part, side)
        rows = jnp.concatenate([att[i * CAP], att[i * CAP + 1], side], axis=0)
        back[i] = rows.astype(BF)
        return 0

    lax.fori_loop(0, peers, lay, 0, unroll=4)
    for c in weights:
        c.wait()


def weigh(states):
    top = functools.reduce(jnp.maximum, [z for _, z in states])
    shares = [jnp.exp(z - top) for _, z in states]
    total = functools.reduce(jnp.add, shares)
    o = functools.reduce(jnp.add, [f * o for f, (o, _) in zip(shares, states)])
    return o / total, top, total


def home_kernel(
    entry_h, table_h, lengths_h, q_h, nk_h, nv_h, kp_h, vp_h,
    o_out, z_out, kp,
    entry, table, lengths, q, nk, nv, vp, o_part, z_part, lent, ids, scores, sems,
):
    requests, blocks = table.shape
    entries = requests * blocks
    copies = fetch_all(
        [(entry_h, entry), (table_h, table), (lengths_h, lengths), (q_h, q), (nk_h, nk), (nv_h, nv), (kp_h, kp), (vp_h, vp)],
        sems,
    )
    z_part[...] = jnp.full(z_part.shape, DEAD, F32)
    o_part[...] = jnp.zeros(o_part.shape, F32)

    def clear(i, _):
        lent[i] = 0
        return 0

    lax.fori_loop(0, entries, clear, 0, unroll=8)
    for c in copies[:6]:
        c.wait()

    def mark(j, _):
        lent[entry[j]] = 1
        return 0

    lax.fori_loop(0, entry.shape[0], mark, 0, unroll=8)

    def listing(e, n):
        ids[n] = e
        alive = lengths[e // blocks] > (e % blocks) * 128
        return n + jnp.where(jnp.logical_and(alive, lent[e] == 0), 1, 0)

    n = lax.fori_loop(0, entries, listing, 0, unroll=4)

    def query(item):
        return q[ids[item] // blocks]

    def slot_of(item):
        e = ids[item]
        return table[e // blocks, e % blocks]

    def live_of(item):
        e = ids[item]
        return lengths[e // blocks] - (e % blocks) * 128

    def store(item, o, z):
        o_part[ids[item]] = o
        z_part[ids[item]] = z

    copies[6].wait()
    attend(n, query, slot_of, live_of, store, kp, vp, scores, copies[7].wait)
    scale = 128**-0.5
    second = lax.broadcasted_iota(jnp.int32, (ROWS, 1), 0) >= HALF
    for r in range(requests):
        qr = q[r].astype(F32)
        k = nk[r].astype(F32)
        v = nv[r].astype(F32)
        s0 = jnp.sum(qr * k[0:1], axis=1, keepdims=True) * scale
        s1 = jnp.sum(qr * k[1:2], axis=1, keepdims=True) * scale
        s1 = jnp.where(second, s1, DEAD)
        m = jnp.maximum(s0, s1)
        p0 = jnp.exp(s0 - m)
        p1 = jnp.where(second, jnp.exp(s1 - m), 0.0)
        l = p0 + p1
        fresh = ((p0 * v[0:1] + p1 * v[1:2]) / l, jnp.broadcast_to(m + jnp.log(l), (ROWS, 128)))
        o, top, total = weigh([fresh] + [(o_part[r * 8 + b], z_part[r * 8 + b]) for b in range(8)])
        o_out[r] = o
        z_out[r] = top + jnp.log(total)


def merge_kernel(
    entry_h, target_h, w_h, w_early, back, o_home, z_home,
    out,
    entry, target, w, o_all, z_all, z_back, att, count, sems,
):
    requests = o_home.shape[0]
    peers = back.shape[0]
    width = out.shape[2]
    early = w_early.shape[0]
    chunks = [(w_h.at[:, pl.ds((early + i) * width, width)], w.at[i]) for i in range(w.shape[0])]
    copies = fetch_all([(entry_h, entry), (target_h, target)] + chunks, sems)
    o_all[...] = jnp.zeros(o_all.shape, F32)
    z_all[...] = jnp.full(z_all.shape, DEAD, F32)
    side = back[...][:, CAP * ROWS :, :].reshape(peers * HALF, 128)
    kinds = 2 * CAP
    lane = lax.broadcasted_iota(jnp.int32, (128, kinds * 128), 0)
    block = lax.broadcasted_iota(jnp.int32, (128, kinds * 128), 1) // 128
    pick = jnp.logical_and(lane >= block * 4, lane < block * 4 + 3)
    z_back[...] = jnp.dot(side, pick.astype(F32).astype(BF), preferred_element_type=F32)

    def clear(i, _):
        count[i] = 0
        return 0

    lax.fori_loop(0, peers, clear, 0, unroll=8)
    for c in copies[:2]:
        c.wait()

    def fetch(j, _):
        e = entry[j]
        t = target[j]
        rank = count[t]
        count[t] = rank + 1
        o_all[e] = back[t, pl.ds(pl.multiple_of(rank * ROWS, ROWS), ROWS), :].astype(F32)
        rows = pl.ds(pl.multiple_of(t * HALF, HALF), HALF)
        for h in range(2):
            cols = pl.ds(pl.multiple_of((h * CAP + rank) * 128, 128), 128)
            z_all[e, h * HALF : (h + 1) * HALF, :] = z_back[rows, cols]
        return 0

    lax.fori_loop(0, entry.shape[0], fetch, 0, unroll=4)
    for r in range(requests):
        parts = [(o_home[r], z_home[r])] + [(o_all[r * 8 + b], z_all[r * 8 + b]) for b in range(8)]
        att[r * ROWS : (r + 1) * ROWS, :] = weigh(parts)[0]
    heads = ROWS // 2
    a = jnp.concatenate(
        [att[pl.ds(g, 2 * requests, stride=heads), :].astype(BF) for g in range(heads)], axis=1
    )
    for i in range(out.shape[0]):
        if i >= early:
            copies[2 + i - early].wait()
        block = w_early[i] if i < early else w[i - early]
        out[i] = jnp.dot(a, block, preferred_element_type=F32).astype(BF)


def sum_kernel(parts, out):
    total = parts[0].astype(F32)
    for i in range(1, parts.shape[0]):
        total = total + parts[i].astype(F32)
    out[...] = total.astype(BF).reshape(out.shape)


def params(limit):
    return pltpu.CompilerParams(vmem_limit_bytes=limit * 1024 * 1024)


def on_device(
    queries,
    new_keys,
    new_values,
    key_pool,
    value_pool,
    block_table,
    lengths,
    lend_entry,
    lend_target,
    out_weight,
):
    requests, steps, heads, size = queries.shape
    peers = lax.axis_size("inst")
    parts = lax.axis_size("tp")
    pool = key_pool.shape[0]
    entries = block_table.size
    lends = lend_entry.shape[0]
    q = queries.reshape(requests, steps * heads, size)
    nk = new_keys.reshape(requests, steps, size)
    nv = new_values.reshape(requests, steps, size)
    k_hbm = key_pool.reshape(pool, 128, size)
    v_hbm = value_pool.reshape(pool, 128, size)
    target = lend_target.reshape(lends)
    held = lambda x: pltpu.with_memory_space_constraint(x, pltpu.HBM)
    smem = lambda *n: pltpu.SMEM(n, jnp.int32)
    sems = lambda n: pltpu.SemaphoreType.DMA((n,))
    like = lambda x: jax.ShapeDtypeStruct(x.shape, x.dtype)
    scores = pltpu.VMEM((2, GROUP, ROWS, 128), F32)

    send = pl.pallas_call(
        pack_kernel,
        out_shape=jax.ShapeDtypeStruct((peers, SLAB, size), BF),
        in_specs=[HB] * 5,
        out_specs=VM,
        scratch_shapes=[
            smem(lends),
            smem(lends),
            smem(*block_table.shape),
            smem(requests),
            pltpu.VMEM(q.shape, BF),
            pltpu.VMEM((peers * CAP, ROWS, size), BF),
            smem(peers),
            smem(peers * CAP),
            smem(peers * CAP),
            sems(5),
        ],
        compiler_params=params(16),
    )(*map(held, (lend_entry, target, block_table, lengths, q)))

    recv = lax.all_to_all(send, "inst", split_axis=0, concat_axis=0, tiled=True)

    tile_state = jax.ShapeDtypeStruct((requests, ROWS, size), F32)
    o_home, z_home, kp = pl.pallas_call(
        home_kernel,
        out_shape=(tile_state, tile_state, like(k_hbm)),
        in_specs=[HB] * 8,
        out_specs=(VM, VM, VM),
        scratch_shapes=[
            smem(lends),
            smem(*block_table.shape),
            smem(requests),
            pltpu.VMEM(q.shape, BF),
            pltpu.VMEM(nk.shape, BF),
            pltpu.VMEM(nv.shape, BF),
            pltpu.VMEM(v_hbm.shape, BF),
            pltpu.VMEM((entries, ROWS, size), F32),
            pltpu.VMEM((entries, ROWS, size), F32),
            smem(entries),
            smem(entries + 1),
            scores,
            sems(8),
        ],
        compiler_params=params(24),
        cost_estimate=pl.CostEstimate(flops=10**9, bytes_accessed=16 * 2**20, transcendentals=0),
    )(*map(held, (lend_entry, block_table, lengths, q, nk, nv, k_hbm, v_hbm)))

    width = out_weight.shape[1] // parts
    early = parts // 2
    back, w_early = pl.pallas_call(
        serve_kernel,
        out_shape=(
            jax.ShapeDtypeStruct((peers, SLAB, size), BF),
            jax.ShapeDtypeStruct((early, out_weight.shape[0], width), BF),
        ),
        in_specs=[HB, HB, VM, VM],
        out_specs=(VM, VM),
        scratch_shapes=[
            pltpu.VMEM(v_hbm.shape, BF),
            pltpu.VMEM((peers * HALF, 128), F32),
            pltpu.VMEM((peers, 128), jnp.int32),
            smem(peers, 128),
            smem(peers * CAP + 1),
            pltpu.VMEM((peers * CAP, ROWS, 128), F32),
            pltpu.VMEM((peers * CAP, ROWS, 128), F32),
            scores,
            sems(2 + early),
        ],
        compiler_params=params(24),
    )(held(v_hbm), held(out_weight), recv, kp)

    mine = lax.all_to_all(back, "inst", split_axis=0, concat_axis=0, tiled=True)

    partial = pl.pallas_call(
        merge_kernel,
        out_shape=jax.ShapeDtypeStruct((parts, requests * steps, out_weight.shape[1] // parts), BF),
        in_specs=[HB] * 3 + [VM] * 4,
        out_specs=VM,
        scratch_shapes=[
            smem(lends),
            smem(lends),
            pltpu.VMEM((parts - early, out_weight.shape[0], width), BF),
            pltpu.VMEM((entries, ROWS, size), F32),
            pltpu.VMEM((entries, ROWS, size), F32),
            pltpu.VMEM((peers * HALF, 2 * CAP * 128), F32),
            pltpu.VMEM((requests * ROWS, size), F32),
            smem(peers),
            sems(2 + parts - early),
        ],
        compiler_params=params(24),
    )(*map(held, (lend_entry, target, out_weight)), w_early, mine, o_home, z_home)

    shares = lax.all_to_all(partial, "tp", split_axis=0, concat_axis=0, tiled=True)

    return pl.pallas_call(
        sum_kernel,
        out_shape=jax.ShapeDtypeStruct((requests, steps, shares.shape[2]), BF),
        in_specs=[VM],
        out_specs=VM,
        compiler_params=params(8),
    )(shares)


def solution(mesh):
    placed = (
        P("inst", None, "tp", None),
        P("inst", None, "tp", None),
        P("inst", None, "tp", None),
        P("inst", "tp", None, None),
        P("inst", "tp", None, None),
        P("inst", None),
        P("inst"),
        P("inst"),
        P("inst", None),
        P("tp", None),
    )
    return jax.shard_map(
        on_device, mesh=mesh, in_specs=placed, out_specs=P("inst", None, "tp"), check_vma=False
    )
```

```python
import functools

import jax
import jax.numpy as jnp
from jax import lax
from jax.experimental import pallas as pl
from jax.experimental.pallas import tpu as pltpu
from jax.sharding import PartitionSpec as P

DEAD = -1e30
CAP = 2
GROUP = 16
ROWS = 16
HALF = 8
SLAB = 40
BF = jnp.bfloat16
F32 = jnp.float32
VM = pl.BlockSpec(memory_space=pltpu.VMEM)
HB = pl.BlockSpec(memory_space=pl.ANY)


def lane_iota(rows=ROWS):
    return lax.broadcasted_iota(jnp.int32, (rows, 128), 1)


def fetch_all(pairs, sems):
    copies = [pltpu.make_async_copy(a, b, sems.at[i]) for i, (a, b) in enumerate(pairs)]
    for c in copies:
        c.start()
    return copies


def pack_kernel(
    entry_h, target_h, table_h, lengths_h, q_h,
    send,
    entry, target, table, lengths, q, tiles, count, slots, lives, sems,
):
    peers = send.shape[0]
    blocks = table.shape[1]
    small = fetch_all(
        [(entry_h, entry), (target_h, target), (table_h, table), (lengths_h, lengths), (q_h, q)],
        sems,
    )

    def clear(i, _):
        count[i] = 0
        for c in range(CAP):
            slots[i * CAP + c] = 0
            lives[i * CAP + c] = 0
        return 0

    lax.fori_loop(0, peers, clear, 0, unroll=4)
    for c in small:
        c.wait()

    def place(j, _):
        e = entry[j]
        t = target[j]
        r = e // blocks
        b = e % blocks
        rank = count[t]
        count[t] = rank + 1
        i = t * CAP + rank
        slots[i] = table[r, b]
        lives[i] = jnp.clip(lengths[r] - b * 128, 0, 128)
        tiles[i] = q[r]
        return 0

    lax.fori_loop(0, entry.shape[0], place, 0, unroll=True)
    lane = lane_iota(HALF)

    def lay(i, _):
        v = jnp.where(lane == 0, slots[i * CAP], 0)
        v = jnp.where(lane == 1, lives[i * CAP], v)
        v = jnp.where(lane == 2, slots[i * CAP + 1], v)
        v = jnp.where(lane == 3, lives[i * CAP + 1], v)
        send[i] = jnp.concatenate(
            [tiles[i * CAP], tiles[i * CAP + 1], v.astype(F32).astype(BF)], axis=0
        )
        return 0

    lax.fori_loop(0, peers, lay, 0, unroll=8)


def attend(n, query, slot_of, live_of, store, kp, vp, scores, ready):
    scale = 128**-0.5
    groups = (n + GROUP - 1) // GROUP
    lane = lane_iota()

    def score(g):
        out = []
        for i in range(GROUP):
            item = jnp.minimum(g * GROUP + i, n - 1)
            out.append(
                lax.dot_general(
                    query(item),
                    kp[slot_of(item)],
                    (((1,), (1,)), ((), ())),
                    preferred_element_type=F32,
                )
            )
        return out

    @pl.when(n > 0)
    def _():
        for i, s in enumerate(score(0)):
            scores[0, i] = s

    ready()

    def work(g, _):
        now = lax.rem(g, 2)
        held = [scores[now, i] for i in range(GROUP)]
        later = score(jnp.minimum(g + 1, groups - 1))
        done = []
        for i in range(GROUP):
            item = jnp.minimum(g * GROUP + i, n - 1)
            s = jnp.where(lane < live_of(item), held[i] * scale, DEAD)
            m = jnp.max(s, axis=1, keepdims=True)
            p = jnp.exp(s - m)
            l = jnp.sum(p, axis=1, keepdims=True)
            o = jnp.dot(p.astype(BF), vp[slot_of(item)], preferred_element_type=F32) / l
            done.append((item, o, jnp.broadcast_to(m + jnp.log(l), (ROWS, 128))))
        for item, o, z in done:
            store(item, o, z)
        for i, s in enumerate(later):
            scores[1 - now, i] = s
        return 0

    lax.fori_loop(0, groups, work, 0)


def serve_kernel(
    vp_h, w_h, recv, kp,
    back, w,
    vp, side_f, side_i, side_s, ids, att, lse, scores, sems,
):
    peers = recv.shape[0]
    values = pltpu.make_async_copy(vp_h, vp, sems.at[1])
    values.start()
    width = w.shape[2]
    chunks = [(w_h.at[:, pl.ds(i * width, width)], w.at[i]) for i in range(w.shape[0])]
    weights = fetch_all(chunks, sems.at[pl.ds(2, len(chunks))])
    side = recv[...][:, CAP * ROWS :, :].astype(F32)
    side_f[...] = side.reshape(peers * HALF, 128)
    side_i[...] = side_f[pl.ds(0, peers, stride=HALF), :].astype(jnp.int32)
    copy = pltpu.make_async_copy(side_i, side_s, sems.at[0])
    copy.start()
    att[...] = jnp.zeros(att.shape, F32)
    lse[...] = jnp.full(lse.shape, DEAD, F32)
    copy.wait()

    def listing(i, n):
        for c in range(CAP):
            ids[n] = i * CAP + c
            n = n + jnp.where(side_s[i, 2 * c + 1] > 0, 1, 0)
        return n

    n = lax.fori_loop(0, peers, listing, 0, unroll=4)

    def query(item):
        i = ids[item]
        return recv[lax.shift_right_logical(i, 1), pl.ds(pl.multiple_of((i & 1) * ROWS, ROWS), ROWS), :]

    def slot_of(item):
        i = ids[item]
        return side_s[lax.shift_right_logical(i, 1), 2 * (i & 1)]

    def live_of(item):
        i = ids[item]
        return side_s[lax.shift_right_logical(i, 1), 2 * (i & 1) + 1]

    def store(item, o, z):
        att[ids[item]] = o
        lse[ids[item]] = z

    attend(n, query, slot_of, live_of, store, kp, vp, scores, values.wait)
    lane = lane_iota(HALF)

    def lay(i, _):
        side = jnp.zeros((HALF, 128), F32)
        for c in range(CAP):
            for h in range(2):
                rest = lse[i * CAP + c, h * HALF : (h + 1) * HALF, :]
                for piece in range(3):
                    part = rest.astype(BF).astype(F32)
                    rest = rest - part
                    side = jnp.where(lane == (h * CAP + c) * 4 + piece, part, side)
        rows = jnp.concatenate([att[i * CAP], att[i * CAP + 1], side], axis=0)
        back[i] = rows.astype(BF)
        return 0

    lax.fori_loop(0, peers, lay, 0, unroll=4)
    for c in weights:
        c.wait()


def weigh(states):
    top = functools.reduce(jnp.maximum, [z for _, z in states])
    shares = [jnp.exp(z - top) for _, z in states]
    total = functools.reduce(jnp.add, shares)
    o = functools.reduce(jnp.add, [f * o for f, (o, _) in zip(shares, states)])
    return o / total, top, total


def home_kernel(
    entry_h, table_h, lengths_h, q_h, nk_h, nv_h, kp_h, vp_h,
    o_out, z_out, kp,
    entry, table, lengths, q, nk, nv, vp, o_part, z_part, lent, ids, scores, sems,
):
    requests, blocks = table.shape
    entries = requests * blocks
    copies = fetch_all(
        [(entry_h, entry), (table_h, table), (lengths_h, lengths), (q_h, q), (nk_h, nk), (nv_h, nv), (kp_h, kp), (vp_h, vp)],
        sems,
    )
    z_part[...] = jnp.full(z_part.shape, DEAD, F32)
    o_part[...] = jnp.zeros(o_part.shape, F32)

    def clear(i, _):
        lent[i] = 0
        return 0

    lax.fori_loop(0, entries, clear, 0, unroll=8)
    for c in copies[:6]:
        c.wait()

    def mark(j, _):
        lent[entry[j]] = 1
        return 0

    lax.fori_loop(0, entry.shape[0], mark, 0, unroll=8)

    def listing(e, n):
        ids[n] = e
        alive = lengths[e // blocks] > (e % blocks) * 128
        return n + jnp.where(jnp.logical_and(alive, lent[e] == 0), 1, 0)

    n = lax.fori_loop(0, entries, listing, 0, unroll=4)

    def query(item):
        return q[ids[item] // blocks]

    def slot_of(item):
        e = ids[item]
        return table[e // blocks, e % blocks]

    def live_of(item):
        e = ids[item]
        return lengths[e // blocks] - (e % blocks) * 128

    def store(item, o, z):
        o_part[ids[item]] = o
        z_part[ids[item]] = z

    copies[6].wait()
    attend(n, query, slot_of, live_of, store, kp, vp, scores, copies[7].wait)
    scale = 128**-0.5
    second = lax.broadcasted_iota(jnp.int32, (ROWS, 1), 0) >= HALF
    for r in range(requests):
        qr = q[r].astype(F32)
        k = nk[r].astype(F32)
        v = nv[r].astype(F32)
        s0 = jnp.sum(qr * k[0:1], axis=1, keepdims=True) * scale
        s1 = jnp.sum(qr * k[1:2], axis=1, keepdims=True) * scale
        s1 = jnp.where(second, s1, DEAD)
        m = jnp.maximum(s0, s1)
        p0 = jnp.exp(s0 - m)
        p1 = jnp.where(second, jnp.exp(s1 - m), 0.0)
        l = p0 + p1
        fresh = ((p0 * v[0:1] + p1 * v[1:2]) / l, jnp.broadcast_to(m + jnp.log(l), (ROWS, 128)))
        o, top, total = weigh([fresh] + [(o_part[r * 8 + b], z_part[r * 8 + b]) for b in range(8)])
        o_out[r] = o
        z_out[r] = top + jnp.log(total)


def merge_kernel(
    entry_h, target_h, w_h, w_early, back, o_home, z_home,
    out,
    entry, target, w, o_all, z_all, z_back, att, count, sems,
):
    requests = o_home.shape[0]
    peers = back.shape[0]
    width = out.shape[2]
    early = w_early.shape[0]
    chunks = [(w_h.at[:, pl.ds((early + i) * width, width)], w.at[i]) for i in range(w.shape[0])]
    copies = fetch_all([(entry_h, entry), (target_h, target)] + chunks, sems)
    o_all[...] = jnp.zeros(o_all.shape, F32)
    z_all[...] = jnp.full(z_all.shape, DEAD, F32)
    side = back[...][:, CAP * ROWS :, :].reshape(peers * HALF, 128)
    kinds = 2 * CAP
    lane = lax.broadcasted_iota(jnp.int32, (128, kinds * 128), 0)
    block = lax.broadcasted_iota(jnp.int32, (128, kinds * 128), 1) // 128
    pick = jnp.logical_and(lane >= block * 4, lane < block * 4 + 3)
    z_back[...] = jnp.dot(side, pick.astype(F32).astype(BF), preferred_element_type=F32)

    def clear(i, _):
        count[i] = 0
        return 0

    lax.fori_loop(0, peers, clear, 0, unroll=8)
    for c in copies[:2]:
        c.wait()

    def fetch(j, _):
        e = entry[j]
        t = target[j]
        rank = count[t]
        count[t] = rank + 1
        o_all[e] = back[t, pl.ds(pl.multiple_of(rank * ROWS, ROWS), ROWS), :].astype(F32)
        rows = pl.ds(pl.multiple_of(t * HALF, HALF), HALF)
        for h in range(2):
            cols = pl.ds(pl.multiple_of((h * CAP + rank) * 128, 128), 128)
            z_all[e, h * HALF : (h + 1) * HALF, :] = z_back[rows, cols]
        return 0

    lax.fori_loop(0, entry.shape[0], fetch, 0, unroll=4)
    for r in range(requests):
        parts = [(o_home[r], z_home[r])] + [(o_all[r * 8 + b], z_all[r * 8 + b]) for b in range(8)]
        att[r * ROWS : (r + 1) * ROWS, :] = weigh(parts)[0]
    heads = ROWS // 2
    a = jnp.concatenate(
        [att[pl.ds(g, 2 * requests, stride=heads), :].astype(BF) for g in range(heads)], axis=1
    )
    for i in range(out.shape[0]):
        if i >= early:
            copies[2 + i - early].wait()
        block = w_early[i] if i < early else w[i - early]
        out[i] = jnp.dot(a, block, preferred_element_type=F32).astype(BF)


def sum_kernel(parts, out):
    total = parts[0].astype(F32)
    for i in range(1, parts.shape[0]):
        total = total + parts[i].astype(F32)
    out[...] = total.astype(BF).reshape(out.shape)


def params(limit):
    return pltpu.CompilerParams(vmem_limit_bytes=limit * 1024 * 1024)


def on_device(
    queries,
    new_keys,
    new_values,
    key_pool,
    value_pool,
    block_table,
    lengths,
    lend_entry,
    lend_target,
    out_weight,
):
    requests, steps, heads, size = queries.shape
    peers = lax.axis_size("inst")
    parts = lax.axis_size("tp")
    pool = key_pool.shape[0]
    entries = block_table.size
    lends = lend_entry.shape[0]
    q = queries.reshape(requests, steps * heads, size)
    nk = new_keys.reshape(requests, steps, size)
    nv = new_values.reshape(requests, steps, size)
    k_hbm = key_pool.reshape(pool, 128, size)
    v_hbm = value_pool.reshape(pool, 128, size)
    target = lend_target.reshape(lends)
    held = lambda x: pltpu.with_memory_space_constraint(x, pltpu.HBM)
    smem = lambda *n: pltpu.SMEM(n, jnp.int32)
    sems = lambda n: pltpu.SemaphoreType.DMA((n,))
    like = lambda x: jax.ShapeDtypeStruct(x.shape, x.dtype)
    scores = pltpu.VMEM((2, GROUP, ROWS, 128), F32)

    send = pl.pallas_call(
        pack_kernel,
        out_shape=jax.ShapeDtypeStruct((peers, SLAB, size), BF),
        in_specs=[HB] * 5,
        out_specs=VM,
        scratch_shapes=[
            smem(lends),
            smem(lends),
            smem(*block_table.shape),
            smem(requests),
            pltpu.VMEM(q.shape, BF),
            pltpu.VMEM((peers * CAP, ROWS, size), BF),
            smem(peers),
            smem(peers * CAP),
            smem(peers * CAP),
            sems(5),
        ],
        compiler_params=params(16),
    )(*map(held, (lend_entry, target, block_table, lengths, q)))

    recv = lax.all_to_all(send, "inst", split_axis=0, concat_axis=0, tiled=True)

    tile_state = jax.ShapeDtypeStruct((requests, ROWS, size), F32)
    o_home, z_home, kp = pl.pallas_call(
        home_kernel,
        out_shape=(tile_state, tile_state, like(k_hbm)),
        in_specs=[HB] * 8,
        out_specs=(VM, VM, VM),
        scratch_shapes=[
            smem(lends),
            smem(*block_table.shape),
            smem(requests),
            pltpu.VMEM(q.shape, BF),
            pltpu.VMEM(nk.shape, BF),
            pltpu.VMEM(nv.shape, BF),
            pltpu.VMEM(v_hbm.shape, BF),
            pltpu.VMEM((entries, ROWS, size), F32),
            pltpu.VMEM((entries, ROWS, size), F32),
            smem(entries),
            smem(entries + 1),
            scores,
            sems(8),
        ],
        compiler_params=params(24),
        cost_estimate=pl.CostEstimate(flops=10**9, bytes_accessed=16 * 2**20, transcendentals=0),
    )(*map(held, (lend_entry, block_table, lengths, q, nk, nv, k_hbm, v_hbm)))

    width = out_weight.shape[1] // parts
    early = 5
    back, w_early = pl.pallas_call(
        serve_kernel,
        out_shape=(
            jax.ShapeDtypeStruct((peers, SLAB, size), BF),
            jax.ShapeDtypeStruct((early, out_weight.shape[0], width), BF),
        ),
        in_specs=[HB, HB, VM, VM],
        out_specs=(VM, VM),
        scratch_shapes=[
            pltpu.VMEM(v_hbm.shape, BF),
            pltpu.VMEM((peers * HALF, 128), F32),
            pltpu.VMEM((peers, 128), jnp.int32),
            smem(peers, 128),
            smem(peers * CAP + 1),
            pltpu.VMEM((peers * CAP, ROWS, 128), F32),
            pltpu.VMEM((peers * CAP, ROWS, 128), F32),
            scores,
            sems(2 + early),
        ],
        compiler_params=params(24),
    )(held(v_hbm), held(out_weight), recv, kp)

    mine = lax.all_to_all(back, "inst", split_axis=0, concat_axis=0, tiled=True)

    partial = pl.pallas_call(
        merge_kernel,
        out_shape=jax.ShapeDtypeStruct((parts, requests * steps, out_weight.shape[1] // parts), BF),
        in_specs=[HB] * 3 + [VM] * 4,
        out_specs=VM,
        scratch_shapes=[
            smem(lends),
            smem(lends),
            pltpu.VMEM((parts - early, out_weight.shape[0], width), BF),
            pltpu.VMEM((entries, ROWS, size), F32),
            pltpu.VMEM((entries, ROWS, size), F32),
            pltpu.VMEM((peers * HALF, 2 * CAP * 128), F32),
            pltpu.VMEM((requests * ROWS, size), F32),
            smem(peers),
            sems(2 + parts - early),
        ],
        compiler_params=params(24),
    )(*map(held, (lend_entry, target, out_weight)), w_early, mine, o_home, z_home)

    shares = lax.all_to_all(partial, "tp", split_axis=0, concat_axis=0, tiled=True)

    return pl.pallas_call(
        sum_kernel,
        out_shape=jax.ShapeDtypeStruct((requests, steps, shares.shape[2]), BF),
        in_specs=[VM],
        out_specs=VM,
        compiler_params=params(8),
    )(shares)


def solution(mesh):
    placed = (
        P("inst", None, "tp", None),
        P("inst", None, "tp", None),
        P("inst", None, "tp", None),
        P("inst", "tp", None, None),
        P("inst", "tp", None, None),
        P("inst", None),
        P("inst"),
        P("inst"),
        P("inst", None),
        P("tp", None),
    )
    return jax.shard_map(
        on_device, mesh=mesh, in_specs=placed, out_specs=P("inst", None, "tp"), check_vma=False
    )
```

```python
import functools

import jax
import jax.numpy as jnp
from jax import lax
from jax.experimental import pallas as pl
from jax.experimental.pallas import tpu as pltpu
from jax.sharding import PartitionSpec as P

DEAD = -1e30
CAP = 2
GROUP = 16
ROWS = 16
HALF = 8
SLAB = CAP * ROWS + 2
BF = jnp.bfloat16
F32 = jnp.float32
VM = pl.BlockSpec(memory_space=pltpu.VMEM)
HB = pl.BlockSpec(memory_space=pl.ANY)


def lane_iota(rows=ROWS):
    return lax.broadcasted_iota(jnp.int32, (rows, 128), 1)


def fetch_all(pairs, sems):
    copies = [pltpu.make_async_copy(a, b, sems.at[i]) for i, (a, b) in enumerate(pairs)]
    for c in copies:
        c.start()
    return copies


def tile_rows(peer, rank):
    return pl.ds(peer * SLAB + rank * ROWS, ROWS)


def side_rows(peers):
    return pl.ds(CAP * ROWS, peers, stride=SLAB)


def pack_kernel(
    entry_h, target_h, table_h, lengths_h, q_h,
    send,
    entry, target, table, lengths, q, wide, count, slots, lives, sems,
):
    peers = count.shape[0]
    blocks = table.shape[1]
    small = fetch_all(
        [(entry_h, entry), (target_h, target), (table_h, table), (lengths_h, lengths), (q_h, q)],
        sems,
    )

    def clear(i, _):
        count[i] = 0
        for c in range(CAP):
            slots[i * CAP + c] = 0
            lives[i * CAP + c] = 0
        return 0

    lax.fori_loop(0, peers, clear, 0, unroll=4)
    for c in small:
        c.wait()

    def place(j, _):
        e = entry[j]
        t = target[j]
        r = e // blocks
        b = e % blocks
        rank = count[t]
        count[t] = rank + 1
        i = t * CAP + rank
        slots[i] = table[r, b]
        lives[i] = jnp.clip(lengths[r] - b * 128, 0, 128)
        wide[tile_rows(t, rank), :] = q[r].astype(F32)
        return 0

    lax.fori_loop(0, entry.shape[0], place, 0, unroll=True)
    lane = lane_iota(2)

    def lay(i, _):
        v = jnp.where(lane == 0, slots[i * CAP], 0)
        v = jnp.where(lane == 1, lives[i * CAP], v)
        v = jnp.where(lane == 2, slots[i * CAP + 1], v)
        v = jnp.where(lane == 3, lives[i * CAP + 1], v)
        wide[pl.ds(i * SLAB + CAP * ROWS, 2), :] = v.astype(F32)
        return 0

    lax.fori_loop(0, peers, lay, 0, unroll=8)
    send[...] = wide[...].astype(BF)


def attend(n, query, slot_of, live_of, store, kp, vp, scores, ready):
    scale = 128**-0.5
    groups = (n + GROUP - 1) // GROUP
    lane = lane_iota()

    def score(g):
        out = []
        for i in range(GROUP):
            item = jnp.minimum(g * GROUP + i, n - 1)
            out.append(
                lax.dot_general(
                    query(item),
                    kp[slot_of(item)],
                    (((1,), (1,)), ((), ())),
                    preferred_element_type=F32,
                )
            )
        return out

    @pl.when(n > 0)
    def _():
        for i, s in enumerate(score(0)):
            scores[0, i] = s

    ready()

    def work(g, _):
        now = lax.rem(g, 2)
        held = [scores[now, i] for i in range(GROUP)]
        later = score(jnp.minimum(g + 1, groups - 1))
        done = []
        for i in range(GROUP):
            item = jnp.minimum(g * GROUP + i, n - 1)
            s = jnp.where(lane < live_of(item), held[i] * scale, DEAD)
            m = jnp.max(s, axis=1, keepdims=True)
            p = jnp.exp(s - m)
            l = jnp.sum(p, axis=1, keepdims=True)
            o = jnp.dot(p.astype(BF), vp[slot_of(item)], preferred_element_type=F32) / l
            done.append((item, o, jnp.broadcast_to(m + jnp.log(l), (ROWS, 128))))
        for item, o, z in done:
            store(item, o, z)
        for i, s in enumerate(later):
            scores[1 - now, i] = s
        return 0

    lax.fori_loop(0, groups, work, 0)


def serve_kernel(
    vp_h, w_h, recv, kp,
    back, w,
    vp, wide, side_i, side_s, ids, answer, lse, scores, sems,
):
    peers = side_i.shape[0]
    values = pltpu.make_async_copy(vp_h, vp, sems.at[1])
    values.start()
    width = w.shape[2]
    chunks = [(w_h.at[:, pl.ds(i * width, width)], w.at[i]) for i in range(w.shape[0])]
    weights = fetch_all(chunks, sems.at[pl.ds(2, len(chunks))])
    wide[...] = recv[...].astype(F32)
    side_i[...] = wide[side_rows(peers), :].astype(jnp.int32)
    copy = pltpu.make_async_copy(side_i, side_s, sems.at[0])
    copy.start()
    answer[...] = jnp.zeros(answer.shape, F32)
    lse[...] = jnp.full(lse.shape, DEAD, F32)
    copy.wait()

    def listing(i, n):
        for c in range(CAP):
            ids[n] = i * CAP + c
            n = n + jnp.where(side_s[i, 2 * c + 1] > 0, 1, 0)
        return n

    n = lax.fori_loop(0, peers, listing, 0, unroll=4)

    def query(item):
        i = ids[item]
        return wide[tile_rows(lax.shift_right_logical(i, 1), i & 1), :].astype(BF)

    def slot_of(item):
        i = ids[item]
        return side_s[lax.shift_right_logical(i, 1), 2 * (i & 1)]

    def live_of(item):
        i = ids[item]
        return side_s[lax.shift_right_logical(i, 1), 2 * (i & 1) + 1]

    def store(item, o, z):
        i = ids[item]
        answer[tile_rows(lax.shift_right_logical(i, 1), i & 1), :] = o
        lse[pl.ds(i, 1), :] = jnp.sum(jnp.where(own, z, 0.0), axis=0, keepdims=True)

    own = lane_iota() % ROWS == lax.broadcasted_iota(jnp.int32, (ROWS, 128), 0)
    attend(n, query, slot_of, live_of, store, kp, vp, scores, values.wait)
    group = lane_iota(peers) // ROWS
    rest = jnp.where(
        group < 3, lse[pl.ds(0, peers, stride=CAP), :], lse[pl.ds(1, peers, stride=CAP), :]
    )
    side = jnp.zeros((peers, 128), F32)
    for piece in range(3):
        part = rest.astype(BF).astype(F32)
        rest = rest - part
        side = jnp.where(group % 3 == piece, part, side)
    answer[side_rows(peers), :] = side
    back[...] = answer[...].astype(BF)
    for c in weights:
        c.wait()


def weigh(states):
    top = functools.reduce(jnp.maximum, [z for _, z in states])
    shares = [jnp.exp(z - top) for _, z in states]
    total = functools.reduce(jnp.add, shares)
    o = functools.reduce(jnp.add, [f * o for f, (o, _) in zip(shares, states)])
    return o / total, top, total


def home_kernel(
    entry_h, table_h, lengths_h, q_h, nk_h, nv_h, kp_h, vp_h,
    o_out, z_out, kp,
    entry, table, lengths, q, nk, nv, vp, o_part, z_part, lent, ids, scores, sems,
):
    requests, blocks = table.shape
    entries = requests * blocks
    copies = fetch_all(
        [(entry_h, entry), (table_h, table), (lengths_h, lengths), (q_h, q), (nk_h, nk), (nv_h, nv), (kp_h, kp), (vp_h, vp)],
        sems,
    )
    z_part[...] = jnp.full(z_part.shape, DEAD, F32)
    o_part[...] = jnp.zeros(o_part.shape, F32)

    def clear(i, _):
        lent[i] = 0
        return 0

    lax.fori_loop(0, entries, clear, 0, unroll=8)
    for c in copies[:6]:
        c.wait()

    def mark(j, _):
        lent[entry[j]] = 1
        return 0

    lax.fori_loop(0, entry.shape[0], mark, 0, unroll=8)

    def listing(e, n):
        ids[n] = e
        alive = lengths[e // blocks] > (e % blocks) * 128
        return n + jnp.where(jnp.logical_and(alive, lent[e] == 0), 1, 0)

    n = lax.fori_loop(0, entries, listing, 0, unroll=4)

    def query(item):
        return q[ids[item] // blocks]

    def slot_of(item):
        e = ids[item]
        return table[e // blocks, e % blocks]

    def live_of(item):
        e = ids[item]
        return lengths[e // blocks] - (e % blocks) * 128

    def store(item, o, z):
        o_part[ids[item]] = o
        z_part[ids[item]] = z

    copies[6].wait()
    attend(n, query, slot_of, live_of, store, kp, vp, scores, copies[7].wait)
    scale = 128**-0.5
    second = lax.broadcasted_iota(jnp.int32, (ROWS, 1), 0) >= HALF
    for r in range(requests):
        qr = q[r].astype(F32)
        k = nk[r].astype(F32)
        v = nv[r].astype(F32)
        s0 = jnp.sum(qr * k[0:1], axis=1, keepdims=True) * scale
        s1 = jnp.sum(qr * k[1:2], axis=1, keepdims=True) * scale
        s1 = jnp.where(second, s1, DEAD)
        m = jnp.maximum(s0, s1)
        p0 = jnp.exp(s0 - m)
        p1 = jnp.where(second, jnp.exp(s1 - m), 0.0)
        l = p0 + p1
        fresh = ((p0 * v[0:1] + p1 * v[1:2]) / l, jnp.broadcast_to(m + jnp.log(l), (ROWS, 128)))
        o, top, total = weigh([fresh] + [(o_part[r * 8 + b], z_part[r * 8 + b]) for b in range(8)])
        o_out[r] = o
        z_out[r] = top + jnp.log(total)


def merge_kernel(
    entry_h, target_h, w_h, w_early, back, o_home, z_home,
    out,
    entry, target, w, wide, o_all, z_all, z_back, att, count, sems,
):
    requests = o_home.shape[0]
    peers = count.shape[0]
    width = out.shape[2]
    early = w_early.shape[0]
    chunks = [(w_h.at[:, pl.ds((early + i) * width, width)], w.at[i]) for i in range(w.shape[0])]
    copies = fetch_all([(entry_h, entry), (target_h, target)] + chunks, sems)
    o_all[...] = jnp.zeros(o_all.shape, F32)
    z_all[...] = jnp.full(z_all.shape, DEAD, F32)
    wide[...] = back[...].astype(F32)
    side = wide[side_rows(peers), :].reshape(peers, 1, 128)
    lane = lax.broadcasted_iota(jnp.int32, (peers, ROWS, 128), 2)
    own = lane % ROWS == lax.broadcasted_iota(jnp.int32, (peers, ROWS, 128), 1)
    ones = jnp.ones((128, 128), BF)
    for c in range(CAP):
        mine = jnp.logical_and(own, lane // (3 * ROWS) == c)
        pieces = jnp.where(mine, side, 0.0).astype(BF).reshape(peers * ROWS, 128)
        z = jnp.dot(pieces, ones, preferred_element_type=F32)
        z_back[c * peers : (c + 1) * peers] = z.reshape(peers, ROWS, 128)

    def clear(i, _):
        count[i] = 0
        return 0

    lax.fori_loop(0, peers, clear, 0, unroll=8)
    for c in copies[:2]:
        c.wait()

    def fetch(j, _):
        e = entry[j]
        t = target[j]
        rank = count[t]
        count[t] = rank + 1
        o_all[e] = wide[tile_rows(t, rank), :]
        z_all[e] = z_back[rank * peers + t]
        return 0

    lax.fori_loop(0, entry.shape[0], fetch, 0, unroll=4)
    for r in range(requests):
        parts = [(o_home[r], z_home[r])] + [(o_all[r * 8 + b], z_all[r * 8 + b]) for b in range(8)]
        att[r * ROWS : (r + 1) * ROWS, :] = weigh(parts)[0]
    heads = ROWS // 2
    a = jnp.concatenate(
        [att[pl.ds(g, 2 * requests, stride=heads), :].astype(BF) for g in range(heads)], axis=1
    )
    for i in range(out.shape[0]):
        if i >= early:
            copies[2 + i - early].wait()
        block = w_early[i] if i < early else w[i - early]
        out[i] = jnp.dot(a, block, preferred_element_type=F32).astype(BF)


def sum_kernel(parts, out):
    total = parts[0].astype(F32)
    for i in range(1, parts.shape[0]):
        total = total + parts[i].astype(F32)
    out[...] = total.astype(BF).reshape(out.shape)


def params(limit):
    return pltpu.CompilerParams(vmem_limit_bytes=limit * 1024 * 1024)


def on_device(
    queries,
    new_keys,
    new_values,
    key_pool,
    value_pool,
    block_table,
    lengths,
    lend_entry,
    lend_target,
    out_weight,
):
    requests, steps, heads, size = queries.shape
    peers = lax.axis_size("inst")
    parts = lax.axis_size("tp")
    pool = key_pool.shape[0]
    entries = block_table.size
    lends = lend_entry.shape[0]
    q = queries.reshape(requests, steps * heads, size)
    nk = new_keys.reshape(requests, steps, size)
    nv = new_values.reshape(requests, steps, size)
    k_hbm = key_pool.reshape(pool, 128, size)
    v_hbm = value_pool.reshape(pool, 128, size)
    target = lend_target.reshape(lends)
    held = lambda x: pltpu.with_memory_space_constraint(x, pltpu.HBM)
    smem = lambda *n: pltpu.SMEM(n, jnp.int32)
    sems = lambda n: pltpu.SemaphoreType.DMA((n,))
    like = lambda x: jax.ShapeDtypeStruct(x.shape, x.dtype)
    wide = pltpu.VMEM((peers * SLAB, size), F32)
    scores = pltpu.VMEM((2, GROUP, ROWS, 128), F32)

    send = pl.pallas_call(
        pack_kernel,
        out_shape=jax.ShapeDtypeStruct((peers * SLAB, size), BF),
        in_specs=[HB] * 5,
        out_specs=VM,
        scratch_shapes=[
            smem(lends),
            smem(lends),
            smem(*block_table.shape),
            smem(requests),
            pltpu.VMEM(q.shape, BF),
            wide,
            smem(peers),
            smem(peers * CAP),
            smem(peers * CAP),
            sems(5),
        ],
        compiler_params=params(16),
    )(*map(held, (lend_entry, target, block_table, lengths, q)))

    def exchange(x):
        y = x.reshape(peers, SLAB // 2, 2, size)
        y = lax.all_to_all(y, "inst", split_axis=0, concat_axis=0, tiled=True)
        return y.reshape(x.shape)

    recv = exchange(send)

    tile_state = jax.ShapeDtypeStruct((requests, ROWS, size), F32)
    o_home, z_home, kp = pl.pallas_call(
        home_kernel,
        out_shape=(tile_state, tile_state, like(k_hbm)),
        in_specs=[HB] * 8,
        out_specs=(VM, VM, VM),
        scratch_shapes=[
            smem(lends),
            smem(*block_table.shape),
            smem(requests),
            pltpu.VMEM(q.shape, BF),
            pltpu.VMEM(nk.shape, BF),
            pltpu.VMEM(nv.shape, BF),
            pltpu.VMEM(v_hbm.shape, BF),
            pltpu.VMEM((entries, ROWS, size), F32),
            pltpu.VMEM((entries, ROWS, size), F32),
            smem(entries),
            smem(entries + 1),
            scores,
            sems(8),
        ],
        compiler_params=params(24),
        cost_estimate=pl.CostEstimate(flops=10**9, bytes_accessed=16 * 2**20, transcendentals=0),
    )(*map(held, (lend_entry, block_table, lengths, q, nk, nv, k_hbm, v_hbm)))

    width = out_weight.shape[1] // parts
    early = 5
    back, w_early = pl.pallas_call(
        serve_kernel,
        out_shape=(
            jax.ShapeDtypeStruct((peers * SLAB, size), BF),
            jax.ShapeDtypeStruct((early, out_weight.shape[0], width), BF),
        ),
        in_specs=[HB, HB, VM, VM],
        out_specs=(VM, VM),
        scratch_shapes=[
            pltpu.VMEM(v_hbm.shape, BF),
            wide,
            pltpu.VMEM((peers, 128), jnp.int32),
            smem(peers, 128),
            smem(peers * CAP + 1),
            wide,
            pltpu.VMEM((peers * CAP, 128), F32),
            scores,
            sems(2 + early),
        ],
        compiler_params=params(24),
    )(held(v_hbm), held(out_weight), recv, kp)

    mine = exchange(back)

    partial = pl.pallas_call(
        merge_kernel,
        out_shape=jax.ShapeDtypeStruct((parts, requests * steps, out_weight.shape[1] // parts), BF),
        in_specs=[HB] * 3 + [VM] * 4,
        out_specs=VM,
        scratch_shapes=[
            smem(lends),
            smem(lends),
            pltpu.VMEM((parts - early, out_weight.shape[0], width), BF),
            wide,
            pltpu.VMEM((entries, ROWS, size), F32),
            pltpu.VMEM((entries, ROWS, size), F32),
            pltpu.VMEM((CAP * peers, ROWS, 128), F32),
            pltpu.VMEM((requests * ROWS, size), F32),
            smem(peers),
            sems(2 + parts - early),
        ],
        compiler_params=params(24),
    )(*map(held, (lend_entry, target, out_weight)), w_early, mine, o_home, z_home)

    shares = lax.all_to_all(partial, "tp", split_axis=0, concat_axis=0, tiled=True)

    return pl.pallas_call(
        sum_kernel,
        out_shape=jax.ShapeDtypeStruct((requests, steps, shares.shape[2]), BF),
        in_specs=[VM],
        out_specs=VM,
        compiler_params=params(8),
    )(shares)


def solution(mesh):
    placed = (
        P("inst", None, "tp", None),
        P("inst", None, "tp", None),
        P("inst", None, "tp", None),
        P("inst", "tp", None, None),
        P("inst", "tp", None, None),
        P("inst", None),
        P("inst"),
        P("inst"),
        P("inst", None),
        P("tp", None),
    )
    return jax.shard_map(
        on_device, mesh=mesh, in_specs=placed, out_specs=P("inst", None, "tp"), check_vma=False
    )
```

```python
import functools

import jax
import jax.numpy as jnp
from jax import lax
from jax.experimental import pallas as pl
from jax.experimental.pallas import tpu as pltpu
from jax.sharding import PartitionSpec as P

DEAD = -1e30
CAP = 2
GROUP = 16
ROWS = 16
HALF = 8
SLAB = CAP * ROWS + 2
BF = jnp.bfloat16
F32 = jnp.float32
VM = pl.BlockSpec(memory_space=pltpu.VMEM)
HB = pl.BlockSpec(memory_space=pl.ANY)


def lane_iota(rows=ROWS):
    return lax.broadcasted_iota(jnp.int32, (rows, 128), 1)


def fetch_all(pairs, sems):
    copies = [pltpu.make_async_copy(a, b, sems.at[i]) for i, (a, b) in enumerate(pairs)]
    for c in copies:
        c.start()
    return copies


def tile_rows(peer, rank):
    return pl.ds(peer * SLAB + rank * ROWS, ROWS)


def side_rows(peers):
    return pl.ds(CAP * ROWS, peers, stride=SLAB)


def pack_kernel(
    entry_h, target_h, table_h, lengths_h, q_h,
    send,
    entry, target, table, lengths, q, wide, count, slots, lives, sems,
):
    peers = count.shape[0]
    blocks = table.shape[1]
    small = fetch_all(
        [(entry_h, entry), (target_h, target), (table_h, table), (lengths_h, lengths), (q_h, q)],
        sems,
    )

    def clear(i, _):
        count[i] = 0
        for c in range(CAP):
            slots[i * CAP + c] = 0
            lives[i * CAP + c] = 0
        return 0

    lax.fori_loop(0, peers, clear, 0, unroll=4)
    for c in small:
        c.wait()

    def place(j, _):
        e = entry[j]
        t = target[j]
        r = e // blocks
        b = e % blocks
        rank = count[t]
        count[t] = rank + 1
        i = t * CAP + rank
        slots[i] = table[r, b]
        lives[i] = jnp.clip(lengths[r] - b * 128, 0, 128)
        wide[tile_rows(t, rank), :] = q[r].astype(F32)
        return 0

    lax.fori_loop(0, entry.shape[0], place, 0, unroll=True)
    lane = lane_iota(2)

    def lay(i, _):
        v = jnp.where(lane == 0, slots[i * CAP], 0)
        v = jnp.where(lane == 1, lives[i * CAP], v)
        v = jnp.where(lane == 2, slots[i * CAP + 1], v)
        v = jnp.where(lane == 3, lives[i * CAP + 1], v)
        wide[pl.ds(i * SLAB + CAP * ROWS, 2), :] = v.astype(F32)
        return 0

    lax.fori_loop(0, peers, lay, 0, unroll=8)
    send[...] = wide[...].astype(BF)


def attend(n, query, slot_of, live_of, store, kp, vp, scores, ready):
    scale = 128**-0.5
    groups = (n + GROUP - 1) // GROUP
    lane = lane_iota()

    def score(g):
        out = []
        for i in range(GROUP):
            item = jnp.minimum(g * GROUP + i, n - 1)
            out.append(
                lax.dot_general(
                    query(item),
                    kp[slot_of(item)],
                    (((1,), (1,)), ((), ())),
                    preferred_element_type=F32,
                )
            )
        return out

    @pl.when(n > 0)
    def _():
        for i, s in enumerate(score(0)):
            scores[0, i] = s

    ready()

    def work(g, _):
        now = lax.rem(g, 2)
        held = [scores[now, i] for i in range(GROUP)]
        later = score(jnp.minimum(g + 1, groups - 1))
        done = []
        for i in range(GROUP):
            item = jnp.minimum(g * GROUP + i, n - 1)
            s = jnp.where(lane < live_of(item), held[i] * scale, DEAD)
            m = jnp.max(s, axis=1, keepdims=True)
            p = jnp.exp(s - m)
            l = jnp.sum(p, axis=1, keepdims=True)
            o = jnp.dot(p.astype(BF), vp[slot_of(item)], preferred_element_type=F32) / l
            done.append((item, o, jnp.broadcast_to(m + jnp.log(l), (ROWS, 128))))
        for item, o, z in done:
            store(item, o, z)
        for i, s in enumerate(later):
            scores[1 - now, i] = s
        return 0

    lax.fori_loop(0, groups, work, 0)


def serve_kernel(
    vp_h, w_h, recv, kp,
    back, w,
    vp, wide, side_i, side_s, ids, answer, lse, scores, sems,
):
    peers = side_i.shape[0]
    values = pltpu.make_async_copy(vp_h, vp, sems.at[1])
    values.start()
    width = w.shape[2]
    chunks = [(w_h.at[:, pl.ds((1 + i) * width, width)], w.at[i]) for i in range(w.shape[0])]
    weights = fetch_all(chunks, sems.at[pl.ds(2, len(chunks))])
    wide[...] = recv[...].astype(F32)
    side_i[...] = wide[side_rows(peers), :].astype(jnp.int32)
    copy = pltpu.make_async_copy(side_i, side_s, sems.at[0])
    copy.start()
    answer[...] = jnp.zeros(answer.shape, F32)
    lse[...] = jnp.full(lse.shape, DEAD, F32)
    copy.wait()

    def listing(i, n):
        for c in range(CAP):
            ids[n] = i * CAP + c
            n = n + jnp.where(side_s[i, 2 * c + 1] > 0, 1, 0)
        return n

    n = lax.fori_loop(0, peers, listing, 0, unroll=4)

    def query(item):
        i = ids[item]
        return wide[tile_rows(lax.shift_right_logical(i, 1), i & 1), :].astype(BF)

    def slot_of(item):
        i = ids[item]
        return side_s[lax.shift_right_logical(i, 1), 2 * (i & 1)]

    def live_of(item):
        i = ids[item]
        return side_s[lax.shift_right_logical(i, 1), 2 * (i & 1) + 1]

    def store(item, o, z):
        i = ids[item]
        answer[tile_rows(lax.shift_right_logical(i, 1), i & 1), :] = o
        lse[pl.ds(i, 1), :] = jnp.sum(jnp.where(own, z, 0.0), axis=0, keepdims=True)

    own = lane_iota() % ROWS == lax.broadcasted_iota(jnp.int32, (ROWS, 128), 0)
    attend(n, query, slot_of, live_of, store, kp, vp, scores, values.wait)
    group = lane_iota(peers) // ROWS
    rest = jnp.where(
        group < 3, lse[pl.ds(0, peers, stride=CAP), :], lse[pl.ds(1, peers, stride=CAP), :]
    )
    side = jnp.zeros((peers, 128), F32)
    for piece in range(3):
        part = rest.astype(BF).astype(F32)
        rest = rest - part
        side = jnp.where(group % 3 == piece, part, side)
    answer[side_rows(peers), :] = side
    back[...] = answer[...].astype(BF)
    for c in weights:
        c.wait()


def weigh(states):
    top = functools.reduce(jnp.maximum, [z for _, z in states])
    shares = [jnp.exp(z - top) for _, z in states]
    total = functools.reduce(jnp.add, shares)
    o = functools.reduce(jnp.add, [f * o for f, (o, _) in zip(shares, states)])
    return o / total, top, total


def home_kernel(
    entry_h, target_h, table_h, lengths_h, q_h, nk_h, nv_h, kp_h, vp_h, w_h,
    o_out, z_out, place_out, kp, w,
    entry, target, table, lengths, q, nk, nv, vp, o_part, z_part, place, count, ids, scores, sems,
):
    requests, blocks = table.shape
    entries = requests * blocks
    copies = fetch_all(
        [(entry_h, entry), (target_h, target), (table_h, table), (lengths_h, lengths), (q_h, q), (nk_h, nk), (nv_h, nv), (kp_h, kp), (vp_h, vp), (w_h.at[:, pl.ds(0, w.shape[1])], w)],
        sems,
    )
    z_part[...] = jnp.full(z_part.shape, DEAD, F32)
    o_part[...] = jnp.zeros(o_part.shape, F32)

    peers = count.shape[0]
    none = peers * CAP

    def clear(i, _):
        place[0, i] = none
        return 0

    lax.fori_loop(0, entries, clear, 0, unroll=8)

    def clear_count(i, _):
        count[i] = 0
        return 0

    lax.fori_loop(0, peers, clear_count, 0, unroll=8)
    for c in copies[:7]:
        c.wait()

    def mark(j, _):
        t = target[j]
        rank = count[t]
        count[t] = rank + 1
        place[0, entry[j]] = t * CAP + rank
        return 0

    lax.fori_loop(0, entry.shape[0], mark, 0, unroll=8)
    placed = pltpu.make_async_copy(place, place_out, sems.at[10])
    placed.start()

    def listing(e, n):
        ids[n] = e
        alive = lengths[e // blocks] > (e % blocks) * 128
        return n + jnp.where(jnp.logical_and(alive, place[0, e] == none), 1, 0)

    n = lax.fori_loop(0, entries, listing, 0, unroll=4)

    def query(item):
        return q[ids[item] // blocks]

    def slot_of(item):
        e = ids[item]
        return table[e // blocks, e % blocks]

    def live_of(item):
        e = ids[item]
        return lengths[e // blocks] - (e % blocks) * 128

    def store(item, o, z):
        o_part[ids[item]] = o
        z_part[ids[item]] = z

    copies[7].wait()
    attend(n, query, slot_of, live_of, store, kp, vp, scores, copies[8].wait)
    scale = 128**-0.5
    second = lax.broadcasted_iota(jnp.int32, (ROWS, 1), 0) >= HALF
    for r in range(requests):
        qr = q[r].astype(F32)
        k = nk[r].astype(F32)
        v = nv[r].astype(F32)
        s0 = jnp.sum(qr * k[0:1], axis=1, keepdims=True) * scale
        s1 = jnp.sum(qr * k[1:2], axis=1, keepdims=True) * scale
        s1 = jnp.where(second, s1, DEAD)
        m = jnp.maximum(s0, s1)
        p0 = jnp.exp(s0 - m)
        p1 = jnp.where(second, jnp.exp(s1 - m), 0.0)
        l = p0 + p1
        fresh = ((p0 * v[0:1] + p1 * v[1:2]) / l, jnp.broadcast_to(m + jnp.log(l), (ROWS, 128)))
        o, top, total = weigh([fresh] + [(o_part[r * 8 + b], z_part[r * 8 + b]) for b in range(8)])
        o_out[r] = o
        z_out[r] = top + jnp.log(total)
    copies[9].wait()
    placed.wait()


def merge_kernel(
    w_h, w_first, w_early, back, o_home, z_home, place_v,
    out,
    place, w, wide, z_back, att, sems,
):
    requests = o_home.shape[0]
    peers = z_back.shape[1] - 1
    rows = peers * SLAB
    width = out.shape[2]
    early = 1 + w_early.shape[0]
    chunks = [(w_h.at[:, pl.ds((early + i) * width, width)], w.at[i]) for i in range(w.shape[0])]
    copies = fetch_all([(place_v, place)] + chunks, sems)
    wide[:rows, :] = back[...].astype(F32)
    wide[rows:, :] = jnp.zeros((ROWS, 128), F32)
    side = wide[side_rows(peers), :].reshape(peers, 1, 128)
    lane = lax.broadcasted_iota(jnp.int32, (peers, ROWS, 128), 2)
    own = lane % ROWS == lax.broadcasted_iota(jnp.int32, (peers, ROWS, 128), 1)
    ones = jnp.ones((128, 128), BF)
    for c in range(CAP):
        mine = jnp.logical_and(own, lane // (3 * ROWS) == c)
        pieces = jnp.where(mine, side, 0.0).astype(BF).reshape(peers * ROWS, 128)
        z = jnp.dot(pieces, ones, preferred_element_type=F32)
        z_back[c, :peers] = z.reshape(peers, ROWS, 128)
    z_back[0, peers] = jnp.full((ROWS, 128), DEAD, F32)
    copies[0].wait()

    for r in range(requests):
        parts = [(o_home[r], z_home[r])]
        for b in range(8):
            i = place[0, r * 8 + b]
            peer, c = lax.shift_right_logical(i, 1), i & 1
            parts.append((wide[tile_rows(peer, c), :], z_back[c, peer]))
        att[r * ROWS : (r + 1) * ROWS, :] = weigh(parts)[0]
    heads = ROWS // 2
    a = jnp.concatenate(
        [att[pl.ds(g, 2 * requests, stride=heads), :].astype(BF) for g in range(heads)], axis=1
    )
    for i in range(out.shape[0]):
        if i >= early:
            copies[1 + i - early].wait()
        block = w_first[...] if i == 0 else w_early[i - 1] if i < early else w[i - early]
        out[i] = jnp.dot(a, block, preferred_element_type=F32).astype(BF)


def sum_kernel(parts, out):
    total = parts[0].astype(F32)
    for i in range(1, parts.shape[0]):
        total = total + parts[i].astype(F32)
    out[...] = total.astype(BF).reshape(out.shape)


def params(limit):
    return pltpu.CompilerParams(vmem_limit_bytes=limit * 1024 * 1024)


def on_device(
    queries,
    new_keys,
    new_values,
    key_pool,
    value_pool,
    block_table,
    lengths,
    lend_entry,
    lend_target,
    out_weight,
):
    requests, steps, heads, size = queries.shape
    peers = lax.axis_size("inst")
    parts = lax.axis_size("tp")
    pool = key_pool.shape[0]
    entries = block_table.size
    lends = lend_entry.shape[0]
    q = queries.reshape(requests, steps * heads, size)
    nk = new_keys.reshape(requests, steps, size)
    nv = new_values.reshape(requests, steps, size)
    k_hbm = key_pool.reshape(pool, 128, size)
    v_hbm = value_pool.reshape(pool, 128, size)
    target = lend_target.reshape(lends)
    held = lambda x: pltpu.with_memory_space_constraint(x, pltpu.HBM)
    smem = lambda *n: pltpu.SMEM(n, jnp.int32)
    sems = lambda n: pltpu.SemaphoreType.DMA((n,))
    like = lambda x: jax.ShapeDtypeStruct(x.shape, x.dtype)
    wide = pltpu.VMEM((peers * SLAB, size), F32)
    scores = pltpu.VMEM((2, GROUP, ROWS, 128), F32)

    send = pl.pallas_call(
        pack_kernel,
        out_shape=jax.ShapeDtypeStruct((peers * SLAB, size), BF),
        in_specs=[HB] * 5,
        out_specs=VM,
        scratch_shapes=[
            smem(lends),
            smem(lends),
            smem(*block_table.shape),
            smem(requests),
            pltpu.VMEM(q.shape, BF),
            wide,
            smem(peers),
            smem(peers * CAP),
            smem(peers * CAP),
            sems(5),
        ],
        compiler_params=params(16),
    )(*map(held, (lend_entry, target, block_table, lengths, q)))

    def exchange(x):
        y = x.reshape(peers, SLAB // 2, 2, size)
        y = lax.all_to_all(y, "inst", split_axis=0, concat_axis=0, tiled=True)
        return y.reshape(x.shape)

    recv = exchange(send)

    tile_state = jax.ShapeDtypeStruct((requests, ROWS, size), F32)
    width = out_weight.shape[1] // parts
    o_home, z_home, place, kp, w_first = pl.pallas_call(
        home_kernel,
        out_shape=(
            tile_state,
            tile_state,
            jax.ShapeDtypeStruct((1, 128), jnp.int32),
            like(k_hbm),
            jax.ShapeDtypeStruct((out_weight.shape[0], width), BF),
        ),
        in_specs=[HB] * 10,
        out_specs=(VM, VM, VM, VM, VM),
        scratch_shapes=[
            smem(lends),
            smem(lends),
            smem(*block_table.shape),
            smem(requests),
            pltpu.VMEM(q.shape, BF),
            pltpu.VMEM(nk.shape, BF),
            pltpu.VMEM(nv.shape, BF),
            pltpu.VMEM(v_hbm.shape, BF),
            pltpu.VMEM((entries, ROWS, size), F32),
            pltpu.VMEM((entries, ROWS, size), F32),
            smem(1, 128),
            smem(peers),
            smem(entries + 1),
            scores,
            sems(11),
        ],
        compiler_params=params(24),
        cost_estimate=pl.CostEstimate(flops=10**9, bytes_accessed=16 * 2**20, transcendentals=0),
    )(*map(held, (lend_entry, target, block_table, lengths, q, nk, nv, k_hbm, v_hbm, out_weight)))

    early = 4
    back, w_early = pl.pallas_call(
        serve_kernel,
        out_shape=(
            jax.ShapeDtypeStruct((peers * SLAB, size), BF),
            jax.ShapeDtypeStruct((early, out_weight.shape[0], width), BF),
        ),
        in_specs=[HB, HB, VM, VM],
        out_specs=(VM, VM),
        scratch_shapes=[
            pltpu.VMEM(v_hbm.shape, BF),
            wide,
            pltpu.VMEM((peers, 128), jnp.int32),
            smem(peers, 128),
            smem(peers * CAP + 1),
            wide,
            pltpu.VMEM((peers * CAP, 128), F32),
            scores,
            sems(2 + early),
        ],
        compiler_params=params(24),
    )(held(v_hbm), held(out_weight), recv, kp)

    mine = exchange(back)

    partial = pl.pallas_call(
        merge_kernel,
        out_shape=jax.ShapeDtypeStruct((parts, requests * steps, out_weight.shape[1] // parts), BF),
        in_specs=[HB] + [VM] * 6,
        out_specs=VM,
        scratch_shapes=[
            smem(1, 128),
            pltpu.VMEM((parts - 1 - early, out_weight.shape[0], width), BF),
            pltpu.VMEM((peers * SLAB + ROWS, size), F32),
            pltpu.VMEM((CAP, peers + 1, ROWS, 128), F32),
            pltpu.VMEM((requests * ROWS, size), F32),
            sems(parts - early),
        ],
        compiler_params=params(24),
    )(held(out_weight), w_first, w_early, mine, o_home, z_home, place)

    shares = lax.all_to_all(partial, "tp", split_axis=0, concat_axis=0, tiled=True)

    return pl.pallas_call(
        sum_kernel,
        out_shape=jax.ShapeDtypeStruct((requests, steps, shares.shape[2]), BF),
        in_specs=[VM],
        out_specs=VM,
        compiler_params=params(8),
    )(shares)


def solution(mesh):
    placed = (
        P("inst", None, "tp", None),
        P("inst", None, "tp", None),
        P("inst", None, "tp", None),
        P("inst", "tp", None, None),
        P("inst", "tp", None, None),
        P("inst", None),
        P("inst"),
        P("inst"),
        P("inst", None),
        P("tp", None),
    )
    return jax.shard_map(
        on_device, mesh=mesh, in_specs=placed, out_specs=P("inst", None, "tp"), check_vma=False
    )
```

```python
import functools

import jax
import jax.numpy as jnp
from jax import lax
from jax.experimental import pallas as pl
from jax.experimental.pallas import tpu as pltpu
from jax.sharding import PartitionSpec as P

DEAD = -1e30
CAP = 2
GROUP = 16
ROWS = 16
HALF = 8
SLAB = CAP * ROWS + 2
BF = jnp.bfloat16
F32 = jnp.float32
VM = pl.BlockSpec(memory_space=pltpu.VMEM)
HB = pl.BlockSpec(memory_space=pl.ANY)


def lane_iota(rows=ROWS):
    return lax.broadcasted_iota(jnp.int32, (rows, 128), 1)


def fetch_all(pairs, sems):
    copies = [pltpu.make_async_copy(a, b, sems.at[i]) for i, (a, b) in enumerate(pairs)]
    for c in copies:
        c.start()
    return copies


MARGIN = 48


def tile_rows(peer, rank):
    return pl.ds(peer * SLAB + rank * ROWS, ROWS)


def side_rows(peers):
    return pl.ds(CAP * ROWS, peers, stride=SLAB)


def note_last(target, latest):
    for j in range(target.shape[0]):
        latest[target[j]] = j


def rank_of(j, t, latest):
    return jnp.where(latest[t] == j, 0, 1)


def pack_kernel(
    entry_h, target_h, table_h, lengths_h, q_h,
    send,
    entry, target, table, lengths, q, wide, packed, latest, slots, lives, sems,
):
    peers = latest.shape[0]
    blocks = table.shape[1]
    small = fetch_all(
        [(entry_h, entry), (target_h, target), (table_h, table), (lengths_h, lengths), (q_h, q)],
        sems,
    )

    def clear(i, _):
        for c in range(CAP):
            slots[i * CAP + c] = 0
            lives[i * CAP + c] = 0
        return 0

    lax.fori_loop(0, peers, clear, 0, unroll=8)
    for c in small:
        c.wait()

    note_last(target, latest)

    def place(j, _):
        e = entry[j]
        t = target[j]
        r = e // blocks
        b = e % blocks
        rank = rank_of(j, t, latest)
        i = t * CAP + rank
        slots[i] = table[r, b]
        lives[i] = jnp.clip(lengths[r] - b * 128, 0, 128)
        wide[tile_rows(t, rank), :] = q[r].astype(F32)
        return 0

    lax.fori_loop(0, entry.shape[0], place, 0, unroll=True)
    lane = lane_iota(2)

    def lay(i, _):
        v = jnp.where(lane == 0, slots[i * CAP], 0)
        v = jnp.where(lane == 1, lives[i * CAP], v)
        v = jnp.where(lane == 2, slots[i * CAP + 1], v)
        v = jnp.where(lane == 3, lives[i * CAP + 1], v)
        wide[pl.ds(i * SLAB + CAP * ROWS, 2), :] = v.astype(F32)
        return 0

    pieces = 4
    size = peers * SLAB // pieces
    copies = []
    for k in range(pieces):
        lax.fori_loop(k * peers // pieces, (k + 1) * peers // pieces, lay, 0, unroll=True)
        rows = pl.ds(k * size, size)
        packed[rows, :] = wide[rows, :].astype(BF)
        copies.append(pltpu.make_async_copy(packed.at[rows, :], send.at[rows, :], sems.at[5 + k]))
        copies[-1].start()
    for c in copies:
        c.wait()


def attend(n, query, slot_of, live_of, store, kp, vp, scores, ready):
    scale = 128**-0.5
    groups = (n + GROUP - 1) // GROUP
    lane = lane_iota()

    def score(g):
        out = []
        for i in range(GROUP):
            item = jnp.minimum(g * GROUP + i, n - 1)
            out.append(
                lax.dot_general(
                    query(item),
                    kp[slot_of(item)],
                    (((1,), (1,)), ((), ())),
                    preferred_element_type=F32,
                )
            )
        return out

    @pl.when(n > 0)
    def _():
        for i, s in enumerate(score(0)):
            scores[0, i] = s

    ready()

    def finish(g):
        now = lax.rem(g, 2)
        done = []
        for i in range(GROUP):
            item = jnp.minimum(g * GROUP + i, n - 1)
            s = jnp.where(lane < live_of(item), scores[now, i] * scale, DEAD)
            m = jnp.max(s, axis=1, keepdims=True)
            p = jnp.exp(s - m)
            l = jnp.sum(p, axis=1, keepdims=True)
            o = jnp.dot(p.astype(BF), vp[slot_of(item)], preferred_element_type=F32) / l
            done.append((item, o, jnp.broadcast_to(m + jnp.log(l), (ROWS, 128))))
        return done

    def work(g, _):
        later = score(g + 1)
        for item, o, z in finish(g):
            store(item, o, z)
        for i, s in enumerate(later):
            scores[lax.rem(g + 1, 2), i] = s
        return 0

    lax.fori_loop(0, groups - 1, work, 0)

    @pl.when(n > 0)
    def _():
        for item, o, z in finish(groups - 1):
            store(item, o, z)


def serve_kernel(
    vp_h, recv, kp,
    back,
    vp, wide, side_i, side_s, ids, answer, lse, scores, sems,
):
    peers = side_i.shape[0]
    values = pltpu.make_async_copy(vp_h, vp, sems.at[1])
    values.start()
    wide[: recv.shape[0], :] = recv[...].astype(F32)
    side_i[...] = wide[side_rows(peers), :].astype(jnp.int32)
    copy = pltpu.make_async_copy(side_i, side_s, sems.at[0])
    copy.start()
    answer[...] = jnp.zeros(answer.shape, F32)
    lse[...] = jnp.full(lse.shape, DEAD, F32)
    copy.wait()

    def listing(i, n):
        for c in range(CAP):
            ids[n] = i * CAP + c
            n = n + jnp.where(side_s[i, 2 * c + 1] > 0, 1, 0)
        return n

    n = lax.fori_loop(0, peers, listing, 0, unroll=4)

    def query(item):
        i = ids[item]
        return wide[tile_rows(lax.shift_right_logical(i, 1), i & 1), :].astype(BF)

    def slot_of(item):
        i = ids[item]
        return side_s[lax.shift_right_logical(i, 1), 2 * (i & 1)]

    def live_of(item):
        i = ids[item]
        return side_s[lax.shift_right_logical(i, 1), 2 * (i & 1) + 1]

    def store(item, o, z):
        i = ids[item]
        answer[tile_rows(lax.shift_right_logical(i, 1), i & 1), :] = o
        lse[pl.ds(i, 1), :] = jnp.sum(jnp.where(own, z, 0.0), axis=0, keepdims=True)

    own = lane_iota() % ROWS == lax.broadcasted_iota(jnp.int32, (ROWS, 128), 0)
    attend(n, query, slot_of, live_of, store, kp, vp, scores, values.wait)
    group = lane_iota(peers) // ROWS
    rest = jnp.where(
        group < 3, lse[pl.ds(0, peers, stride=CAP), :], lse[pl.ds(1, peers, stride=CAP), :]
    )
    side = jnp.zeros((peers, 128), F32)
    for piece in range(3):
        part = rest.astype(BF).astype(F32)
        rest = rest - part
        side = jnp.where(group % 3 == piece, part, side)
    answer[side_rows(peers), :] = side
    back[...] = answer[: back.shape[0], :].astype(BF)


def weigh(states):
    top = functools.reduce(jnp.maximum, [z for _, z in states])
    shares = [jnp.exp(z - top) for _, z in states]
    total = functools.reduce(jnp.add, shares)
    o = functools.reduce(jnp.add, [f * o for f, (o, _) in zip(shares, states)])
    return o / total, top, total


def home_kernel(
    entry_h, target_h, table_h, lengths_h, q_h, nk_h, nv_h, kp_h, vp_h,
    o_out, z_out, place_out, kp,
    entry, target, table, lengths, q, nk, nv, vp, o_part, z_part, place, latest, ids, scores, sems,
):
    requests, blocks = table.shape
    entries = requests * blocks
    copies = fetch_all(
        [(entry_h, entry), (target_h, target), (table_h, table), (lengths_h, lengths), (q_h, q), (nk_h, nk), (nv_h, nv), (kp_h, kp), (vp_h, vp)],
        sems,
    )
    z_part[...] = jnp.full(z_part.shape, DEAD, F32)
    o_part[...] = jnp.zeros(o_part.shape, F32)

    peers = latest.shape[0]
    none = peers * CAP

    def clear(i, _):
        place[0, i] = none
        return 0

    lax.fori_loop(0, entries, clear, 0, unroll=8)

    for c in copies[:7]:
        c.wait()

    note_last(target, latest)

    def mark(j, _):
        t = target[j]
        place[0, entry[j]] = t * CAP + rank_of(j, t, latest)
        return 0

    lax.fori_loop(0, entry.shape[0], mark, 0, unroll=8)
    placed = pltpu.make_async_copy(place, place_out, sems.at[9])
    placed.start()

    def listing(e, n):
        ids[n] = e
        alive = lengths[e // blocks] > (e % blocks) * 128
        return n + jnp.where(jnp.logical_and(alive, place[0, e] == none), 1, 0)

    n = lax.fori_loop(0, entries, listing, 0, unroll=4)

    def query(item):
        return q[ids[item] // blocks]

    def slot_of(item):
        e = ids[item]
        return table[e // blocks, e % blocks]

    def live_of(item):
        e = ids[item]
        return lengths[e // blocks] - (e % blocks) * 128

    def store(item, o, z):
        o_part[ids[item]] = o
        z_part[ids[item]] = z

    copies[7].wait()
    attend(n, query, slot_of, live_of, store, kp, vp, scores, copies[8].wait)
    scale = 128**-0.5
    second = lax.broadcasted_iota(jnp.int32, (ROWS, 1), 0) >= HALF
    for r in range(requests):
        qr = q[r].astype(F32)
        k = nk[r].astype(F32)
        v = nv[r].astype(F32)
        s0 = jnp.sum(qr * k[0:1], axis=1, keepdims=True) * scale
        s1 = jnp.sum(qr * k[1:2], axis=1, keepdims=True) * scale
        s1 = jnp.where(second, s1, DEAD)
        m = jnp.maximum(s0, s1)
        p0 = jnp.exp(s0 - m)
        p1 = jnp.where(second, jnp.exp(s1 - m), 0.0)
        l = p0 + p1
        fresh = ((p0 * v[0:1] + p1 * v[1:2]) / l, jnp.broadcast_to(m + jnp.log(l), (ROWS, 128)))
        o, top, total = weigh([fresh] + [(o_part[r * 8 + b], z_part[r * 8 + b]) for b in range(8)])
        o_out[r] = o
        z_out[r] = top + jnp.log(total)
    placed.wait()


def merge_kernel(
    w, back, o_home, z_home, place_v,
    out,
    place, wide, z_back, att, sems,
):
    requests = o_home.shape[0]
    peers = z_back.shape[1] - 1
    rows = peers * SLAB
    width = out.shape[2]
    copy = pltpu.make_async_copy(place_v, place, sems.at[0])
    copy.start()
    wide[:rows, :] = back[...].astype(F32)
    wide[rows:, :] = jnp.zeros((MARGIN, 128), F32)
    side = wide[side_rows(peers), :].reshape(peers, 1, 128)
    lane = lax.broadcasted_iota(jnp.int32, (peers, ROWS, 128), 2)
    own = lane % ROWS == lax.broadcasted_iota(jnp.int32, (peers, ROWS, 128), 1)
    ones = jnp.ones((128, 128), BF)
    for c in range(CAP):
        mine = jnp.logical_and(own, lane // (3 * ROWS) == c)
        pieces = jnp.where(mine, side, 0.0).astype(BF).reshape(peers * ROWS, 128)
        z = jnp.dot(pieces, ones, preferred_element_type=F32)
        z_back[c, :peers] = z.reshape(peers, ROWS, 128)
    z_back[0, peers] = jnp.full((ROWS, 128), DEAD, F32)
    copy.wait()

    for r in range(requests):
        parts = [(o_home[r], z_home[r])]
        for b in range(8):
            i = place[0, r * 8 + b]
            peer, c = lax.shift_right_logical(i, 1), i & 1
            parts.append((wide[tile_rows(peer, c), :], z_back[c, peer]))
        att[r * ROWS : (r + 1) * ROWS, :] = weigh(parts)[0]
    heads = ROWS // 2
    a = jnp.concatenate(
        [att[pl.ds(g, 2 * requests, stride=heads), :].astype(BF) for g in range(heads)], axis=1
    )
    for i in range(out.shape[0]):
        block = w[:, i * width : (i + 1) * width]
        out[i] = jnp.dot(a, block, preferred_element_type=F32).astype(BF)


def sum_kernel(parts, out):
    total = parts[0].astype(F32)
    for i in range(1, parts.shape[0]):
        total = total + parts[i].astype(F32)
    out[...] = total.astype(BF).reshape(out.shape)


def params(limit):
    return pltpu.CompilerParams(vmem_limit_bytes=limit * 1024 * 1024)


def on_device(
    queries,
    new_keys,
    new_values,
    key_pool,
    value_pool,
    block_table,
    lengths,
    lend_entry,
    lend_target,
    out_weight,
):
    requests, steps, heads, size = queries.shape
    peers = lax.axis_size("inst")
    parts = lax.axis_size("tp")
    pool = key_pool.shape[0]
    entries = block_table.size
    lends = lend_entry.shape[0]
    q = queries.reshape(requests, steps * heads, size)
    nk = new_keys.reshape(requests, steps, size)
    nv = new_values.reshape(requests, steps, size)
    k_hbm = key_pool.reshape(pool, 128, size)
    v_hbm = value_pool.reshape(pool, 128, size)
    target = lend_target.reshape(lends)
    held = lambda x: pltpu.with_memory_space_constraint(x, pltpu.HBM)
    smem = lambda *n: pltpu.SMEM(n, jnp.int32)
    sems = lambda n: pltpu.SemaphoreType.DMA((n,))
    like = lambda x: jax.ShapeDtypeStruct(x.shape, x.dtype)
    wide = pltpu.VMEM((peers * SLAB + MARGIN, size), F32)
    scores = pltpu.VMEM((2, GROUP, ROWS, 128), F32)

    send = pl.pallas_call(
        pack_kernel,
        out_shape=jax.ShapeDtypeStruct((peers * SLAB, size), BF),
        in_specs=[HB] * 5,
        out_specs=HB,
        scratch_shapes=[
            smem(lends),
            smem(lends),
            smem(*block_table.shape),
            smem(requests),
            pltpu.VMEM(q.shape, BF),
            wide,
            pltpu.VMEM((peers * SLAB, size), BF),
            smem(peers),
            smem(peers * CAP),
            smem(peers * CAP),
            sems(9),
        ],
        compiler_params=params(16),
    )(*map(held, (lend_entry, target, block_table, lengths, q)))

    def exchange(x):
        y = x.reshape(peers, SLAB // 2, 2, size)
        y = lax.all_to_all(y, "inst", split_axis=0, concat_axis=0, tiled=True)
        return y.reshape(x.shape)

    recv = exchange(send)

    tile_state = jax.ShapeDtypeStruct((requests, ROWS, size), F32)
    o_home, z_home, place, kp = pl.pallas_call(
        home_kernel,
        out_shape=(
            tile_state,
            tile_state,
            jax.ShapeDtypeStruct((1, 128), jnp.int32),
            like(k_hbm),
        ),
        in_specs=[HB] * 9,
        out_specs=(VM, VM, VM, VM),
        scratch_shapes=[
            smem(lends),
            smem(lends),
            smem(*block_table.shape),
            smem(requests),
            pltpu.VMEM(q.shape, BF),
            pltpu.VMEM(nk.shape, BF),
            pltpu.VMEM(nv.shape, BF),
            pltpu.VMEM(v_hbm.shape, BF),
            pltpu.VMEM((entries, ROWS, size), F32),
            pltpu.VMEM((entries, ROWS, size), F32),
            smem(1, 128),
            smem(peers),
            smem(entries + 1),
            scores,
            sems(10),
        ],
        compiler_params=params(24),
        cost_estimate=pl.CostEstimate(flops=10**9, bytes_accessed=16 * 2**20, transcendentals=0),
    )(*map(held, (lend_entry, target, block_table, lengths, q, nk, nv, k_hbm, v_hbm)))

    back = pl.pallas_call(
        serve_kernel,
        out_shape=jax.ShapeDtypeStruct((peers * SLAB, size), BF),
        in_specs=[HB, VM, VM],
        out_specs=VM,
        scratch_shapes=[
            pltpu.VMEM(v_hbm.shape, BF),
            wide,
            pltpu.VMEM((peers, 128), jnp.int32),
            smem(peers, 128),
            smem(peers * CAP + 1),
            wide,
            pltpu.VMEM((peers * CAP + MARGIN, 128), F32),
            scores,
            sems(2),
        ],
        compiler_params=params(16),
        cost_estimate=pl.CostEstimate(flops=10000000000, bytes_accessed=16777216, transcendentals=0),
    )(held(v_hbm), recv, kp)

    mine = exchange(back)

    partial = pl.pallas_call(
        merge_kernel,
        out_shape=jax.ShapeDtypeStruct((parts, requests * steps, out_weight.shape[1] // parts), BF),
        in_specs=[VM] * 5,
        out_specs=VM,
        scratch_shapes=[
            smem(1, 128),
            wide,
            pltpu.VMEM((CAP, peers + 1, ROWS, 128), F32),
            pltpu.VMEM((requests * ROWS + MARGIN, size), F32),
            sems(1),
        ],
        compiler_params=params(24),
    )(out_weight, mine, o_home, z_home, place)

    shares = lax.all_to_all(partial, "tp", split_axis=0, concat_axis=0, tiled=True)

    return pl.pallas_call(
        sum_kernel,
        out_shape=jax.ShapeDtypeStruct((requests, steps, shares.shape[2]), BF),
        in_specs=[VM],
        out_specs=VM,
        compiler_params=params(8),
    )(shares)


def solution(mesh):
    placed = (
        P("inst", None, "tp", None),
        P("inst", None, "tp", None),
        P("inst", None, "tp", None),
        P("inst", "tp", None, None),
        P("inst", "tp", None, None),
        P("inst", None),
        P("inst"),
        P("inst"),
        P("inst", None),
        P("tp", None),
    )
    return jax.shard_map(
        on_device, mesh=mesh, in_specs=placed, out_specs=P("inst", None, "tp"), check_vma=False
    )
```

```python
import functools

import jax
import jax.numpy as jnp
from jax import lax
from jax.experimental import pallas as pl
from jax.experimental.pallas import tpu as pltpu
from jax.sharding import PartitionSpec as P

DEAD = -1e30
CAP = 2
GROUP = 24
ROWS = 16
HALF = 8
SLAB = CAP * ROWS + 2
BF = jnp.bfloat16
F32 = jnp.float32
VM = pl.BlockSpec(memory_space=pltpu.VMEM)
HB = pl.BlockSpec(memory_space=pl.ANY)


def lane_iota(rows=ROWS):
    return lax.broadcasted_iota(jnp.int32, (rows, 128), 1)


def fetch_all(pairs, sems):
    copies = [pltpu.make_async_copy(a, b, sems.at[i]) for i, (a, b) in enumerate(pairs)]
    for c in copies:
        c.start()
    return copies


MARGIN = 48


def tile_rows(peer, rank):
    return pl.ds(peer * SLAB + rank * ROWS, ROWS)


def side_rows(peers):
    return pl.ds(CAP * ROWS, peers, stride=SLAB)


def note_last(target, latest):
    for j in range(target.shape[0]):
        latest[target[j]] = j


def rank_of(j, t, latest):
    return jnp.where(latest[t] == j, 0, 1)


def pack_kernel(
    entry_h, target_h, table_h, lengths_h, q_h,
    send,
    entry, target, table, lengths, q, wide, packed, latest, slots, lives, sems,
):
    peers = latest.shape[0]
    blocks = table.shape[1]
    small = fetch_all(
        [(entry_h, entry), (target_h, target), (table_h, table), (lengths_h, lengths), (q_h, q)],
        sems,
    )

    def clear(i, _):
        for c in range(CAP):
            slots[i * CAP + c] = 0
            lives[i * CAP + c] = 0
        return 0

    lax.fori_loop(0, peers, clear, 0, unroll=8)
    for c in small:
        c.wait()

    note_last(target, latest)

    def place(j, _):
        e = entry[j]
        t = target[j]
        r = e // blocks
        b = e % blocks
        rank = rank_of(j, t, latest)
        i = t * CAP + rank
        slots[i] = table[r, b]
        lives[i] = jnp.clip(lengths[r] - b * 128, 0, 128)
        wide[tile_rows(t, rank), :] = q[r].astype(F32)
        return 0

    lax.fori_loop(0, entry.shape[0], place, 0, unroll=True)
    lane = lane_iota(2)

    def lay(i, _):
        v = jnp.where(lane == 0, slots[i * CAP], 0)
        v = jnp.where(lane == 1, lives[i * CAP], v)
        v = jnp.where(lane == 2, slots[i * CAP + 1], v)
        v = jnp.where(lane == 3, lives[i * CAP + 1], v)
        wide[pl.ds(i * SLAB + CAP * ROWS, 2), :] = v.astype(F32)
        return 0

    pieces = 4
    size = peers * SLAB // pieces
    copies = []
    for k in range(pieces):
        lax.fori_loop(k * peers // pieces, (k + 1) * peers // pieces, lay, 0, unroll=True)
        rows = pl.ds(k * size, size)
        packed[rows, :] = wide[rows, :].astype(BF)
        copies.append(pltpu.make_async_copy(packed.at[rows, :], send.at[rows, :], sems.at[5 + k]))
        copies[-1].start()
    for c in copies:
        c.wait()


def attend(n, query, slot_of, live_of, store, kp, vp, scores, ready):
    scale = 128**-0.5
    groups = (n + GROUP - 1) // GROUP
    lane = lane_iota()

    def score(g):
        out = []
        for i in range(0, GROUP, 2):
            pair = [jnp.minimum(g * GROUP + i + k, n - 1) for k in range(2)]
            s = lax.dot_general(
                jnp.concatenate([query(item) for item in pair], axis=0),
                jnp.concatenate([kp[slot_of(item)] for item in pair], axis=0),
                (((1,), (1,)), ((), ())),
                preferred_element_type=F32,
            )
            out += [s[:ROWS, :128], s[ROWS:, 128:]]
        return out

    @pl.when(n > 0)
    def _():
        for i, s in enumerate(score(0)):
            scores[0, i] = s

    ready()

    def finish(g):
        now = lax.rem(g, 2)
        done = []
        for i in range(0, GROUP, 2):
            pair = [jnp.minimum(g * GROUP + i + k, n - 1) for k in range(2)]
            weights, totals, ends = [], [], []
            for k, item in enumerate(pair):
                s = jnp.where(lane < live_of(item), scores[now, i + k] * scale, DEAD)
                m = jnp.max(s, axis=1, keepdims=True)
                p = jnp.exp(s - m)
                l = jnp.sum(p, axis=1, keepdims=True)
                weights.append(p.astype(BF))
                totals.append(l)
                ends.append(jnp.broadcast_to(m + jnp.log(l), (ROWS, 128)))
            nil = jnp.zeros((ROWS, 128), BF)
            o = jnp.dot(
                jnp.concatenate(
                    [
                        jnp.concatenate([weights[0], nil], axis=1),
                        jnp.concatenate([nil, weights[1]], axis=1),
                    ],
                    axis=0,
                ),
                jnp.concatenate([vp[slot_of(item)] for item in pair], axis=0),
                preferred_element_type=F32,
            )
            parts = [o[:ROWS], o[ROWS:]]
            for k, item in enumerate(pair):
                done.append((item, parts[k] / totals[k], ends[k]))
        return done

    def work(g, _):
        later = score(g + 1)
        for item, o, z in finish(g):
            store(item, o, z)
        for i, s in enumerate(later):
            scores[lax.rem(g + 1, 2), i] = s
        return 0

    lax.fori_loop(0, groups - 1, work, 0)

    @pl.when(n > 0)
    def _():
        for item, o, z in finish(groups - 1):
            store(item, o, z)


def serve_kernel(
    vp_h, recv, kp,
    back,
    vp, wide, side_i, side_s, ids, answer, lse, scores, sems,
):
    peers = side_i.shape[0]
    values = pltpu.make_async_copy(vp_h, vp, sems.at[1])
    values.start()
    wide[: recv.shape[0], :] = recv[...].astype(F32)
    side_i[...] = wide[side_rows(peers), :].astype(jnp.int32)
    copy = pltpu.make_async_copy(side_i, side_s, sems.at[0])
    copy.start()
    answer[...] = jnp.zeros(answer.shape, F32)
    lse[...] = jnp.full(lse.shape, DEAD, F32)
    copy.wait()

    def listing(i, n):
        for c in range(CAP):
            ids[n] = i * CAP + c
            n = n + jnp.where(side_s[i, 2 * c + 1] > 0, 1, 0)
        return n

    n = lax.fori_loop(0, peers, listing, 0, unroll=4)

    def query(item):
        i = ids[item]
        return wide[tile_rows(lax.shift_right_logical(i, 1), i & 1), :].astype(BF)

    def slot_of(item):
        i = ids[item]
        return side_s[lax.shift_right_logical(i, 1), 2 * (i & 1)]

    def live_of(item):
        i = ids[item]
        return side_s[lax.shift_right_logical(i, 1), 2 * (i & 1) + 1]

    def store(item, o, z):
        i = ids[item]
        answer[tile_rows(lax.shift_right_logical(i, 1), i & 1), :] = o
        lse[pl.ds(i, 1), :] = jnp.sum(jnp.where(own, z, 0.0), axis=0, keepdims=True)

    own = lane_iota() % ROWS == lax.broadcasted_iota(jnp.int32, (ROWS, 128), 0)
    attend(n, query, slot_of, live_of, store, kp, vp, scores, values.wait)
    group = lane_iota(peers) // ROWS
    rest = jnp.where(
        group < 3, lse[pl.ds(0, peers, stride=CAP), :], lse[pl.ds(1, peers, stride=CAP), :]
    )
    side = jnp.zeros((peers, 128), F32)
    for piece in range(3):
        part = rest.astype(BF).astype(F32)
        rest = rest - part
        side = jnp.where(group % 3 == piece, part, side)
    answer[side_rows(peers), :] = side
    back[...] = answer[: back.shape[0], :].astype(BF)


def weigh(states):
    top = functools.reduce(jnp.maximum, [z for _, z in states])
    shares = [jnp.exp(z - top) for _, z in states]
    total = functools.reduce(jnp.add, shares)
    o = functools.reduce(jnp.add, [f * o for f, (o, _) in zip(shares, states)])
    return o / total, top, total


def home_kernel(
    entry_h, target_h, table_h, lengths_h, q_h, nk_h, nv_h, kp_h, vp_h,
    o_out, z_out, place_out, kp,
    entry, target, table, lengths, q, nk, nv, vp, o_part, z_part, place, latest, ids, scores, sems,
):
    requests, blocks = table.shape
    entries = requests * blocks
    copies = fetch_all(
        [(entry_h, entry), (target_h, target), (table_h, table), (lengths_h, lengths), (q_h, q), (nk_h, nk), (nv_h, nv), (kp_h, kp), (vp_h, vp)],
        sems,
    )
    z_part[...] = jnp.full(z_part.shape, DEAD, F32)
    o_part[...] = jnp.zeros(o_part.shape, F32)

    peers = latest.shape[0]
    none = peers * CAP

    def clear(i, _):
        place[0, i] = none
        return 0

    lax.fori_loop(0, entries, clear, 0, unroll=8)

    for c in copies[:7]:
        c.wait()

    note_last(target, latest)

    def mark(j, _):
        t = target[j]
        place[0, entry[j]] = t * CAP + rank_of(j, t, latest)
        return 0

    lax.fori_loop(0, entry.shape[0], mark, 0, unroll=8)
    placed = pltpu.make_async_copy(place, place_out, sems.at[9])
    placed.start()

    def listing(e, n):
        ids[n] = e
        alive = lengths[e // blocks] > (e % blocks) * 128
        return n + jnp.where(jnp.logical_and(alive, place[0, e] == none), 1, 0)

    n = lax.fori_loop(0, entries, listing, 0, unroll=4)

    def query(item):
        return q[ids[item] // blocks]

    def slot_of(item):
        e = ids[item]
        return table[e // blocks, e % blocks]

    def live_of(item):
        e = ids[item]
        return lengths[e // blocks] - (e % blocks) * 128

    def store(item, o, z):
        o_part[ids[item]] = o
        z_part[ids[item]] = z

    copies[7].wait()
    attend(n, query, slot_of, live_of, store, kp, vp, scores, copies[8].wait)
    scale = 128**-0.5
    second = lax.broadcasted_iota(jnp.int32, (ROWS, 1), 0) >= HALF
    for r in range(requests):
        qr = q[r].astype(F32)
        k = nk[r].astype(F32)
        v = nv[r].astype(F32)
        s0 = jnp.sum(qr * k[0:1], axis=1, keepdims=True) * scale
        s1 = jnp.sum(qr * k[1:2], axis=1, keepdims=True) * scale
        s1 = jnp.where(second, s1, DEAD)
        m = jnp.maximum(s0, s1)
        p0 = jnp.exp(s0 - m)
        p1 = jnp.where(second, jnp.exp(s1 - m), 0.0)
        l = p0 + p1
        fresh = ((p0 * v[0:1] + p1 * v[1:2]) / l, jnp.broadcast_to(m + jnp.log(l), (ROWS, 128)))
        o, top, total = weigh([fresh] + [(o_part[r * 8 + b], z_part[r * 8 + b]) for b in range(8)])
        o_out[r] = o
        z_out[r] = top + jnp.log(total)
    placed.wait()


def merge_kernel(
    w, back, o_home, z_home, place_v,
    out,
    place, wide, z_back, att, sems,
):
    requests = o_home.shape[0]
    peers = z_back.shape[1] - 1
    rows = peers * SLAB
    width = out.shape[2]
    copy = pltpu.make_async_copy(place_v, place, sems.at[0])
    copy.start()
    wide[:rows, :] = back[...].astype(F32)
    wide[rows:, :] = jnp.zeros((MARGIN, 128), F32)
    side = wide[side_rows(peers), :].reshape(peers, 1, 128)
    lane = lax.broadcasted_iota(jnp.int32, (peers, ROWS, 128), 2)
    own = lane % ROWS == lax.broadcasted_iota(jnp.int32, (peers, ROWS, 128), 1)
    ones = jnp.ones((128, 128), BF)
    for c in range(CAP):
        mine = jnp.logical_and(own, lane // (3 * ROWS) == c)
        pieces = jnp.where(mine, side, 0.0).astype(BF).reshape(peers * ROWS, 128)
        z = jnp.dot(pieces, ones, preferred_element_type=F32)
        z_back[c, :peers] = z.reshape(peers, ROWS, 128)
    z_back[0, peers] = jnp.full((ROWS, 128), DEAD, F32)
    copy.wait()

    for r in range(requests):
        parts = [(o_home[r], z_home[r])]
        for b in range(8):
            i = place[0, r * 8 + b]
            peer, c = lax.shift_right_logical(i, 1), i & 1
            parts.append((wide[tile_rows(peer, c), :], z_back[c, peer]))
        att[r * ROWS : (r + 1) * ROWS, :] = weigh(parts)[0]
    heads = ROWS // 2
    a = jnp.concatenate(
        [att[pl.ds(g, 2 * requests, stride=heads), :].astype(BF) for g in range(heads)], axis=1
    )
    for i in range(out.shape[0]):
        block = w[:, i * width : (i + 1) * width]
        out[i] = jnp.dot(a, block, preferred_element_type=F32).astype(BF)


def sum_kernel(parts, out):
    total = parts[0].astype(F32)
    for i in range(1, parts.shape[0]):
        total = total + parts[i].astype(F32)
    out[...] = total.astype(BF).reshape(out.shape)


def params(limit):
    return pltpu.CompilerParams(vmem_limit_bytes=limit * 1024 * 1024)


def on_device(
    queries,
    new_keys,
    new_values,
    key_pool,
    value_pool,
    block_table,
    lengths,
    lend_entry,
    lend_target,
    out_weight,
):
    requests, steps, heads, size = queries.shape
    peers = lax.axis_size("inst")
    parts = lax.axis_size("tp")
    pool = key_pool.shape[0]
    entries = block_table.size
    lends = lend_entry.shape[0]
    q = queries.reshape(requests, steps * heads, size)
    nk = new_keys.reshape(requests, steps, size)
    nv = new_values.reshape(requests, steps, size)
    k_hbm = key_pool.reshape(pool, 128, size)
    v_hbm = value_pool.reshape(pool, 128, size)
    target = lend_target.reshape(lends)
    held = lambda x: pltpu.with_memory_space_constraint(x, pltpu.HBM)
    smem = lambda *n: pltpu.SMEM(n, jnp.int32)
    sems = lambda n: pltpu.SemaphoreType.DMA((n,))
    like = lambda x: jax.ShapeDtypeStruct(x.shape, x.dtype)
    wide = pltpu.VMEM((peers * SLAB + MARGIN, size), F32)
    scores = pltpu.VMEM((2, GROUP, ROWS, 128), F32)

    send = pl.pallas_call(
        pack_kernel,
        out_shape=jax.ShapeDtypeStruct((peers * SLAB, size), BF),
        in_specs=[HB] * 5,
        out_specs=HB,
        scratch_shapes=[
            smem(lends),
            smem(lends),
            smem(*block_table.shape),
            smem(requests),
            pltpu.VMEM(q.shape, BF),
            wide,
            pltpu.VMEM((peers * SLAB, size), BF),
            smem(peers),
            smem(peers * CAP),
            smem(peers * CAP),
            sems(9),
        ],
        compiler_params=params(16),
    )(*map(held, (lend_entry, target, block_table, lengths, q)))

    def exchange(x):
        y = x.reshape(peers, SLAB // 2, 2, size)
        y = lax.all_to_all(y, "inst", split_axis=0, concat_axis=0, tiled=True)
        return y.reshape(x.shape)

    recv = exchange(send)

    tile_state = jax.ShapeDtypeStruct((requests, ROWS, size), F32)
    o_home, z_home, place, kp = pl.pallas_call(
        home_kernel,
        out_shape=(
            tile_state,
            tile_state,
            jax.ShapeDtypeStruct((1, 128), jnp.int32),
            like(k_hbm),
        ),
        in_specs=[HB] * 9,
        out_specs=(VM, VM, VM, VM),
        scratch_shapes=[
            smem(lends),
            smem(lends),
            smem(*block_table.shape),
            smem(requests),
            pltpu.VMEM(q.shape, BF),
            pltpu.VMEM(nk.shape, BF),
            pltpu.VMEM(nv.shape, BF),
            pltpu.VMEM(v_hbm.shape, BF),
            pltpu.VMEM((entries, ROWS, size), F32),
            pltpu.VMEM((entries, ROWS, size), F32),
            smem(1, 128),
            smem(peers),
            smem(entries + 1),
            scores,
            sems(10),
        ],
        compiler_params=params(24),
        cost_estimate=pl.CostEstimate(flops=10**9, bytes_accessed=16 * 2**20, transcendentals=0),
    )(*map(held, (lend_entry, target, block_table, lengths, q, nk, nv, k_hbm, v_hbm)))

    back = pl.pallas_call(
        serve_kernel,
        out_shape=jax.ShapeDtypeStruct((peers * SLAB, size), BF),
        in_specs=[HB, VM, VM],
        out_specs=VM,
        scratch_shapes=[
            pltpu.VMEM(v_hbm.shape, BF),
            wide,
            pltpu.VMEM((peers, 128), jnp.int32),
            smem(peers, 128),
            smem(peers * CAP + 1),
            wide,
            pltpu.VMEM((peers * CAP + MARGIN, 128), F32),
            scores,
            sems(2),
        ],
        compiler_params=params(16),
        cost_estimate=pl.CostEstimate(flops=10000000000, bytes_accessed=16777216, transcendentals=0),
    )(held(v_hbm), recv, kp)

    mine = exchange(back)

    partial = pl.pallas_call(
        merge_kernel,
        out_shape=jax.ShapeDtypeStruct((parts, requests * steps, out_weight.shape[1] // parts), BF),
        in_specs=[VM] * 5,
        out_specs=VM,
        scratch_shapes=[
            smem(1, 128),
            wide,
            pltpu.VMEM((CAP, peers + 1, ROWS, 128), F32),
            pltpu.VMEM((requests * ROWS + MARGIN, size), F32),
            sems(1),
        ],
        compiler_params=params(24),
    )(out_weight, mine, o_home, z_home, place)

    shares = lax.all_to_all(partial, "tp", split_axis=0, concat_axis=0, tiled=True)

    return pl.pallas_call(
        sum_kernel,
        out_shape=jax.ShapeDtypeStruct((requests, steps, shares.shape[2]), BF),
        in_specs=[VM],
        out_specs=VM,
        compiler_params=params(8),
    )(shares)


def solution(mesh):
    placed = (
        P("inst", None, "tp", None),
        P("inst", None, "tp", None),
        P("inst", None, "tp", None),
        P("inst", "tp", None, None),
        P("inst", "tp", None, None),
        P("inst", None),
        P("inst"),
        P("inst"),
        P("inst", None),
        P("tp", None),
    )
    return jax.shard_map(
        on_device, mesh=mesh, in_specs=placed, out_specs=P("inst", None, "tp"), check_vma=False
    )
```

```python
import functools

import jax
import jax.numpy as jnp
from jax import lax
from jax.experimental import pallas as pl
from jax.experimental.pallas import tpu as pltpu
from jax.sharding import PartitionSpec as P

DEAD = -1e30
CAP = 2
GROUP = 24
ROWS = 16
HALF = 8
SLAB = CAP * ROWS + 2
BF = jnp.bfloat16
F32 = jnp.float32
VM = pl.BlockSpec(memory_space=pltpu.VMEM)
HB = pl.BlockSpec(memory_space=pl.ANY)


def lane_iota(rows=ROWS):
    return lax.broadcasted_iota(jnp.int32, (rows, 128), 1)


def fetch_all(pairs, sems):
    copies = [pltpu.make_async_copy(a, b, sems.at[i]) for i, (a, b) in enumerate(pairs)]
    for c in copies:
        c.start()
    return copies


MARGIN = 48


def tile_rows(peer, rank):
    return pl.ds(peer * SLAB + rank * ROWS, ROWS)


def side_rows(peers):
    return pl.ds(CAP * ROWS, peers, stride=SLAB)


def split(entry):
    return lax.shift_right_logical(entry, 3), entry & 7


def note_last(target, latest):
    for j in range(target.shape[0]):
        latest[target[j]] = j


def rank_of(j, t, latest):
    return jnp.where(latest[t] == j, 0, 1)


def pack_kernel(
    entry_h, target_h, table_h, lengths_h, q_h,
    send,
    entry, target, table, lengths, q, wide, packed, latest, slots, lives, sems,
):
    peers = latest.shape[0]
    small = fetch_all(
        [(entry_h, entry), (target_h, target), (table_h, table), (lengths_h, lengths), (q_h, q)],
        sems,
    )

    def clear(i, _):
        for c in range(CAP):
            slots[i * CAP + c] = 0
            lives[i * CAP + c] = 0
        return 0

    lax.fori_loop(0, peers, clear, 0, unroll=8)
    for c in small:
        c.wait()

    note_last(target, latest)

    def place(j, _):
        e = entry[j]
        t = target[j]
        r, b = split(e)
        rank = rank_of(j, t, latest)
        i = t * CAP + rank
        slots[i] = table[r, b]
        lives[i] = jnp.clip(lengths[r] - b * 128, 0, 128)
        wide[tile_rows(t, rank), :] = q[r].astype(F32)
        return 0

    lax.fori_loop(0, entry.shape[0], place, 0, unroll=True)
    lane = lane_iota(2)

    def lay(i, _):
        v = jnp.where(lane == 0, slots[i * CAP], 0)
        v = jnp.where(lane == 1, lives[i * CAP], v)
        v = jnp.where(lane == 2, slots[i * CAP + 1], v)
        v = jnp.where(lane == 3, lives[i * CAP + 1], v)
        wide[pl.ds(i * SLAB + CAP * ROWS, 2), :] = v.astype(F32)
        return 0

    pieces = 4
    size = peers * SLAB // pieces
    copies = []
    for k in range(pieces):
        lax.fori_loop(k * peers // pieces, (k + 1) * peers // pieces, lay, 0, unroll=True)
        rows = pl.ds(k * size, size)
        packed[rows, :] = wide[rows, :].astype(BF)
        copies.append(pltpu.make_async_copy(packed.at[rows, :], send.at[rows, :], sems.at[5 + k]))
        copies[-1].start()
    for c in copies:
        c.wait()


def attend(n, query, slot_of, live_of, store, kp, vp, scores, ready):
    scale = 128**-0.5
    groups = (n + GROUP - 1) // GROUP
    lane = lane_iota()

    def score(g):
        out = []
        for i in range(0, GROUP, 2):
            pair = [jnp.minimum(g * GROUP + i + k, n - 1) for k in range(2)]
            s = lax.dot_general(
                jnp.concatenate([query(item) for item in pair], axis=0),
                jnp.concatenate([kp[slot_of(item)] for item in pair], axis=0),
                (((1,), (1,)), ((), ())),
                preferred_element_type=F32,
            )
            out += [s[:ROWS, :128], s[ROWS:, 128:]]
        return out

    @pl.when(n > 0)
    def _():
        for i, s in enumerate(score(0)):
            scores[0, i] = s

    ready()

    def finish(g):
        now = lax.rem(g, 2)
        done = []
        for i in range(0, GROUP, 2):
            pair = [jnp.minimum(g * GROUP + i + k, n - 1) for k in range(2)]
            weights, totals, ends = [], [], []
            for k, item in enumerate(pair):
                s = jnp.where(lane < live_of(item), scores[now, i + k] * scale, DEAD)
                m = jnp.max(s, axis=1, keepdims=True)
                p = jnp.exp(s - m)
                l = jnp.sum(p, axis=1, keepdims=True)
                weights.append(p.astype(BF))
                totals.append(l)
                ends.append(jnp.broadcast_to(m + jnp.log(l), (ROWS, 128)))
            nil = jnp.zeros((ROWS, 128), BF)
            o = jnp.dot(
                jnp.concatenate(
                    [
                        jnp.concatenate([weights[0], nil], axis=1),
                        jnp.concatenate([nil, weights[1]], axis=1),
                    ],
                    axis=0,
                ),
                jnp.concatenate([vp[slot_of(item)] for item in pair], axis=0),
                preferred_element_type=F32,
            )
            parts = [o[:ROWS], o[ROWS:]]
            for k, item in enumerate(pair):
                done.append((item, parts[k] / totals[k], ends[k]))
        return done

    def work(g, _):
        later = score(g + 1)
        for item, o, z in finish(g):
            store(item, o, z)
        for i, s in enumerate(later):
            scores[lax.rem(g + 1, 2), i] = s
        return 0

    lax.fori_loop(0, groups - 1, work, 0)

    @pl.when(n > 0)
    def _():
        for item, o, z in finish(groups - 1):
            store(item, o, z)


def serve_kernel(
    vp_h, recv, kp,
    back,
    vp, wide, side_i, side_s, ids, answer, lse, scores, sems,
):
    peers = side_i.shape[0]
    values = pltpu.make_async_copy(vp_h, vp, sems.at[1])
    values.start()
    wide[: recv.shape[0], :] = recv[...].astype(F32)
    side_i[...] = wide[side_rows(peers), :].astype(jnp.int32)
    copy = pltpu.make_async_copy(side_i, side_s, sems.at[0])
    copy.start()
    answer[...] = jnp.zeros(answer.shape, F32)
    lse[...] = jnp.full(lse.shape, DEAD, F32)
    copy.wait()

    def listing(i, n):
        for c in range(CAP):
            ids[n] = i * CAP + c
            n = n + jnp.where(side_s[i, 2 * c + 1] > 0, 1, 0)
        return n

    n = lax.fori_loop(0, peers, listing, 0, unroll=4)

    def query(item):
        i = ids[item]
        return wide[tile_rows(lax.shift_right_logical(i, 1), i & 1), :].astype(BF)

    def slot_of(item):
        i = ids[item]
        return side_s[lax.shift_right_logical(i, 1), 2 * (i & 1)]

    def live_of(item):
        i = ids[item]
        return side_s[lax.shift_right_logical(i, 1), 2 * (i & 1) + 1]

    def store(item, o, z):
        i = ids[item]
        answer[tile_rows(lax.shift_right_logical(i, 1), i & 1), :] = o
        lse[pl.ds(i, 1), :] = jnp.sum(jnp.where(own, z, 0.0), axis=0, keepdims=True)

    own = lane_iota() % ROWS == lax.broadcasted_iota(jnp.int32, (ROWS, 128), 0)
    attend(n, query, slot_of, live_of, store, kp, vp, scores, values.wait)
    group = lane_iota(peers) // ROWS
    rest = jnp.where(
        group < 3, lse[pl.ds(0, peers, stride=CAP), :], lse[pl.ds(1, peers, stride=CAP), :]
    )
    side = jnp.zeros((peers, 128), F32)
    for piece in range(3):
        part = rest.astype(BF).astype(F32)
        rest = rest - part
        side = jnp.where(group % 3 == piece, part, side)
    answer[side_rows(peers), :] = side
    back[...] = answer[: back.shape[0], :].astype(BF)


def weigh(states):
    top = functools.reduce(jnp.maximum, [z for _, z in states])
    shares = [jnp.exp(z - top) for _, z in states]
    total = functools.reduce(jnp.add, shares)
    o = functools.reduce(jnp.add, [f * o for f, (o, _) in zip(shares, states)])
    return o / total, top, total


def home_kernel(
    entry_h, target_h, table_h, lengths_h, q_h, nk_h, nv_h, kp_h, vp_h,
    o_out, z_out, place_out, kp,
    entry, target, table, lengths, q, nk, nv, vp, o_part, z_part, place, latest, ids, scores, sems,
):
    requests, blocks = table.shape
    entries = requests * blocks
    copies = fetch_all(
        [(entry_h, entry), (target_h, target), (table_h, table), (lengths_h, lengths), (q_h, q), (nk_h, nk), (nv_h, nv), (kp_h, kp), (vp_h, vp)],
        sems,
    )
    z_part[...] = jnp.full(z_part.shape, DEAD, F32)
    o_part[...] = jnp.zeros(o_part.shape, F32)

    peers = latest.shape[0]
    none = peers * CAP

    def clear(i, _):
        place[0, i] = none
        return 0

    lax.fori_loop(0, entries, clear, 0, unroll=8)

    for c in copies[:7]:
        c.wait()

    note_last(target, latest)

    def mark(j, _):
        t = target[j]
        place[0, entry[j]] = t * CAP + rank_of(j, t, latest)
        return 0

    lax.fori_loop(0, entry.shape[0], mark, 0, unroll=8)
    placed = pltpu.make_async_copy(place, place_out, sems.at[9])
    placed.start()

    def listing(e, n):
        ids[n] = e
        r, b = split(e)
        alive = lengths[r] > b * 128
        return n + jnp.where(jnp.logical_and(alive, place[0, e] == none), 1, 0)

    n = lax.fori_loop(0, entries, listing, 0, unroll=4)

    def query(item):
        return q[split(ids[item])[0]]

    def slot_of(item):
        r, b = split(ids[item])
        return table[r, b]

    def live_of(item):
        r, b = split(ids[item])
        return lengths[r] - b * 128

    def store(item, o, z):
        o_part[ids[item]] = o
        z_part[ids[item]] = z

    copies[7].wait()
    attend(n, query, slot_of, live_of, store, kp, vp, scores, copies[8].wait)
    scale = 128**-0.5
    second = lax.broadcasted_iota(jnp.int32, (ROWS, 1), 0) >= HALF
    for r in range(requests):
        qr = q[r].astype(F32)
        k = nk[r].astype(F32)
        v = nv[r].astype(F32)
        s0 = jnp.sum(qr * k[0:1], axis=1, keepdims=True) * scale
        s1 = jnp.sum(qr * k[1:2], axis=1, keepdims=True) * scale
        s1 = jnp.where(second, s1, DEAD)
        m = jnp.maximum(s0, s1)
        p0 = jnp.exp(s0 - m)
        p1 = jnp.where(second, jnp.exp(s1 - m), 0.0)
        l = p0 + p1
        fresh = ((p0 * v[0:1] + p1 * v[1:2]) / l, jnp.broadcast_to(m + jnp.log(l), (ROWS, 128)))
        o, top, total = weigh([fresh] + [(o_part[r * 8 + b], z_part[r * 8 + b]) for b in range(8)])
        o_out[r] = o
        z_out[r] = top + jnp.log(total)
    placed.wait()


def merge_kernel(
    w, back, o_home, z_home, place_v,
    out,
    place, wide, z_back, att, sems,
):
    requests = o_home.shape[0]
    peers = z_back.shape[1] - 1
    rows = peers * SLAB
    width = out.shape[2]
    copy = pltpu.make_async_copy(place_v, place, sems.at[0])
    copy.start()
    wide[:rows, :] = back[...].astype(F32)
    wide[rows:, :] = jnp.zeros((MARGIN, 128), F32)
    side = wide[side_rows(peers), :].reshape(peers, 1, 128)
    lane = lax.broadcasted_iota(jnp.int32, (peers, ROWS, 128), 2)
    own = lane % ROWS == lax.broadcasted_iota(jnp.int32, (peers, ROWS, 128), 1)
    ones = jnp.ones((128, 128), BF)
    for c in range(CAP):
        mine = jnp.logical_and(own, lane // (3 * ROWS) == c)
        pieces = jnp.where(mine, side, 0.0).astype(BF).reshape(peers * ROWS, 128)
        z = jnp.dot(pieces, ones, preferred_element_type=F32)
        z_back[c, :peers] = z.reshape(peers, ROWS, 128)
    z_back[0, peers] = jnp.full((ROWS, 128), DEAD, F32)
    copy.wait()

    for r in range(requests):
        parts = [(o_home[r], z_home[r])]
        for b in range(8):
            i = place[0, r * 8 + b]
            peer, c = lax.shift_right_logical(i, 1), i & 1
            parts.append((wide[tile_rows(peer, c), :], z_back[c, peer]))
        att[r * ROWS : (r + 1) * ROWS, :] = weigh(parts)[0]
    heads = ROWS // 2
    a = jnp.concatenate(
        [att[pl.ds(g, 2 * requests, stride=heads), :].astype(BF) for g in range(heads)], axis=1
    )
    for i in range(out.shape[0]):
        block = w[:, i * width : (i + 1) * width]
        out[i] = jnp.dot(a, block, preferred_element_type=F32).astype(BF)


def sum_kernel(parts, out):
    total = parts[0].astype(F32)
    for i in range(1, parts.shape[0]):
        total = total + parts[i].astype(F32)
    out[...] = total.astype(BF).reshape(out.shape)


def params(limit):
    return pltpu.CompilerParams(vmem_limit_bytes=limit * 1024 * 1024)


def on_device(
    queries,
    new_keys,
    new_values,
    key_pool,
    value_pool,
    block_table,
    lengths,
    lend_entry,
    lend_target,
    out_weight,
):
    requests, steps, heads, size = queries.shape
    peers = lax.axis_size("inst")
    parts = lax.axis_size("tp")
    pool = key_pool.shape[0]
    entries = block_table.size
    lends = lend_entry.shape[0]
    q = queries.reshape(requests, steps * heads, size)
    nk = new_keys.reshape(requests, steps, size)
    nv = new_values.reshape(requests, steps, size)
    k_hbm = key_pool.reshape(pool, 128, size)
    v_hbm = value_pool.reshape(pool, 128, size)
    target = lend_target.reshape(lends)
    held = lambda x: pltpu.with_memory_space_constraint(x, pltpu.HBM)
    smem = lambda *n: pltpu.SMEM(n, jnp.int32)
    sems = lambda n: pltpu.SemaphoreType.DMA((n,))
    like = lambda x: jax.ShapeDtypeStruct(x.shape, x.dtype)
    wide = pltpu.VMEM((peers * SLAB + MARGIN, size), F32)
    scores = pltpu.VMEM((2, GROUP, ROWS, 128), F32)

    send = pl.pallas_call(
        pack_kernel,
        out_shape=jax.ShapeDtypeStruct((peers * SLAB, size), BF),
        in_specs=[HB] * 5,
        out_specs=HB,
        scratch_shapes=[
            smem(lends),
            smem(lends),
            smem(*block_table.shape),
            smem(requests),
            pltpu.VMEM(q.shape, BF),
            wide,
            pltpu.VMEM((peers * SLAB, size), BF),
            smem(peers),
            smem(peers * CAP),
            smem(peers * CAP),
            sems(9),
        ],
        compiler_params=params(16),
    )(*map(held, (lend_entry, target, block_table, lengths, q)))

    def exchange(x):
        y = x.reshape(peers, SLAB // 2, 2, size)
        y = lax.all_to_all(y, "inst", split_axis=0, concat_axis=0, tiled=True)
        return y.reshape(x.shape)

    recv = exchange(send)

    tile_state = jax.ShapeDtypeStruct((requests, ROWS, size), F32)
    o_home, z_home, place, kp = pl.pallas_call(
        home_kernel,
        out_shape=(
            tile_state,
            tile_state,
            jax.ShapeDtypeStruct((1, 128), jnp.int32),
            like(k_hbm),
        ),
        in_specs=[HB] * 9,
        out_specs=(VM, VM, VM, VM),
        scratch_shapes=[
            smem(lends),
            smem(lends),
            smem(*block_table.shape),
            smem(requests),
            pltpu.VMEM(q.shape, BF),
            pltpu.VMEM(nk.shape, BF),
            pltpu.VMEM(nv.shape, BF),
            pltpu.VMEM(v_hbm.shape, BF),
            pltpu.VMEM((entries, ROWS, size), F32),
            pltpu.VMEM((entries, ROWS, size), F32),
            smem(1, 128),
            smem(peers),
            smem(entries + 1),
            scores,
            sems(10),
        ],
        compiler_params=params(24),
        cost_estimate=pl.CostEstimate(flops=10**9, bytes_accessed=16 * 2**20, transcendentals=0),
    )(*map(held, (lend_entry, target, block_table, lengths, q, nk, nv, k_hbm, v_hbm)))

    back = pl.pallas_call(
        serve_kernel,
        out_shape=jax.ShapeDtypeStruct((peers * SLAB, size), BF),
        in_specs=[HB, VM, VM],
        out_specs=VM,
        scratch_shapes=[
            pltpu.VMEM(v_hbm.shape, BF),
            wide,
            pltpu.VMEM((peers, 128), jnp.int32),
            smem(peers, 128),
            smem(peers * CAP + 1),
            wide,
            pltpu.VMEM((peers * CAP + MARGIN, 128), F32),
            scores,
            sems(2),
        ],
        compiler_params=params(16),
        cost_estimate=pl.CostEstimate(flops=10000000000, bytes_accessed=16777216, transcendentals=0),
    )(held(v_hbm), recv, kp)

    mine = exchange(back)

    partial = pl.pallas_call(
        merge_kernel,
        out_shape=jax.ShapeDtypeStruct((parts, requests * steps, out_weight.shape[1] // parts), BF),
        in_specs=[VM] * 5,
        out_specs=VM,
        scratch_shapes=[
            smem(1, 128),
            wide,
            pltpu.VMEM((CAP, peers + 1, ROWS, 128), F32),
            pltpu.VMEM((requests * ROWS + MARGIN, size), F32),
            sems(1),
        ],
        compiler_params=params(24),
    )(out_weight, mine, o_home, z_home, place)

    shares = lax.all_to_all(partial, "tp", split_axis=0, concat_axis=0, tiled=True)

    return pl.pallas_call(
        sum_kernel,
        out_shape=jax.ShapeDtypeStruct((requests, steps, shares.shape[2]), BF),
        in_specs=[VM],
        out_specs=VM,
        compiler_params=params(8),
    )(shares)


def solution(mesh):
    placed = (
        P("inst", None, "tp", None),
        P("inst", None, "tp", None),
        P("inst", None, "tp", None),
        P("inst", "tp", None, None),
        P("inst", "tp", None, None),
        P("inst", None),
        P("inst"),
        P("inst"),
        P("inst", None),
        P("tp", None),
    )
    return jax.shard_map(
        on_device, mesh=mesh, in_specs=placed, out_specs=P("inst", None, "tp"), check_vma=False
    )
```
